512 devices in a mesh: row: 8 (over y, core), col: 32 (over z_lo, x), grp: 2 (over z_hi).
Axes of the slice: x: 4, y: 4, z: 16 (z_hi: 2, z_lo: 8; z = z_hi * 8 + z_lo), core: 2. Of those that a mesh axis runs over, the one named last changes fastest.
Arguments:
- momentum: float32 [2, 4096, 16384], P('grp', 'row', 'col'), may hold values from -6 to 6
- gradient: bfloat16 [2, 4096, 16384], P('grp', 'row', 'col'), may hold values from -6 to 6
- factor_q: float32 [2, 16384, 256], P('grp', 'col', 'row'), may hold values from -0.046875 to 0.046875
- weights: float32 [2, 4096, 16384], P(None, 'row', ('col', 'grp')), may hold values from -6 to 6
- tokens: bfloat16 [256, 4096], P(None, 'row'), may hold values from -0.08984375 to 0.08984375
Outputs:
- momentum_out: float32 [2, 4096, 16384], P('grp', 'row', 'col')
- factor_out: float32 [2, 16384, 256], P('grp', 'col', 'row')
- weights_out: float32 [2, 4096, 16384], P(None, 'row', ('col', 'grp'))
- hidden: bfloat16 [256, 16384], P('row', ('col', 'grp'))
The draws below stay inside these ranges and needn't reach their ends.
All inputs are finite; a program needn't handle non-finite values.
Results may differ from the reference program's by a relative error of at most 0.0061.
Values may be sent and summed in bfloat16 or wider, within the bound.
A program may use at most 64 MiB of HBM per device.

```python
import math
import jax
import jax.numpy as jnp
from jax import lax

D = 4096
HID = 16384
RANK = 256
BATCH = 256


def level_of(rng, extent, pieces, smallest, largest):
    level = 1.0
    for axis_at, shards_of in pieces:
        steps = jax.random.uniform(jax.random.fold_in(jax.random.fold_in(rng, 6), axis_at), (shards_of,), jnp.float32, smallest / len(pieces), largest / len(pieces))
        level = level * jnp.repeat(jnp.exp(steps), extent[axis_at] // shards_of).reshape((-1,) + (1,) * (len(extent) - 1 - axis_at))
    return level


def normal_values(stream_key, extent, width, bound, cuts=(), dtype=jnp.bfloat16):
    drawn = jax.random.normal(stream_key, extent, jnp.float32) * width
    if len(cuts) > 0:
        drawn = level_of(stream_key, extent, cuts, -0.22, 0.18) * drawn
    return jnp.clip(drawn, min=-bound, max=bound).astype(dtype)


def setup_inputs(seed: int = 0) -> dict:
    arg_keys = jax.random.split(jax.random.key(seed), 6)
    momentum = normal_values(arg_keys[0], (2, D, HID), 1.0, 6.0, ((0, 2), (1, 8), (2, 32)), jnp.float32)
    gradient = normal_values(arg_keys[1], (2, D, HID), 1.0, 6.0, ((0, 2), (1, 8), (2, 32)))
    factor_q = normal_values(arg_keys[2], (2, HID, RANK), HID ** -0.5, 0.046875, ((0, 2), (1, 32), (2, 8)), jnp.float32)
    weights = normal_values(arg_keys[3], (2, D, HID), 1.0, 6.0, ((1, 8), (2, 64)), jnp.float32)
    tokens = normal_values(arg_keys[4], (BATCH, D), 0.015625, 0.08984375, ((1, 8),))
    return {"momentum": momentum, "gradient": gradient, "factor_q": factor_q, "weights": weights, "tokens": tokens}


feedback = 0.05
epsilon = 1e-06

def reference(momentum, gradient, factor_q, weights, tokens):
    step_size = 0.4 * math.sqrt(max(D, HID))
    mom_list = []
    q_list = []
    weight_list = []
    act_list = []
    for which in range(2):
        buffer = momentum[which] + gradient[which].astype(jnp.float32)
        buffer_h = buffer.astype(jnp.bfloat16)
        q_h = factor_q[which].astype(jnp.bfloat16)
        raw_left = jnp.dot(buffer_h.astype(jnp.float32), q_h.astype(jnp.float32), preferred_element_type=jnp.float32)
        gram_sum = jnp.dot(raw_left.T, raw_left, precision=lax.Precision.HIGHEST)
        factor_l = jnp.linalg.cholesky(gram_sum)
        ortho_left = jax.scipy.linalg.solve_triangular(factor_l, raw_left.T, lower=True).T
        left_h = ortho_left.astype(jnp.bfloat16)
        right_full = jnp.dot(buffer_h.T.astype(jnp.float32), left_h.astype(jnp.float32), preferred_element_type=jnp.float32)
        right_h = right_full.astype(jnp.bfloat16)
        mom_list.append(buffer - feedback * jnp.dot(left_h.astype(jnp.float32), right_h.T.astype(jnp.float32), preferred_element_type=jnp.float32))
        col_norms = jnp.sqrt(lax.optimization_barrier(jnp.sum(right_full * right_full, axis=0)) + epsilon)
        new_q = right_full / col_norms
        q_list.append(new_q)
        new_q_h = new_q.astype(jnp.bfloat16)
        new_weight = weights[which] - step_size * jnp.dot(left_h.astype(jnp.float32), new_q_h.T.astype(jnp.float32), preferred_element_type=jnp.float32)
        weight_list.append(new_weight)
        act_list.append(jnp.dot(tokens.astype(jnp.float32), new_weight.astype(jnp.bfloat16).astype(jnp.float32), preferred_element_type=jnp.float32))
    hidden = (jax.nn.silu(act_list[0]) * act_list[1]).astype(jnp.bfloat16)
    return (jnp.stack(mom_list), jnp.stack(q_list), jnp.stack(weight_list), hidden)
```

```python
import functools
import math

import jax
import jax.numpy as jnp
from jax import lax
from jax.experimental import pallas as pl
from jax.experimental.pallas import tpu as pltpu
from jax.sharding import PartitionSpec as P

D = 4096
HID = 16384
RANK = 256
BATCH = 256
FEEDBACK = 0.05
EPSILON = 1e-06
STEP = 0.4 * math.sqrt(max(D, HID))
NX = 4

f32, bf16 = jnp.float32, jnp.bfloat16
HI = lax.Precision.HIGHEST
MESH = pl.DeviceIdType.MESH
NN = (((1,), (0,)), ((), ()))
NT = (((1,), (1,)), ((), ()))
TN = (((0,), (0,)), ((), ()))


def mm(a, b, dims=NN, precision=None):
    return lax.dot_general(a, b, dims, precision=precision, preferred_element_type=f32)


def wrap(i, d, n):
    return lax.rem(i + d, n)


class Place:
    def __init__(self, sizes):
        self.nr, self.nc, self.ng = sizes
        self.nx, self.nz = NX, self.nc // NX
        self.r, self.c, self.g = (lax.axis_index(a) for a in ("row", "col", "grp"))
        self.x, self.z = lax.rem(self.c, self.nx), lax.div(self.c, self.nx)

    def at(self, dr=0, dx=0, dz=0, dg=0):
        c = wrap(self.z, dz, self.nz) * self.nx + wrap(self.x, dx, self.nx)
        return (wrap(self.r, dr, self.nr), c, wrap(self.g, dg, self.ng))


def greet(partners):
    barrier = pltpu.get_barrier_semaphore()
    for device in partners:
        pl.semaphore_signal(barrier, inc=1, device_id=device, device_id_type=MESH)
    return lambda: pl.semaphore_wait(barrier, len(partners))


def send(src, dst, sems, k, device):
    copy = pltpu.make_async_remote_copy(
        src_ref=src, dst_ref=dst, send_sem=sems.at[0, k], recv_sem=sems.at[1, k], device_id=device, device_id_type=MESH
    )
    copy.start()
    return copy


def arrived(copies):
    for copy in copies:
        copy.wait_recv()


def left_kernel(sizes, mom, grad, fq, w, tok, left_o, gram_o, base_o,
                bufh, qbuf, part, rx, sx, rz, l512, gp, rg, gf, pre, rpre,
                s_q, s_x, s_z, s_az, s_ax, s_g, s_ag, s_p):
    at = Place(sizes)
    nr, nx, nz = at.nr, at.nx, at.nz
    plane = [(dx, dr) for dx in range(nx) for dr in range(nr) if dx or dr]
    ready = greet([at.at(dr=dr, dx=dx) for dx, dr in plane] + [at.at(dz=d) for d in range(1, nz)])
    r, x, z = at.r, at.x, at.z
    sent = []

    qbuf[r] = fq[...].T.astype(bf16)
    bufh[...] = (mom[...] + grad[...].astype(f32)).astype(bf16)
    ready()
    got_q = [send(qbuf.at[r], qbuf.at[r], s_q, d - 1, at.at(dr=d)) for d in range(1, nr)]
    for p in range(2):
        high = w[p].astype(bf16)
        low = (w[p] - high.astype(f32)).astype(bf16)
        pre[:, p] = (mm(tok[...], high) + mm(tok[...], low)).reshape(pre[:, p].shape)
    arrived(got_q)
    part[...] = mm(bufh[...], qbuf[...].reshape(RANK, -1), NT).reshape(part.shape)
    got_x = [send(part.at[wrap(x, d, nx)], rx.at[d - 1], s_x, d - 1, at.at(dx=d)) for d in range(1, nx)]
    got_p = [send(pre.at[wrap(r, d, nr)], rpre.at[d - 1], s_p, d - 1, at.at(dr=d)) for d in range(1, nr)]
    arrived(got_x)
    sx[...] = (part[x] + jnp.sum(rx[...], axis=0)).reshape(sx.shape)
    got_z = [send(sx.at[wrap(z, d, nz)], rz.at[d - 1], s_z, d - 1, at.at(dz=d)) for d in range(1, nz)]
    arrived(got_z)
    l512[x, z] = sx[z] + jnp.sum(rz[...], axis=0)
    got_az = [send(l512.at[x, z], l512.at[x, z], s_az, d - 1, at.at(dz=d)) for d in range(1, nz)]
    arrived(got_az)
    rows = l512[x].reshape(-1, RANK)
    gp[...] = mm(rows, rows, TN, HI).reshape(gp.shape)
    got_g = []
    for k, (dx, dr) in enumerate(plane):
        m = wrap(x, dx, nx) * nr + wrap(r, dr, nr)
        got_g.append(send(gp.at[m], rg.at[k], s_g, k, at.at(dr=dr, dx=dx)))
    got_ax = [send(l512.at[x], l512.at[x], s_ax, d - 1, at.at(dx=d)) for d in range(1, nx)]
    arrived(got_g)
    m = x * nr + r
    gf[m] = gp[m] + jnp.sum(rg[...], axis=0)
    got_ag = [send(gf.at[m], gf.at[m], s_ag, k, at.at(dr=dr, dx=dx)) for k, (dx, dr) in enumerate(plane)]
    arrived(got_p)
    base_o[...] = pre[r] + jnp.sum(rpre[...], axis=0)
    arrived(got_ax)
    left_o[...] = l512[...].reshape(left_o.shape)
    arrived(got_ag)
    gram_o[...] = gf[...].reshape(gram_o.shape)
    for copies in (got_q, got_x, got_p, got_z, got_az, got_g, got_ax, got_ag):
        for copy in copies:
            copy.wait_send()


def right_kernel(sizes, mom, grad, left, wt, w, base, tok, mom_o, fac_o, new_o, hid_o,
                 bufh, lh, oth, rt, rrt, tl, rtl, tls, tlo, rh, sho, rho, sq, rsq, nb,
                 s_l, s_rt, s_tl, s_lz, s_lx, s_rh, s_sh, s_ro, s_sq, s_nb, s_to):
    at = Place(sizes)
    nr, nx, nz, ng = at.nr, at.nx, at.nz, at.ng
    r, c, g, x, z = at.r, at.c, at.g, at.x, at.z
    column = [(dg, dz, dx) for dg in range(ng) for dz in range(nz) for dx in range(nx) if dg or dz or dx]
    ready = greet([at.at(dr=d) for d in range(1, nr)] + [at.at(dg=dg, dz=dz, dx=dx) for dg, dz, dx in column])
    o = 1 - g
    kr = RANK // nr
    half = w.shape[2]

    buffer = mom[...] + grad[...].astype(f32)
    bufh[...] = buffer.astype(bf16)
    left_h = mm(left[...], wt[...], NN, HI).astype(bf16)
    lh[...] = left_h.reshape(lh.shape)
    ready()
    got_l = [send(lh.at[x, z], oth.at[x, z], s_l, 0, at.at(dg=1))]
    rt[...] = mm(left_h, bufh[...], TN).reshape(rt.shape)
    got_rt = [send(rt.at[wrap(r, d, nr)], rrt.at[d - 1], s_rt, d - 1, at.at(dr=d)) for d in range(1, nr)]
    tl[...] = mm(tok[...], left_h).reshape(tl.shape)
    got_tl = [send(tl.at[wrap(r, d, nr)], rtl.at[d - 1], s_tl, d - 1, at.at(dr=d)) for d in range(1, nr)]
    arrived(got_l)
    got_lz = [send(oth.at[x, z], oth.at[x, z], s_lz, d - 1, at.at(dz=d)) for d in range(1, nz)]

    arrived(got_rt)
    share = rt[r] + jnp.sum(rrt[...], axis=0)
    rt[r] = share
    rh[r] = share.astype(bf16)
    sho[...] = rt[r, :, pl.ds(pl.multiple_of(o * half, half), half)].astype(bf16)
    got_sh = [send(sho, rho.at[r], s_sh, 0, at.at(dg=1))]
    eye = lax.broadcasted_iota(jnp.int32, (kr, 128), 0) == lax.broadcasted_iota(jnp.int32, (kr, 128), 1)
    squares = jnp.sum(share * share, axis=1, keepdims=True)
    line = jnp.sum(jnp.where(eye, squares, 0.0), axis=0, keepdims=True)
    rsq[g, c] = line
    sq[...] = line
    got_sq = [send(sq, rsq.at[g, c], s_sq, k, at.at(dg=dg, dz=dz, dx=dx)) for k, (dg, dz, dx) in enumerate(column)]
    got_rh = [send(rh.at[r], rh.at[r], s_rh, d - 1, at.at(dr=d)) for d in range(1, nr)]
    arrived(got_lz)
    got_lx = [send(oth.at[x], oth.at[x], s_lx, d - 1, at.at(dx=d)) for d in range(1, nx)]
    arrived(got_sq)
    nb[r] = jnp.sum(rsq[...], axis=1)
    got_nb = [send(nb.at[r], nb.at[r], s_nb, d - 1, at.at(dr=d)) for d in range(1, nr)]
    arrived(got_sh)
    got_ro = [send(rho.at[r], rho.at[r], s_ro, d - 1, at.at(dr=d)) for d in range(1, nr)]
    arrived(got_tl)
    tls[...] = tl[r] + jnp.sum(rtl[...], axis=0)
    got_to = [send(tls, tlo, s_to, 0, at.at(dg=1))]
    fac_o[...] = (share.T / jnp.sqrt(nb[r, g][:, :kr] + EPSILON))
    arrived(got_rh)
    mom_o[...] = buffer - FEEDBACK * mm(left_h, rh[...].reshape(RANK, -1))

    arrived(got_nb)

    def normalised(p, right):
        norms = jnp.sqrt(nb[:, p] + EPSILON)
        norms = jnp.broadcast_to(norms, (nr, kr, 128))
        norms = jnp.sum(jnp.where(eye[None], norms, 0.0), axis=2, keepdims=True)
        return (right.astype(f32) / norms).astype(bf16).reshape(RANK, -1)

    own_q = normalised(g, rh[:, :, pl.ds(pl.multiple_of(g * half, half), half)])
    new_o[g] = w[g] - STEP * mm(left_h, own_q)
    own_pre = base[g] - STEP * mm(tls[...], own_q.astype(f32), NN, HI)
    arrived(got_ro)
    other_q = normalised(o, rho[...])
    arrived(got_lx)
    new_o[o] = w[o] - STEP * mm(oth[...].reshape(-1, RANK), other_q)
    arrived(got_to)
    other_pre = base[o] - STEP * mm(tlo[...], other_q.astype(f32), NN, HI)
    gate = jnp.where(g == 0, own_pre, other_pre)
    up = jnp.where(g == 0, other_pre, own_pre)
    hid_o[...] = (gate / (1.0 + jnp.exp(-gate)) * up).astype(bf16)
    for copies in (got_l, got_rt, got_tl, got_lz, got_sh, got_sq, got_rh, got_lx, got_nb, got_ro, got_to):
        for copy in copies:
            copy.wait_send()


def vmem(*shape, dtype=f32):
    return pltpu.VMEM(shape, dtype)


def pairs(n):
    return pltpu.SemaphoreType.DMA((2, n))


def call(kernel, outs, scratch, collective_id, *args):
    return pl.pallas_call(
        kernel,
        out_shape=[jax.ShapeDtypeStruct(s, t) for s, t in outs],
        in_specs=[pl.BlockSpec(memory_space=pltpu.VMEM)] * len(args),
        out_specs=[pl.BlockSpec(memory_space=pltpu.VMEM)] * len(outs),
        scratch_shapes=scratch,
        compiler_params=pltpu.CompilerParams(
            collective_id=collective_id, has_side_effects=True, vmem_limit_bytes=40 << 20
        ),
    )(*args)


def inverse_factor(gram):
    factor_l = jnp.linalg.cholesky(gram)
    return jax.scipy.linalg.solve_triangular(factor_l, jnp.eye(RANK, dtype=f32), lower=True).T


def local(sizes, momentum, gradient, factor_q, weights, tokens):
    nr, nc, ng = sizes
    nx, nz = NX, nc // NX
    mom, grad, fq = momentum[0], gradient[0], factor_q[0]
    rows, hid = mom.shape
    part, kr, nb = nx * nr, RANK // nr, BATCH // nr
    half = hid // ng
    left, gram, base = call(
        functools.partial(left_kernel, sizes),
        [((rows, RANK), f32), ((RANK, RANK), f32), ((2, nb, half), f32)],
        [
            vmem(rows, hid, dtype=bf16), vmem(nr, kr, hid, dtype=bf16),
            vmem(nx, rows // nx, RANK), vmem(nx - 1, rows // nx, RANK),
            vmem(nz, rows // nc, RANK), vmem(nz - 1, rows // nc, RANK), vmem(nx, nz, rows // nc, RANK),
            vmem(part, RANK // part, RANK), vmem(part - 1, RANK // part, RANK), vmem(part, RANK // part, RANK),
            vmem(nr, 2, nb, half), vmem(nr - 1, 2, nb, half),
            pairs(nr - 1), pairs(nx - 1), pairs(nz - 1), pairs(nz - 1), pairs(nx - 1), pairs(part - 1), pairs(part - 1),
            pairs(nr - 1),
        ],
        0, mom, grad, fq, weights, tokens,
    )
    wt = inverse_factor(gram)
    mom_new, fac, new, hidden = call(
        functools.partial(right_kernel, sizes),
        [((rows, hid), f32), ((hid, kr), f32), (weights.shape, f32), ((nb, half), bf16)],
        [
            vmem(rows, hid, dtype=bf16), vmem(nx, nz, rows // nc, RANK, dtype=bf16),
            vmem(nx, nz, rows // nc, RANK, dtype=bf16), vmem(nr, kr, hid), vmem(nr - 1, kr, hid),
            vmem(nr, nb, RANK), vmem(nr - 1, nb, RANK), vmem(nb, RANK), vmem(nb, RANK),
            vmem(nr, kr, hid, dtype=bf16), vmem(kr, half, dtype=bf16), vmem(nr, kr, half, dtype=bf16),
            vmem(1, 128), vmem(ng, nc, 1, 128), vmem(nr, ng, 1, 128),
            pairs(1), pairs(nr - 1), pairs(nr - 1), pairs(nz - 1), pairs(nx - 1), pairs(nr - 1), pairs(1), pairs(nr - 1),
            pairs(ng * nc - 1), pairs(nr - 1), pairs(1),
        ],
        1, mom, grad, left, wt, weights, base, tokens,
    )
    return mom_new[None], fac[None], new, hidden


def solution(mesh):
    sizes = tuple(mesh.shape[a] for a in ("row", "col", "grp"))
    in_specs = (
        P("grp", "row", "col"),
        P("grp", "row", "col"),
        P("grp", "col", "row"),
        P(None, "row", ("col", "grp")),
        P(None, "row"),
    )
    out_specs = (
        P("grp", "row", "col"),
        P("grp", "col", "row"),
        P(None, "row", ("col", "grp")),
        P("row", ("col", "grp")),
    )
    return jax.shard_map(
        functools.partial(local, sizes), mesh=mesh, in_specs=in_specs, out_specs=out_specs, check_vma=False
    )
```

```python
import functools
import math

import jax
import jax.numpy as jnp
from jax import lax
from jax.experimental import pallas as pl
from jax.experimental.pallas import tpu as pltpu
from jax.sharding import PartitionSpec as P

D = 4096
HID = 16384
RANK = 256
BATCH = 256
FEEDBACK = 0.05
EPSILON = 1e-06
STEP = 0.4 * math.sqrt(max(D, HID))
CHUNKS = 4
NX = 4

f32, bf16 = jnp.float32, jnp.bfloat16
HI = lax.Precision.HIGHEST
MESH = pl.DeviceIdType.MESH
NN = (((1,), (0,)), ((), ()))
NT = (((1,), (1,)), ((), ()))
TN = (((0,), (0,)), ((), ()))


def mm(a, b, dims=NN, precision=None):
    return lax.dot_general(a, b, dims, precision=precision, preferred_element_type=f32)


def around(i, n):
    return [i if d == 0 else i + d - jnp.where(i + d >= n, n, 0) for d in range(n)]


class Place:
    def __init__(self, sizes):
        self.nr, self.nc, self.ng = sizes
        self.nx, self.nz = NX, self.nc // NX
        self.r, self.c, self.g = (lax.axis_index(a) for a in ("row", "col", "grp"))
        self.x, self.z = lax.rem(self.c, self.nx), lax.div(self.c, self.nx)
        self.rs, self.xs, self.zs = around(self.r, self.nr), around(self.x, self.nx), around(self.z, self.nz)
        self.gs = [self.g, 1 - self.g]

    def at(self, dr=0, dx=0, dz=0, dg=0):
        return (self.rs[dr], self.zs[dz] * self.nx + self.xs[dx], self.gs[dg])


def greet(partners):
    barrier = pltpu.get_barrier_semaphore()
    for device in partners:
        pl.semaphore_signal(barrier, inc=1, device_id=device, device_id_type=MESH)
    return lambda: pl.semaphore_wait(barrier, len(partners))


def send(src, dst, sems, k, device):
    copy = pltpu.make_async_remote_copy(
        src_ref=src, dst_ref=dst, send_sem=sems.at[0, k], recv_sem=sems.at[1, k], device_id=device, device_id_type=MESH
    )
    copy.start()
    return copy


def arrived(copies):
    for copy in copies:
        copy.wait_recv()


def left_kernel(sizes, mom_h, grad_h, fq_h, w_h, tok_h, left_o, gram_o, base_o, bufh,
                mom, grad, fq, w, tok, s_in, qbuf, part, partb, rx, sx, sxb, rz, l512, gp, rg, gf, pre, rpre,
                s_q, s_x, s_z, s_az, s_ax, s_g, s_ag, s_p):
    at = Place(sizes)
    nr, nx, nz = at.nr, at.nx, at.nz
    plane = [(dx, dr) for dx in range(nx) for dr in range(nr) if dx or dr]
    ready = greet([at.at(dr=dr, dx=dx) for dx, dr in plane] + [at.at(dz=d) for d in range(1, nz)])
    r, x, z = at.r, at.x, at.z
    loads = [
        pltpu.make_async_copy(a, b, s_in.at[k])
        for k, (a, b) in enumerate(((fq_h, fq), (mom_h, mom), (grad_h, grad), (tok_h, tok), (w_h, w)))
    ]
    for load in loads:
        load.start()
    loads[0].wait()
    qbuf[r] = fq[...].astype(bf16)
    ready()
    got_q = [send(qbuf.at[r], qbuf.at[r], s_q, d - 1, at.at(dr=d)) for d in range(1, nr)]
    loads[1].wait()
    loads[2].wait()
    bufh[...] = (mom[...] + grad[...].astype(f32)).astype(bf16)
    arrived(got_q)
    part[...] = mm(bufh[...], qbuf[...].reshape(RANK, -1), NT).reshape(part.shape)
    partb[...] = part[...].astype(bf16)
    got_x = [send(partb.at[at.xs[d]], rx.at[d - 1], s_x, d - 1, at.at(dx=d)) for d in range(1, nx)]
    loads[3].wait()
    loads[4].wait()
    for p in range(2):
        high = w[p].astype(bf16)
        low = (w[p] - high.astype(f32)).astype(bf16)
        pre[:, p] = (mm(tok[...], high) + mm(tok[...], low)).reshape(pre[:, p].shape)
    arrived(got_x)
    sx[...] = (part[x] + jnp.sum(rx[...].astype(f32), axis=0)).reshape(sx.shape)
    sxb[...] = sx[...].astype(bf16)
    got_z = [send(sxb.at[at.zs[d]], rz.at[d - 1], s_z, d - 1, at.at(dz=d)) for d in range(1, nz)]
    got_p = [send(pre.at[at.rs[d]], rpre.at[d - 1], s_p, d - 1, at.at(dr=d)) for d in range(1, nr)]
    arrived(got_z)
    l512[x, z] = (sx[z] + jnp.sum(rz[...].astype(f32), axis=0)).astype(bf16)
    got_az = [send(l512.at[x, z], l512.at[x, z], s_az, d - 1, at.at(dz=d)) for d in range(1, nz)]
    arrived(got_az)
    rows = l512[x].reshape(-1, RANK)
    gp[...] = mm(rows, rows, TN).reshape(gp.shape)
    got_g = []
    for k, (dx, dr) in enumerate(plane):
        m = at.xs[dx] * nr + at.rs[dr]
        got_g.append(send(gp.at[m], rg.at[k], s_g, k, at.at(dr=dr, dx=dx)))
    got_ax = [send(l512.at[x], l512.at[x], s_ax, d - 1, at.at(dx=d)) for d in range(1, nx)]
    arrived(got_g)
    m = x * nr + r
    gf[m] = gp[m] + jnp.sum(rg[...], axis=0)
    got_ag = [send(gf.at[m], gf.at[m], s_ag, k, at.at(dr=dr, dx=dx)) for k, (dx, dr) in enumerate(plane)]
    arrived(got_p)
    base_o[...] = pre[r] + jnp.sum(rpre[...], axis=0)
    arrived(got_ax)
    left_o[...] = l512[...].reshape(left_o.shape)
    arrived(got_ag)
    gram_o[...] = gf[...].reshape(gram_o.shape)
    for copies in (got_q, got_x, got_p, got_z, got_az, got_g, got_ax, got_ag):
        for copy in copies:
            copy.wait_send()


def right_kernel(sizes, bufh, left, linv, tok, lh_o, oth_o, rh_o, rho_o, nb_o, share_o, tl_o,
                 lh, oth, rt, rtb, rrt, tl, tlb, rtl, tls, tlo, rh, sho, rho, sq, sqx, sqz, nb,
                 s_l, s_rt, s_tl, s_lz, s_lx, s_rh, s_sh, s_ro, s_sq, s_sz, s_nb, s_to):
    at = Place(sizes)
    nr, nx, nz, ng = at.nr, at.nx, at.nz, at.ng
    r, c, g, x, z = at.r, at.c, at.g, at.x, at.z
    side = [(dx, dg) for dx in range(nx) for dg in range(ng) if dx or dg]
    ready = greet(
        [at.at(dr=d) for d in range(1, nr)] + [at.at(dz=d) for d in range(1, nz)] + [at.at(dx=dx, dg=dg) for dx, dg in side]
    )
    o = 1 - g
    kr = RANK // nr
    half = sho.shape[1]

    high = linv[...].astype(bf16)
    low = (linv[...] - high.astype(f32)).astype(bf16)
    left_h = (mm(left[...], high, NT) + mm(left[...], low, NT)).astype(bf16)
    lh[...] = left_h.reshape(lh.shape)
    ready()
    got_l = [send(lh.at[x, z], oth.at[x, z], s_l, 0, at.at(dg=1))]
    rt[...] = mm(left_h, bufh[...], TN).reshape(rt.shape)
    rtb[...] = rt[...].astype(bf16)
    got_rt = [send(rtb.at[at.rs[d]], rrt.at[d - 1], s_rt, d - 1, at.at(dr=d)) for d in range(1, nr)]
    tl[...] = mm(tok[...], left_h).reshape(tl.shape)
    tlb[...] = tl[...].astype(bf16)
    got_tl = [send(tlb.at[at.rs[d]], rtl.at[d - 1], s_tl, d - 1, at.at(dr=d)) for d in range(1, nr)]
    arrived(got_rt)
    share = rt[r] + jnp.sum(rrt[...].astype(f32), axis=0)
    share_o[...] = share
    rh[r] = share.astype(bf16)
    sho[...] = share_o[:, pl.ds(pl.multiple_of(o * half, half), half)].astype(bf16)
    got_sh = [send(sho, rho.at[r], s_sh, 0, at.at(dg=1))]
    eye = lax.broadcasted_iota(jnp.int32, (kr, 128), 0) == lax.broadcasted_iota(jnp.int32, (kr, 128), 1)
    squares = jnp.sum(share * share, axis=1, keepdims=True)
    line = jnp.sum(jnp.where(eye, squares, 0.0), axis=0, keepdims=True)
    sqx[g, x] = line
    sq[...] = line
    got_sq = [send(sq, sqx.at[g, x], s_sq, k, at.at(dx=dx, dg=dg)) for k, (dx, dg) in enumerate(side)]
    got_rh = [send(rh.at[r], rh.at[r], s_rh, d - 1, at.at(dr=d)) for d in range(1, nr)]
    arrived(got_l)
    got_lz = [send(oth.at[x, z], oth.at[x, z], s_lz, d - 1, at.at(dz=d)) for d in range(1, nz)]
    arrived(got_sq)
    sqz[z] = jnp.sum(sqx[...], axis=1)
    got_sz = [send(sqz.at[z], sqz.at[z], s_sz, d - 1, at.at(dz=d)) for d in range(1, nz)]
    arrived(got_sh)
    got_ro = [send(rho.at[r], rho.at[r], s_ro, d - 1, at.at(dr=d)) for d in range(1, nr)]
    arrived(got_sz)
    nb[r] = jnp.sum(sqz[...], axis=0)
    got_nb = [send(nb.at[r], nb.at[r], s_nb, d - 1, at.at(dr=d)) for d in range(1, nr)]
    arrived(got_lz)
    got_lx = [send(oth.at[x], oth.at[x], s_lx, d - 1, at.at(dx=d)) for d in range(1, nx)]
    arrived(got_tl)
    tls[...] = (tl[r] + jnp.sum(rtl[...].astype(f32), axis=0)).astype(bf16)
    got_to = [send(tls, tlo, s_to, 0, at.at(dg=1))]
    lh_o[...] = lh[...].reshape(lh_o.shape)
    arrived(got_rh)
    rh_o[...] = rh[...].reshape(rh_o.shape)
    arrived(got_lx)
    oth_o[...] = oth[...].reshape(oth_o.shape)
    arrived(got_nb)
    nb_o[...] = nb[...]
    arrived(got_ro)
    rho_o[...] = rho[...]
    arrived(got_to)
    tl_o[0] = tls[...]
    tl_o[1] = tlo[...]
    for copies in (got_l, got_rt, got_tl, got_lz, got_sh, got_sq, got_sz, got_rh, got_lx, got_nb, got_ro, got_to):
        for copy in copies:
            copy.wait_send()


def last_kernel(mom, grad, w, base, lh, oth, rh, rho, nb, share, tl, mom_h, new_h, fac_o, hid_o, mom_v, new_v, sems):
    r, g = lax.axis_index("row"), lax.axis_index("grp")
    o = 1 - g
    nr, kr, half = rho.shape
    rows = lh.shape[0]
    chunk = rows // CHUNKS
    copies = []

    def out(src, dst):
        copies.append(pltpu.make_async_copy(src, dst, sems.at[len(copies)]))
        copies[-1].start()

    for k in range(CHUNKS):
        at = pl.ds(k * chunk, chunk)
        mom_v[at] = mom[at] + grad[at].astype(f32) - FEEDBACK * mm(lh[at], rh[...])
        out(mom_v.at[at], mom_h.at[at])
    eye = lax.broadcasted_iota(jnp.int32, (kr, 128), 0) == lax.broadcasted_iota(jnp.int32, (kr, 128), 1)

    def columns(norms):
        norms = jnp.broadcast_to(jnp.sqrt(norms + EPSILON), (norms.shape[0], kr, 128))
        return jnp.sum(jnp.where(eye[None], norms, 0.0), axis=2, keepdims=True)

    own = rh[:, pl.ds(pl.multiple_of(g * half, half), half)].astype(f32).reshape(rho.shape)
    own_q = (own / columns(nb[:, g])).astype(bf16).reshape(RANK, half)
    other_q = (rho[...].astype(f32) / columns(nb[:, o])).astype(bf16).reshape(RANK, half)
    for p, q, factor in ((g, own_q, lh), (o, other_q, oth)):
        for k in range(CHUNKS):
            at = pl.ds(k * chunk, chunk)
            new_v[p, at] = w[p, at] - STEP * mm(factor[at], q)
            out(new_v.at[p, at], new_h.at[p, at])
    fac_o[...] = share[...] / columns(nb[r, g][None])[0]
    own_pre = base[g] - STEP * mm(tl[0], own_q)
    other_pre = base[o] - STEP * mm(tl[1], other_q)
    gate = jnp.where(g == 0, own_pre, other_pre)
    up = jnp.where(g == 0, other_pre, own_pre)
    hid_o[...] = (gate / (1.0 + jnp.exp(-gate)) * up).astype(bf16)
    for copy in copies:
        copy.wait()


def tri_half(e):
    i, j = (lax.broadcasted_iota(jnp.int32, e.shape, d) for d in (0, 1))
    return jnp.where(i > j, e, jnp.where(i == j, 0.5 * e, 0.0))


def inverse_kernel(gram, inv_o, a, w, s):
    n = RANK
    i, j = (lax.broadcasted_iota(jnp.int32, (n, n), d) for d in (0, 1))
    eye = jnp.where(i == j, 1.0, 0.0)
    diagonal = jnp.where(i == j, gram[...], 0.0)
    down = lax.rsqrt(jnp.sum(diagonal, axis=1, keepdims=True))
    across = lax.rsqrt(jnp.sum(diagonal, axis=0, keepdims=True))
    a[...] = gram[...] * down * across
    first = jnp.where(i == j, 0.0, a[...])
    w[...] = eye - tri_half(first)

    def step(state):
        count, _ = state
        left = w[...]
        e = mm(mm(left, a[...], NN, HI), left, NT, HI) - eye
        w[...] = left - mm(tri_half(e), left, NN, HI)
        return count + 1, jnp.max(jnp.abs(e))

    _, worst = lax.while_loop(lambda t: (t[0] < 12) & ~(t[1] < 4e-4), step, (0, jnp.float32(1.0)))
    inv_o[...] = w[...] * across

    @pl.when(~(worst < 4e-4))
    def _():
        s[:, :n] = gram[...]
        s[:, n:] = eye
        row = lax.broadcasted_iota(jnp.int32, (n, 1), 0)

        def eliminate(k, _):
            line = s[pl.ds(k, 1), :]
            column = jnp.sum(jnp.where(j == k, s[:, :n], 0.0), axis=1, keepdims=True)
            pivot = jnp.sum(jnp.where(row == k, column, 0.0), axis=0, keepdims=True)
            s[...] = s[...] - jnp.where(row > k, column / pivot, 0.0) * line
            return 0

        lax.fori_loop(0, n, eliminate, 0)
        pivots = jnp.sum(jnp.where(i == j, s[:, :n], 0.0), axis=1, keepdims=True)
        inv_o[...] = s[:, n:] / jnp.sqrt(pivots)


def vmem(*shape, dtype=f32):
    return pltpu.VMEM(shape, dtype)


def pairs(n):
    return pltpu.SemaphoreType.DMA((2, n))


def call(kernel, ins, outs, scratch, args, collective_id=None, limit=24):
    where = {"v": pltpu.VMEM, "h": pltpu.HBM}
    params = {} if collective_id is None else dict(collective_id=collective_id, has_side_effects=True)
    return pl.pallas_call(
        kernel,
        out_shape=[jax.ShapeDtypeStruct(s, t) for s, t, _ in outs],
        in_specs=[pl.BlockSpec(memory_space=where[k]) for k in ins],
        out_specs=[pl.BlockSpec(memory_space=where[k]) for _, _, k in outs],
        scratch_shapes=scratch,
        compiler_params=pltpu.CompilerParams(vmem_limit_bytes=int(limit * 2**20), **params),
    )(*args)


def local(sizes, momentum, gradient, factor_q, weights, tokens):
    nr, nc, ng = sizes
    nx, nz = NX, nc // NX
    mom, grad, fq = momentum[0], gradient[0], factor_q[0].T
    rows, hid = mom.shape
    part, kr, nb = nx * nr, RANK // nr, BATCH // nr
    half = hid // ng
    left, gram, base, bufh = call(
        functools.partial(left_kernel, sizes),
        "hhhhh",
        [((rows, RANK), bf16, "v"), ((RANK, RANK), f32, "v"), ((2, nb, half), f32, "v"), ((rows, hid), bf16, "v")],
        [
            vmem(rows, hid), vmem(rows, hid, dtype=bf16), vmem(kr, hid), vmem(*weights.shape), vmem(*tokens.shape, dtype=bf16),
            pltpu.SemaphoreType.DMA((5,)), vmem(nr, kr, hid, dtype=bf16),
            vmem(nx, rows // nx, RANK), vmem(nx, rows // nx, RANK, dtype=bf16), vmem(nx - 1, rows // nx, RANK, dtype=bf16),
            vmem(nz, rows // nc, RANK), vmem(nz, rows // nc, RANK, dtype=bf16), vmem(nz - 1, rows // nc, RANK, dtype=bf16),
            vmem(nx, nz, rows // nc, RANK, dtype=bf16),
            vmem(part, RANK // part, RANK), vmem(part - 1, RANK // part, RANK), vmem(part, RANK // part, RANK),
            vmem(nr, 2, nb, half), vmem(nr - 1, 2, nb, half),
            pairs(nr - 1), pairs(nx - 1), pairs(nz - 1), pairs(nz - 1), pairs(nx - 1), pairs(part - 1), pairs(part - 1),
            pairs(nr - 1),
        ],
        (mom, grad, fq, weights, tokens), 0, limit=52.3,
    )
    (linv,) = call(
        inverse_kernel, "v", [((RANK, RANK), f32, "v")],
        [vmem(RANK, RANK), vmem(RANK, RANK), vmem(RANK, 2 * RANK)], (gram,),
    )
    lh, oth, rh, rho, norms, share, tl = call(
        functools.partial(right_kernel, sizes),
        "vvvv",
        [
            ((rows, RANK), bf16, "v"), ((rows, RANK), bf16, "v"), ((RANK, hid), bf16, "v"), ((nr, kr, half), bf16, "v"),
            ((nr, ng, 1, 128), f32, "v"), ((kr, hid), f32, "v"), ((2, nb, RANK), bf16, "v"),
        ],
        [
            vmem(nx, nz, rows // nc, RANK, dtype=bf16),
            vmem(nx, nz, rows // nc, RANK, dtype=bf16), vmem(nr, kr, hid), vmem(nr, kr, hid, dtype=bf16),
            vmem(nr - 1, kr, hid, dtype=bf16), vmem(nr, nb, RANK), vmem(nr, nb, RANK, dtype=bf16),
            vmem(nr - 1, nb, RANK, dtype=bf16), vmem(nb, RANK, dtype=bf16), vmem(nb, RANK, dtype=bf16),
            vmem(nr, kr, hid, dtype=bf16), vmem(kr, half, dtype=bf16), vmem(nr, kr, half, dtype=bf16),
            vmem(1, 128), vmem(ng, nx, 1, 128), vmem(nz, ng, 1, 128), vmem(nr, ng, 1, 128),
            pairs(1), pairs(nr - 1), pairs(nr - 1), pairs(nz - 1), pairs(nx - 1), pairs(nr - 1), pairs(1), pairs(nr - 1),
            pairs(ng * nx - 1), pairs(nz - 1), pairs(nr - 1), pairs(1),
        ],
        (bufh, left, linv, tokens), 1,
    )
    mom_new, new, fac, hidden = call(
        last_kernel, "v" * 11,
        [((rows, hid), f32, "h"), (weights.shape, f32, "h"), ((kr, hid), f32, "v"), ((nb, half), bf16, "v")],
        [vmem(rows, hid), vmem(*weights.shape), pltpu.SemaphoreType.DMA((3 * CHUNKS,))],
        (mom, grad, weights, base, lh, oth, rh, rho, norms, share, tl),
    )
    return mom_new[None], fac.T[None], new, hidden


def solution(mesh):
    sizes = tuple(mesh.shape[a] for a in ("row", "col", "grp"))
    in_specs = (
        P("grp", "row", "col"),
        P("grp", "row", "col"),
        P("grp", "col", "row"),
        P(None, "row", ("col", "grp")),
        P(None, "row"),
    )
    out_specs = (
        P("grp", "row", "col"),
        P("grp", "col", "row"),
        P(None, "row", ("col", "grp")),
        P("row", ("col", "grp")),
    )
    return jax.shard_map(
        functools.partial(local, sizes), mesh=mesh, in_specs=in_specs, out_specs=out_specs, check_vma=False
    )
```

```python
import functools
import math

import jax
import jax.numpy as jnp
from jax import lax
from jax.experimental import pallas as pl
from jax.experimental.pallas import tpu as pltpu
from jax.sharding import PartitionSpec as P

D = 4096
HID = 16384
RANK = 256
BATCH = 256
FEEDBACK = 0.05
EPSILON = 1e-06
STEP = 0.4 * math.sqrt(max(D, HID))
CHUNKS = 4
NEAR = 0.16
NX = 4

f32, bf16 = jnp.float32, jnp.bfloat16
HI = lax.Precision.HIGHEST
MESH = pl.DeviceIdType.MESH
NN = (((1,), (0,)), ((), ()))
NT = (((1,), (1,)), ((), ()))
TN = (((0,), (0,)), ((), ()))


def mm(a, b, dims=NN, precision=None):
    return lax.dot_general(a, b, dims, precision=precision, preferred_element_type=f32)


def around(i, n):
    return [i if d == 0 else i + d - jnp.where(i + d >= n, n, 0) for d in range(n)]


class Place:
    def __init__(self, sizes):
        self.nr, self.nc, self.ng = sizes
        self.nx, self.nz = NX, self.nc // NX
        self.r, self.c, self.g = (lax.axis_index(a) for a in ("row", "col", "grp"))
        self.x, self.z = lax.rem(self.c, self.nx), lax.div(self.c, self.nx)
        self.rs, self.xs, self.zs = around(self.r, self.nr), around(self.x, self.nx), around(self.z, self.nz)
        self.gs = [self.g, 1 - self.g]

    def at(self, dr=0, dx=0, dz=0, dg=0):
        return (self.rs[dr], self.zs[dz] * self.nx + self.xs[dx], self.gs[dg])


def greet(partners):
    barrier = pltpu.get_barrier_semaphore()
    for device in partners:
        pl.semaphore_signal(barrier, inc=1, device_id=device, device_id_type=MESH)
    return lambda: pl.semaphore_wait(barrier, len(partners))


def send(src, dst, sems, k, device):
    copy = pltpu.make_async_remote_copy(
        src_ref=src, dst_ref=dst, send_sem=sems.at[0, k], recv_sem=sems.at[1, k], device_id=device, device_id_type=MESH
    )
    copy.start()
    return copy


def arrived(copies):
    for copy in copies:
        copy.wait_recv()


def left_kernel(sizes, mom_h, grad_h, fq_h, w_h, tok_h, left_o, gram_o, base_o, bufh,
                mom, grad, fq, w, tok, s_in, qbuf, part, partb, rx, sx, sxb, rz, l512, gp, rg, gf, pre, rpre,
                s_q, s_x, s_z, s_az, s_ax, s_g, s_ag, s_p):
    at = Place(sizes)
    nr, nx, nz = at.nr, at.nx, at.nz
    plane = [(dx, dr) for dx in range(nx) for dr in range(nr) if dx or dr]
    ready = greet([at.at(dr=dr, dx=dx) for dx, dr in plane] + [at.at(dz=d) for d in range(1, nz)])
    r, x, z = at.r, at.x, at.z
    loads = [
        pltpu.make_async_copy(a, b, s_in.at[k])
        for k, (a, b) in enumerate(((fq_h, fq), (mom_h, mom), (grad_h, grad), (tok_h, tok), (w_h, w)))
    ]
    for load in loads:
        load.start()
    loads[0].wait()
    qbuf[r] = fq[...].astype(bf16)
    ready()
    got_q = [send(qbuf.at[r], qbuf.at[r], s_q, d - 1, at.at(dr=d)) for d in range(1, nr)]
    loads[1].wait()
    loads[2].wait()
    bufh[...] = (mom[...] + grad[...].astype(f32)).astype(bf16)
    arrived(got_q)
    part[...] = mm(bufh[...], qbuf[...].reshape(RANK, -1), NT).reshape(part.shape)
    partb[...] = part[...].astype(bf16)
    got_x = [send(partb.at[at.xs[d]], rx.at[d - 1], s_x, d - 1, at.at(dx=d)) for d in range(1, nx)]
    loads[3].wait()
    loads[4].wait()
    for p in range(2):
        high = w[p].astype(bf16)
        low = (w[p] - high.astype(f32)).astype(bf16)
        pre[:, p] = (mm(tok[...], high) + mm(tok[...], low)).reshape(pre[:, p].shape)
    arrived(got_x)
    sx[...] = (part[x] + jnp.sum(rx[...].astype(f32), axis=0)).reshape(sx.shape)
    sxb[...] = sx[...].astype(bf16)
    got_z = [send(sxb.at[at.zs[d]], rz.at[d - 1], s_z, d - 1, at.at(dz=d)) for d in range(1, nz)]
    got_p = [send(pre.at[at.rs[d]], rpre.at[d - 1], s_p, d - 1, at.at(dr=d)) for d in range(1, nr)]
    arrived(got_z)
    l512[x, z] = (sx[z] + jnp.sum(rz[...].astype(f32), axis=0)).astype(bf16)
    got_az = [send(l512.at[x, z], l512.at[x, z], s_az, d - 1, at.at(dz=d)) for d in range(1, nz)]
    arrived(got_az)
    rows = l512[x].reshape(-1, RANK)
    gram = mm(rows, rows, TN)
    h = RANK // 2
    i, j = (lax.broadcasted_iota(jnp.int32, (h, h), d) for d in (0, 1))
    packed = jnp.where(i >= j, gram[:h, :h], gram[h:, h:])
    gp[: gp.shape[0] // 2, :-1] = packed.reshape(gp.shape[0] // 2, -1, h)
    gp[gp.shape[0] // 2 :, :-1] = gram[h:, :h].reshape(gp.shape[0] // 2, -1, h)
    gp[:, -1:] = jnp.broadcast_to(
        jnp.sum(jnp.where(i == j, gram[h:, h:], 0.0), axis=0, keepdims=True), (gp.shape[0], 1, h)
    )
    got_g = []
    for k, (dx, dr) in enumerate(plane):
        m = at.xs[dx] * nr + at.rs[dr]
        got_g.append(send(gp.at[m], rg.at[k], s_g, k, at.at(dr=dr, dx=dx)))
    got_ax = [send(l512.at[x], l512.at[x], s_ax, d - 1, at.at(dx=d)) for d in range(1, nx)]
    arrived(got_g)
    m = x * nr + r
    gf[m] = gp[m] + jnp.sum(rg[...], axis=0)
    got_ag = [send(gf.at[m], gf.at[m], s_ag, k, at.at(dr=dr, dx=dx)) for k, (dx, dr) in enumerate(plane)]
    arrived(got_p)
    base_o[...] = pre[r] + jnp.sum(rpre[...], axis=0)
    arrived(got_ax)
    left_o[...] = l512[...].reshape(left_o.shape)
    arrived(got_ag)
    gram_o[:RANK] = gf[:, :-1].reshape(RANK, -1)
    gram_o[RANK:] = jnp.broadcast_to(gf[0, -1:], (8, gf.shape[2]))
    for copies in (got_q, got_x, got_p, got_z, got_az, got_g, got_ax, got_ag):
        for copy in copies:
            copy.wait_send()


def tri_half(e):
    i, j = (lax.broadcasted_iota(jnp.int32, e.shape, d) for d in (0, 1))
    return jnp.where(i > j, e, jnp.where(i == j, 0.5 * e, 0.0))


def residual(w, a, precision=None):
    i, j = (lax.broadcasted_iota(jnp.int32, a.shape, d) for d in (0, 1))
    return mm(mm(w, a, NN, precision), w, NT, precision) - jnp.where(i == j, 1.0, 0.0)


def start_kernel(packed, a_o, w_o, across_o, near_o, gram, s):
    n, h = RANK, RANK // 2
    i, j = (lax.broadcasted_iota(jnp.int32, (h, h), d) for d in (0, 1))
    both, turned = packed[:h], packed[:h].T
    gram[:h, :h] = jnp.where(i >= j, both, turned)
    gram[h:, h:] = jnp.where(i > j, turned, jnp.where(i == j, packed[n : n + 1], both))
    gram[h:, :h] = packed[h:n]
    gram[:h, h:] = packed[h:n].T
    i, j = (lax.broadcasted_iota(jnp.int32, (n, n), d) for d in (0, 1))
    eye = jnp.where(i == j, 1.0, 0.0)
    diagonal = jnp.where(i == j, gram[...], 0.0)
    down = lax.rsqrt(jnp.sum(diagonal, axis=1, keepdims=True))
    across = lax.rsqrt(jnp.sum(diagonal, axis=0, keepdims=True))
    a = gram[...] * down * across
    a_o[...] = a
    across_o[...] = jnp.broadcast_to(across, across_o.shape)
    w = eye - tri_half(jnp.where(i == j, 0.0, a))
    w = w - mm(tri_half(residual(w, a)), w)
    w_o[...] = w
    e = residual(w, a)
    far = jnp.sum(e * e)
    near_o[...] = jnp.ones(near_o.shape, f32)

    @pl.when(~(far < NEAR))
    def _():
        s[:, :n] = gram[...]
        s[:, n:] = eye
        row = lax.broadcasted_iota(jnp.int32, (n, 1), 0)

        def eliminate(k, _):
            line = s[pl.ds(k, 1), :]
            column = jnp.sum(jnp.where(j == k, s[:, :n], 0.0), axis=1, keepdims=True)
            pivot = jnp.sum(jnp.where(row == k, column, 0.0), axis=0, keepdims=True)
            s[...] = s[...] - jnp.where(row > k, column / pivot, 0.0) * line
            return 0

        lax.fori_loop(0, n, eliminate, 0)
        pivots = jnp.sum(jnp.where(i == j, s[:, :n], 0.0), axis=1, keepdims=True)
        w_o[...] = s[:, n:] / jnp.sqrt(pivots)
        across_o[...] = jnp.ones(across_o.shape, f32)
        near_o[...] = jnp.zeros(near_o.shape, f32)


def right_kernel(sizes, bufh, left, a, w, across, near, tok, lh_o, oth_o, rh_o, rho_o, nb_o, share_o, tl_o,
                 lh, oth, rt, rtb, rrt, tl, tlb, rtl, tls, tlo, rh, sho, rho, sq, sqz, sqx, nb,
                 s_l, s_rt, s_tl, s_lz, s_lx, s_rh, s_sh, s_ro, s_sq, s_sx, s_nb, s_to):
    at = Place(sizes)
    nr, nx, nz, ng = at.nr, at.nx, at.nz, at.ng
    r, c, g, x, z = at.r, at.c, at.g, at.x, at.z
    line_up = [(dz, dg) for dz in range(nz) for dg in range(ng) if dz or dg]
    ready = greet(
        [at.at(dr=d) for d in range(1, nr)] + [at.at(dx=d) for d in range(1, nx)] + [at.at(dz=dz, dg=dg) for dz, dg in line_up]
    )
    o = 1 - g
    kr = RANK // nr
    half = sho.shape[1]

    inverse = w[...]
    for _ in range(3):
        error = jnp.where(near[:1, :1] > 0, tri_half(residual(inverse, a[...], HI)), 0.0)
        inverse = inverse - mm(error, inverse, NN, HI)
    inverse = inverse * across[:1]
    high = inverse.astype(bf16)
    low = (inverse - high.astype(f32)).astype(bf16)
    left_h = (mm(left[...], high, NT) + mm(left[...], low, NT)).astype(bf16)
    lh[...] = left_h.reshape(lh.shape)
    ready()
    got_l = [send(lh.at[x, z], oth.at[x, z], s_l, 0, at.at(dg=1))]
    rt[...] = mm(left_h, bufh[...], TN).reshape(rt.shape)
    rtb[...] = rt[...].astype(bf16)
    got_rt = [send(rtb.at[at.rs[d]], rrt.at[d - 1], s_rt, d - 1, at.at(dr=d)) for d in range(1, nr)]
    tl[...] = mm(tok[...], left_h).reshape(tl.shape)
    tlb[...] = tl[...].astype(bf16)
    got_tl = [send(tlb.at[at.rs[d]], rtl.at[d - 1], s_tl, d - 1, at.at(dr=d)) for d in range(1, nr)]
    arrived(got_rt)
    share = rt[r] + jnp.sum(rrt[...].astype(f32), axis=0)
    share_o[...] = share
    rh[r] = share.astype(bf16)
    sho[...] = share_o[:, pl.ds(pl.multiple_of(o * half, half), half)].astype(bf16)
    got_sh = [send(sho, rho.at[r], s_sh, 0, at.at(dg=1))]
    eye = lax.broadcasted_iota(jnp.int32, (kr, 128), 0) == lax.broadcasted_iota(jnp.int32, (kr, 128), 1)
    squares = jnp.sum(share * share, axis=1, keepdims=True)
    line = jnp.sum(jnp.where(eye, squares, 0.0), axis=0, keepdims=True)
    sqz[g, z] = line
    sq[...] = line
    got_sq = [send(sq, sqz.at[g, z], s_sq, k, at.at(dz=dz, dg=dg)) for k, (dz, dg) in enumerate(line_up)]
    got_rh = [send(rh.at[r], rh.at[r], s_rh, d - 1, at.at(dr=d)) for d in range(1, nr)]
    arrived(got_tl)
    tls[...] = (tl[r] + jnp.sum(rtl[...].astype(f32), axis=0)).astype(bf16)
    got_to = [send(tls, tlo, s_to, 0, at.at(dg=1))]
    arrived(got_l)
    got_lz = [send(oth.at[x, z], oth.at[x, z], s_lz, d - 1, at.at(dz=d)) for d in range(1, nz)]
    arrived(got_sh)
    got_ro = [send(rho.at[r], rho.at[r], s_ro, d - 1, at.at(dr=d)) for d in range(1, nr)]
    arrived(got_sq)
    sqx[x] = jnp.sum(sqz[...], axis=1)
    got_sx = [send(sqx.at[x], sqx.at[x], s_sx, d - 1, at.at(dx=d)) for d in range(1, nx)]
    arrived(got_lz)
    got_lx = [send(oth.at[x], oth.at[x], s_lx, d - 1, at.at(dx=d)) for d in range(1, nx)]
    arrived(got_sx)
    nb[r] = jnp.sum(sqx[...], axis=0)
    got_nb = [send(nb.at[r], nb.at[r], s_nb, d - 1, at.at(dr=d)) for d in range(1, nr)]
    lh_o[...] = lh[...].reshape(lh_o.shape)
    arrived(got_rh)
    rh_o[...] = rh[...].reshape(rh_o.shape)
    arrived(got_lx)
    oth_o[...] = oth[...].reshape(oth_o.shape)
    arrived(got_nb)
    nb_o[...] = nb[...]
    arrived(got_ro)
    rho_o[...] = rho[...]
    arrived(got_to)
    tl_o[0] = tls[...]
    tl_o[1] = tlo[...]
    for copies in (got_l, got_rt, got_tl, got_lz, got_sh, got_sq, got_sx, got_rh, got_lx, got_nb, got_ro, got_to):
        for copy in copies:
            copy.wait_send()


def last_kernel(mom, grad, w, base, lh, oth, rh, rho, nb, share, tl, mom_h, new_h, fac_o, hid_o, mom_v, new_v, sems):
    r, g = lax.axis_index("row"), lax.axis_index("grp")
    o = 1 - g
    nr, kr, half = rho.shape
    rows = lh.shape[0]
    chunk = rows // CHUNKS
    copies = []

    def out(src, dst):
        copies.append(pltpu.make_async_copy(src, dst, sems.at[len(copies)]))
        copies[-1].start()

    for k in range(CHUNKS):
        at = pl.ds(k * chunk, chunk)
        mom_v[at] = mom[at] + grad[at].astype(f32) - FEEDBACK * mm(lh[at], rh[...])
        out(mom_v.at[at], mom_h.at[at])
    eye = lax.broadcasted_iota(jnp.int32, (kr, 128), 0) == lax.broadcasted_iota(jnp.int32, (kr, 128), 1)

    def columns(norms):
        norms = jnp.broadcast_to(jnp.sqrt(norms + EPSILON), (norms.shape[0], kr, 128))
        return jnp.sum(jnp.where(eye[None], norms, 0.0), axis=2, keepdims=True)

    own = rh[:, pl.ds(pl.multiple_of(g * half, half), half)].astype(f32).reshape(rho.shape)
    own_q = (own / columns(nb[:, g])).astype(bf16).reshape(RANK, half)
    other_q = (rho[...].astype(f32) / columns(nb[:, o])).astype(bf16).reshape(RANK, half)
    for p, q, factor in ((g, own_q, lh), (o, other_q, oth)):
        for k in range(CHUNKS):
            at = pl.ds(k * chunk, chunk)
            new_v[p, at] = w[p, at] - STEP * mm(factor[at], q)
            out(new_v.at[p, at], new_h.at[p, at])
    fac_o[...] = share[...] / columns(nb[r, g][None])[0]
    own_pre = base[g] - STEP * mm(tl[0], own_q)
    other_pre = base[o] - STEP * mm(tl[1], other_q)
    gate = jnp.where(g == 0, own_pre, other_pre)
    up = jnp.where(g == 0, other_pre, own_pre)
    hid_o[...] = (gate / (1.0 + jnp.exp(-gate)) * up).astype(bf16)
    for copy in copies:
        copy.wait()


def vmem(*shape, dtype=f32):
    return pltpu.VMEM(shape, dtype)


def pairs(n):
    return pltpu.SemaphoreType.DMA((2, n))


def call(kernel, ins, outs, scratch, args, collective_id=None, limit=24):
    where = {"v": pltpu.VMEM, "h": pltpu.HBM}
    params = {} if collective_id is None else dict(collective_id=collective_id, has_side_effects=True)
    return pl.pallas_call(
        kernel,
        out_shape=[jax.ShapeDtypeStruct(s, t) for s, t, _ in outs],
        in_specs=[pl.BlockSpec(memory_space=where[k]) for k in ins],
        out_specs=[pl.BlockSpec(memory_space=where[k]) for _, _, k in outs],
        scratch_shapes=scratch,
        compiler_params=pltpu.CompilerParams(vmem_limit_bytes=int(limit * 2**20), **params),
    )(*args)


def local(sizes, momentum, gradient, factor_q, weights, tokens):
    nr, nc, ng = sizes
    nx, nz = NX, nc // NX
    mom, grad, fq = momentum[0], gradient[0], factor_q[0].T
    rows, hid = mom.shape
    part, kr, nb = nx * nr, RANK // nr, BATCH // nr
    half = hid // ng

    def piece(n):
        return n, RANK // part + 1, RANK // 2

    left, gram, base, bufh = call(
        functools.partial(left_kernel, sizes),
        "hhhhh",
        [((rows, RANK), bf16, "v"), ((RANK + 8, RANK // 2), f32, "v"), ((2, nb, half), f32, "v"), ((rows, hid), bf16, "v")],
        [
            vmem(rows, hid), vmem(rows, hid, dtype=bf16), vmem(kr, hid), vmem(*weights.shape), vmem(*tokens.shape, dtype=bf16),
            pltpu.SemaphoreType.DMA((5,)), vmem(nr, kr, hid, dtype=bf16),
            vmem(nx, rows // nx, RANK), vmem(nx, rows // nx, RANK, dtype=bf16), vmem(nx - 1, rows // nx, RANK, dtype=bf16),
            vmem(nz, rows // nc, RANK), vmem(nz, rows // nc, RANK, dtype=bf16), vmem(nz - 1, rows // nc, RANK, dtype=bf16),
            vmem(nx, nz, rows // nc, RANK, dtype=bf16),
            vmem(*piece(part)), vmem(*piece(part - 1)), vmem(*piece(part)),
            vmem(nr, 2, nb, half), vmem(nr - 1, 2, nb, half),
            pairs(nr - 1), pairs(nx - 1), pairs(nz - 1), pairs(nz - 1), pairs(nx - 1), pairs(part - 1), pairs(part - 1),
            pairs(nr - 1),
        ],
        (mom, grad, fq, weights, tokens), 0, limit=52.3,
    )
    square = ((RANK, RANK), f32, "v")
    start = call(
        start_kernel, "v", [square, square, ((8, RANK), f32, "v"), ((8, 128), f32, "v")],
        [vmem(RANK, RANK), vmem(RANK, 2 * RANK)], (gram,),
    )
    lh, oth, rh, rho, norms, share, tl = call(
        functools.partial(right_kernel, sizes),
        "v" * 7,
        [
            ((rows, RANK), bf16, "v"), ((rows, RANK), bf16, "v"), ((RANK, hid), bf16, "v"), ((nr, kr, half), bf16, "v"),
            ((nr, ng, 1, 128), f32, "v"), ((kr, hid), f32, "v"), ((2, nb, RANK), bf16, "v"),
        ],
        [
            vmem(nx, nz, rows // nc, RANK, dtype=bf16),
            vmem(nx, nz, rows // nc, RANK, dtype=bf16), vmem(nr, kr, hid), vmem(nr, kr, hid, dtype=bf16),
            vmem(nr - 1, kr, hid, dtype=bf16), vmem(nr, nb, RANK), vmem(nr, nb, RANK, dtype=bf16),
            vmem(nr - 1, nb, RANK, dtype=bf16), vmem(nb, RANK, dtype=bf16), vmem(nb, RANK, dtype=bf16),
            vmem(nr, kr, hid, dtype=bf16), vmem(kr, half, dtype=bf16), vmem(nr, kr, half, dtype=bf16),
            vmem(1, 128), vmem(ng, nz, 1, 128), vmem(nx, ng, 1, 128), vmem(nr, ng, 1, 128),
            pairs(1), pairs(nr - 1), pairs(nr - 1), pairs(nz - 1), pairs(nx - 1), pairs(nr - 1), pairs(1), pairs(nr - 1),
            pairs(ng * nz - 1), pairs(nx - 1), pairs(nr - 1), pairs(1),
        ],
        (bufh, left, *start, tokens), 1,
    )
    mom_new, new, fac, hidden = call(
        last_kernel, "v" * 11,
        [((rows, hid), f32, "h"), (weights.shape, f32, "h"), ((kr, hid), f32, "v"), ((nb, half), bf16, "v")],
        [vmem(rows, hid), vmem(*weights.shape), pltpu.SemaphoreType.DMA((3 * CHUNKS,))],
        (mom, grad, weights, base, lh, oth, rh, rho, norms, share, tl),
    )
    return mom_new[None], fac.T[None], new, hidden


def solution(mesh):
    sizes = tuple(mesh.shape[a] for a in ("row", "col", "grp"))
    in_specs = (
        P("grp", "row", "col"),
        P("grp", "row", "col"),
        P("grp", "col", "row"),
        P(None, "row", ("col", "grp")),
        P(None, "row"),
    )
    out_specs = (
        P("grp", "row", "col"),
        P("grp", "col", "row"),
        P(None, "row", ("col", "grp")),
        P("row", ("col", "grp")),
    )
    return jax.shard_map(
        functools.partial(local, sizes), mesh=mesh, in_specs=in_specs, out_specs=out_specs, check_vma=False
    )
```

```python
import functools
import math

import jax
import jax.numpy as jnp
from jax import lax
from jax.experimental import pallas as pl
from jax.experimental.pallas import tpu as pltpu
from jax.sharding import PartitionSpec as P

D = 4096
HID = 16384
RANK = 256
BATCH = 256
FEEDBACK = 0.05
EPSILON = 1e-06
STEP = 0.4 * math.sqrt(max(D, HID))
CHUNKS = 4
NEAR = 0.16
NX = 4

f32, bf16 = jnp.float32, jnp.bfloat16
HI = lax.Precision.HIGHEST
MESH = pl.DeviceIdType.MESH
NN = (((1,), (0,)), ((), ()))
NT = (((1,), (1,)), ((), ()))
TN = (((0,), (0,)), ((), ()))


def mm(a, b, dims=NN, precision=None):
    return lax.dot_general(a, b, dims, precision=precision, preferred_element_type=f32)


def around(i, n):
    return [i if d == 0 else i + d - jnp.where(i + d >= n, n, 0) for d in range(n)]


def far_first(offsets, *rings):
    def way(offset):
        return sum(min(d, n - d) for d, n in zip(offset, rings))

    return sorted((offset for offset in offsets if any(offset)), key=lambda offset: -way(offset))


class Place:
    def __init__(self, sizes):
        self.nr, self.nc, self.ng = sizes
        self.nx, self.nz, self.ny = NX, self.nc // NX, self.nr // 2
        self.r, self.c, self.g = (lax.axis_index(a) for a in ("row", "col", "grp"))
        self.x, self.z = lax.rem(self.c, self.nx), lax.div(self.c, self.nx)
        self.core = lax.rem(self.r, 2)
        self.xs = around(self.x, self.nx)
        ys = around(lax.div(self.r, 2), self.ny)
        self.rs = {(dy, dc): 2 * ys[dy] + (1 - self.core if dc else self.core) for dy in range(self.ny) for dc in range(2)}
        self.row = far_first(self.rs, self.ny)
        self.line = [(d,) for d in range(1, self.nx)]
        self.line = [d for (d,) in far_first(self.line, self.nx)]
        self.plane = far_first([(dx, *d) for dx in range(self.nx) for d in self.rs], self.nx, self.ny)
        last = self.nz - 1
        self.stack = [
            jnp.where(
                self.z <= last // 2,
                last - k - jnp.where(last - k <= self.z, 1, 0),
                k + jnp.where(k >= self.z, 1, 0),
            )
            for k in range(last)
        ]
        around_both = around(self.g * self.nz + self.z, self.ng * self.nz)
        self.ring = [around_both[d] for (d,) in far_first([(d,) for d in range(len(around_both))], len(around_both))]

    def at(self, row=(0, 0), dx=0, z=None, g=None):
        z = self.z if z is None else z
        return (self.rs[row], z * self.nx + self.xs[dx], self.g if g is None else g)

    def up(self, k):
        g = jnp.where(self.ring[k] >= self.nz, 1, 0)
        return self.at(z=self.ring[k] - g * self.nz, g=g)


def greet(partners):
    barrier = pltpu.get_barrier_semaphore()
    for device in partners:
        pl.semaphore_signal(barrier, inc=1, device_id=device, device_id_type=MESH)
    return lambda: pl.semaphore_wait(barrier, len(partners))


def remote(src, dst, sent, received, device):
    return pltpu.make_async_remote_copy(
        src_ref=src, dst_ref=dst, send_sem=sent, recv_sem=received, device_id=device, device_id_type=MESH
    )


def send(src, dst, sems, k, device):
    copy = remote(src, dst, sems.at[0, k], sems.at[1, k], device)
    copy.start()
    return copy


def send_line(pick, slot, sems, at):
    waits = []
    for k, other in enumerate(at.stack):
        device = at.at(z=other)
        remote(pick(other), slot(at.z), sems.at[0, k], sems.at[1, at.z], device).start()
        waits.append(remote(pick(other), slot(other), sems.at[0, k], sems.at[1, other], device))
    return waits


def arrived(copies):
    for copy in copies:
        copy.wait_recv()


def left_kernel(sizes, mom_h, grad_h, fq_h, w_h, tok_h, left_o, gram_o, base_o, bufh,
                mom, grad, fq, w, tok, s_in, qbuf, part, partb, rx, sx, sxb, rz, l512, gp, rg, gf, pre, rpre,
                s_q, s_x, s_z, s_az, s_ax, s_g, s_ag, s_p):
    at = Place(sizes)
    nr, nx, nz = at.nr, at.nx, at.nz
    ready = greet([at.at(z=other) for other in at.stack] + [at.at(row=d[1:], dx=d[0]) for d in at.plane])
    r, x, z = at.r, at.x, at.z
    loads = [
        pltpu.make_async_copy(a, b, s_in.at[k])
        for k, (a, b) in enumerate(((fq_h, fq), (mom_h, mom), (grad_h, grad), (tok_h, tok), (w_h, w)))
    ]
    for load in loads:
        load.start()
    loads[0].wait()
    qbuf[r] = fq[...].astype(bf16)
    ready()
    got_q = [send(qbuf.at[r], qbuf.at[r], s_q, k, at.at(row=d)) for k, d in enumerate(at.row)]
    loads[1].wait()
    loads[2].wait()
    bufh[...] = (mom[...] + grad[...].astype(f32)).astype(bf16)
    arrived(got_q)
    part[...] = mm(bufh[...], qbuf[...].reshape(RANK, -1), NT).reshape(part.shape)
    partb[...] = part[...].astype(bf16)
    got_x = [send(partb.at[at.xs[d]], rx.at[k], s_x, k, at.at(dx=d)) for k, d in enumerate(at.line)]
    loads[3].wait()
    loads[4].wait()
    for p in range(2):
        high = w[p].astype(bf16)
        low = (w[p] - high.astype(f32)).astype(bf16)
        pre[:, p] = (mm(tok[...], high) + mm(tok[...], low)).reshape(pre[:, p].shape)
    arrived(got_x)
    sx[...] = (part[x] + jnp.sum(rx[...].astype(f32), axis=0)).reshape(sx.shape)
    sxb[...] = sx[...].astype(bf16)
    rz[z] = jnp.zeros(rz.shape[1:], bf16)
    got_z = send_line(lambda other: sxb.at[other], lambda place: rz.at[place], s_z, at)
    got_p = [send(pre.at[at.rs[d]], rpre.at[k], s_p, k, at.at(row=d)) for k, d in enumerate(at.row)]
    arrived(got_z)
    l512[x, z] = (sx[z] + jnp.sum(rz[...].astype(f32), axis=0)).astype(bf16)
    got_az = send_line(lambda other: l512.at[x, z], lambda place: l512.at[x, place], s_az, at)
    arrived(got_az)
    rows = l512[x].reshape(-1, RANK)
    gram = mm(rows, rows, TN)
    h = RANK // 2
    i, j = (lax.broadcasted_iota(jnp.int32, (h, h), d) for d in (0, 1))
    packed = jnp.where(i >= j, gram[:h, :h], gram[h:, h:])
    gp[: gp.shape[0] // 2, :-1] = packed.reshape(gp.shape[0] // 2, -1, h)
    gp[gp.shape[0] // 2 :, :-1] = gram[h:, :h].reshape(gp.shape[0] // 2, -1, h)
    gp[:, -1:] = jnp.broadcast_to(
        jnp.sum(jnp.where(i == j, gram[h:, h:], 0.0), axis=0, keepdims=True), (gp.shape[0], 1, h)
    )
    got_g = []
    for k, (dx, *d) in enumerate(at.plane):
        m = at.xs[dx] * nr + at.rs[*d]
        got_g.append(send(gp.at[m], rg.at[k], s_g, k, at.at(row=(*d,), dx=dx)))
    got_ax = [send(l512.at[x], l512.at[x], s_ax, k, at.at(dx=d)) for k, d in enumerate(at.line)]
    arrived(got_g)
    m = x * nr + r
    gf[m] = gp[m] + jnp.sum(rg[...], axis=0)
    got_ag = [send(gf.at[m], gf.at[m], s_ag, k, at.at(row=d[1:], dx=d[0])) for k, d in enumerate(at.plane)]
    arrived(got_p)
    base_o[...] = pre[r] + jnp.sum(rpre[...], axis=0)
    arrived(got_ax)
    left_o[...] = l512[...].reshape(left_o.shape)
    arrived(got_ag)
    gram_o[:RANK] = gf[:, :-1].reshape(RANK, -1)
    gram_o[RANK:] = jnp.broadcast_to(gf[0, -1:], (8, gf.shape[2]))
    for copies in (got_q, got_x, got_p, got_z, got_az, got_g, got_ax, got_ag):
        for copy in copies:
            copy.wait_send()


def tri_half(e):
    i, j = (lax.broadcasted_iota(jnp.int32, e.shape, d) for d in (0, 1))
    return jnp.where(i > j, e, jnp.where(i == j, 0.5 * e, 0.0))


def residual(w, a, precision=None):
    i, j = (lax.broadcasted_iota(jnp.int32, a.shape, d) for d in (0, 1))
    return mm(mm(w, a, NN, precision), w, NT, precision) - jnp.where(i == j, 1.0, 0.0)


def start_kernel(packed, a_o, w_o, across_o, near_o, gram, s):
    n, h = RANK, RANK // 2
    i, j = (lax.broadcasted_iota(jnp.int32, (h, h), d) for d in (0, 1))
    both, turned = packed[:h], packed[:h].T
    gram[:h, :h] = jnp.where(i >= j, both, turned)
    gram[h:, h:] = jnp.where(i > j, turned, jnp.where(i == j, packed[n : n + 1], both))
    gram[h:, :h] = packed[h:n]
    gram[:h, h:] = packed[h:n].T
    i, j = (lax.broadcasted_iota(jnp.int32, (n, n), d) for d in (0, 1))
    eye = jnp.where(i == j, 1.0, 0.0)
    diagonal = jnp.where(i == j, gram[...], 0.0)
    down = lax.rsqrt(jnp.sum(diagonal, axis=1, keepdims=True))
    across = lax.rsqrt(jnp.sum(diagonal, axis=0, keepdims=True))
    a = gram[...] * down * across
    a_o[...] = a
    across_o[...] = jnp.broadcast_to(across, across_o.shape)
    w = eye - tri_half(jnp.where(i == j, 0.0, a))
    w = w - mm(tri_half(residual(w, a)), w)
    w_o[...] = w
    e = residual(w, a)
    far = jnp.sum(e * e)
    near_o[...] = jnp.ones(near_o.shape, f32)

    @pl.when(~(far < NEAR))
    def _():
        s[:, :n] = gram[...]
        s[:, n:] = eye
        row = lax.broadcasted_iota(jnp.int32, (n, 1), 0)

        def eliminate(k, _):
            line = s[pl.ds(k, 1), :]
            column = jnp.sum(jnp.where(j == k, s[:, :n], 0.0), axis=1, keepdims=True)
            pivot = jnp.sum(jnp.where(row == k, column, 0.0), axis=0, keepdims=True)
            s[...] = s[...] - jnp.where(row > k, column / pivot, 0.0) * line
            return 0

        lax.fori_loop(0, n, eliminate, 0)
        pivots = jnp.sum(jnp.where(i == j, s[:, :n], 0.0), axis=1, keepdims=True)
        w_o[...] = s[:, n:] / jnp.sqrt(pivots)
        across_o[...] = jnp.ones(across_o.shape, f32)
        near_o[...] = jnp.zeros(near_o.shape, f32)


def right_kernel(sizes, bufh, left, a, w, across, near, tok, mom_h, grad_h, mom_o, lh_o, oth_o, rh_o, rho_o, nb_o, share_o, tl_o,
                 mom, grad, s_in, lh, oth, rt, rtb, rrt, tl, tlb, rtl, tls, tlo, rh, sho, rho, sq, sqz, sqx, nb,
                 s_l, s_rt, s_tl, s_lz, s_lx, s_rh, s_sh, s_ro, s_sq, s_sx, s_nb, s_to):
    at = Place(sizes)
    nr, nx, nz, ng = at.nr, at.nx, at.nz, at.ng
    r, c, g, x, z = at.r, at.c, at.g, at.x, at.z
    upwards = range(len(at.ring))
    ready = greet(
        [at.up(k) for k in upwards] + [at.at(row=d) for d in at.row] + [at.at(dx=d) for d in at.line]
    )
    o = 1 - g
    kr = RANK // nr
    half = sho.shape[1]

    loads = [pltpu.make_async_copy(mom_h, mom, s_in.at[0]), pltpu.make_async_copy(grad_h, grad, s_in.at[1])]
    for load in loads:
        load.start()
    inverse = w[...]
    for _ in range(3):
        error = jnp.where(near[:1, :1] > 0, tri_half(residual(inverse, a[...], HI)), 0.0)
        inverse = inverse - mm(error, inverse, NN, HI)
    inverse = inverse * across[:1]
    high = inverse.astype(bf16)
    low = (inverse - high.astype(f32)).astype(bf16)
    left_h = (mm(left[...], high, NT) + mm(left[...], low, NT)).astype(bf16)
    lh[...] = left_h.reshape(lh.shape)
    ready()
    got_l = [send(lh.at[x, z], oth.at[x, z], s_l, 0, at.at(g=o))]
    rt[...] = mm(left_h, bufh[...], TN).reshape(rt.shape)
    rtb[...] = rt[...].astype(bf16)
    got_rt = [send(rtb.at[at.rs[d]], rrt.at[k], s_rt, k, at.at(row=d)) for k, d in enumerate(at.row)]
    tl[...] = mm(tok[...], left_h).reshape(tl.shape)
    tlb[...] = tl[...].astype(bf16)
    got_tl = [send(tlb.at[at.rs[d]], rtl.at[k], s_tl, k, at.at(row=d)) for k, d in enumerate(at.row)]
    arrived(got_rt)
    share = rt[r] + jnp.sum(rrt[...].astype(f32), axis=0)
    share_o[...] = share
    rh[r] = share.astype(bf16)
    sho[...] = share_o[:, pl.ds(pl.multiple_of(o * half, half), half)].astype(bf16)
    got_sh = [send(sho, rho.at[r], s_sh, 0, at.at(g=o))]
    eye = lax.broadcasted_iota(jnp.int32, (kr, 128), 0) == lax.broadcasted_iota(jnp.int32, (kr, 128), 1)
    squares = jnp.sum(share * share, axis=1, keepdims=True)
    line = jnp.sum(jnp.where(eye, squares, 0.0), axis=0, keepdims=True)
    sqz[g, z] = line
    sq[...] = line
    got_sq = [send(sq, sqz.at[g, z], s_sq, k, at.up(k)) for k in upwards]
    got_rh = [send(rh.at[r], rh.at[r], s_rh, k, at.at(row=d)) for k, d in enumerate(at.row)]
    arrived(got_tl)
    tls[...] = (tl[r] + jnp.sum(rtl[...].astype(f32), axis=0)).astype(bf16)
    got_to = [send(tls, tlo, s_to, 0, at.at(g=o))]
    arrived(got_l)
    got_lz = send_line(lambda other: oth.at[x, z], lambda place: oth.at[x, place], s_lz, at)
    arrived(got_sh)
    got_ro = [send(rho.at[r], rho.at[r], s_ro, k, at.at(row=d)) for k, d in enumerate(at.row)]
    arrived(got_sq)
    sqx[x] = jnp.sum(sqz[...], axis=1)
    got_sx = [send(sqx.at[x], sqx.at[x], s_sx, k, at.at(dx=d)) for k, d in enumerate(at.line)]
    arrived(got_lz)
    got_lx = [send(oth.at[x], oth.at[x], s_lx, k, at.at(dx=d)) for k, d in enumerate(at.line)]
    arrived(got_sx)
    nb[r] = jnp.sum(sqx[...], axis=0)
    got_nb = [send(nb.at[r], nb.at[r], s_nb, k, at.at(row=d)) for k, d in enumerate(at.row)]
    lh_o[...] = lh[...].reshape(lh_o.shape)
    for load in loads:
        load.wait()
    arrived(got_rh)
    mom_o[...] = mom[...] + grad[...].astype(f32) - FEEDBACK * mm(left_h, rh[...].reshape(RANK, -1))
    rh_o[...] = rh[...].reshape(rh_o.shape)
    arrived(got_lx)
    oth_o[...] = oth[...].reshape(oth_o.shape)
    arrived(got_nb)
    nb_o[...] = nb[...]
    arrived(got_ro)
    rho_o[...] = rho[...]
    arrived(got_to)
    tl_o[0] = tls[...]
    tl_o[1] = tlo[...]
    for copies in (got_l, got_rt, got_tl, got_lz, got_sh, got_sq, got_sx, got_rh, got_lx, got_nb, got_ro, got_to):
        for copy in copies:
            copy.wait_send()


def last_kernel(mom, w, base, lh, oth, rh, rho, nb, share, tl, mom_h, new_h, fac_o, hid_o, new_v, sems):
    r, g = lax.axis_index("row"), lax.axis_index("grp")
    o = 1 - g
    nr, kr, half = rho.shape
    rows = lh.shape[0]
    chunk = rows // CHUNKS
    copies = []

    def out(src, dst):
        copies.append(pltpu.make_async_copy(src, dst, sems.at[len(copies)]))
        copies[-1].start()

    out(mom, mom_h)
    eye = lax.broadcasted_iota(jnp.int32, (kr, 128), 0) == lax.broadcasted_iota(jnp.int32, (kr, 128), 1)

    def columns(norms):
        norms = jnp.broadcast_to(jnp.sqrt(norms + EPSILON), (norms.shape[0], kr, 128))
        return jnp.sum(jnp.where(eye[None], norms, 0.0), axis=2, keepdims=True)

    own = rh[:, pl.ds(pl.multiple_of(g * half, half), half)].astype(f32).reshape(rho.shape)
    own_q = (own / columns(nb[:, g])).astype(bf16).reshape(RANK, half)
    other_q = (rho[...].astype(f32) / columns(nb[:, o])).astype(bf16).reshape(RANK, half)
    for p, q, factor in ((g, own_q, lh), (o, other_q, oth)):
        for k in range(CHUNKS):
            at = pl.ds(k * chunk, chunk)
            new_v[p, at] = w[p, at] - STEP * mm(factor[at], q)
            out(new_v.at[p, at], new_h.at[p, at])
    fac_o[...] = share[...] / columns(nb[r, g][None])[0]
    own_pre = base[g] - STEP * mm(tl[0], own_q)
    other_pre = base[o] - STEP * mm(tl[1], other_q)
    gate = jnp.where(g == 0, own_pre, other_pre)
    up = jnp.where(g == 0, other_pre, own_pre)
    hid_o[...] = (gate / (1.0 + jnp.exp(-gate)) * up).astype(bf16)
    for copy in copies:
        copy.wait()


def vmem(*shape, dtype=f32):
    return pltpu.VMEM(shape, dtype)


def pairs(n):
    return pltpu.SemaphoreType.DMA((2, n))


def call(kernel, ins, outs, scratch, args, collective_id=None, limit=24):
    where = {"v": pltpu.VMEM, "h": pltpu.HBM}
    params = {} if collective_id is None else dict(collective_id=collective_id, has_side_effects=True)
    return pl.pallas_call(
        kernel,
        out_shape=[jax.ShapeDtypeStruct(s, t) for s, t, _ in outs],
        in_specs=[pl.BlockSpec(memory_space=where[k]) for k in ins],
        out_specs=[pl.BlockSpec(memory_space=where[k]) for _, _, k in outs],
        scratch_shapes=scratch,
        compiler_params=pltpu.CompilerParams(vmem_limit_bytes=int(limit * 2**20), **params),
    )(*args)


def local(sizes, momentum, gradient, factor_q, weights, tokens):
    nr, nc, ng = sizes
    nx, nz = NX, nc // NX
    mom, grad, fq = momentum[0], gradient[0], factor_q[0].T
    rows, hid = mom.shape
    part, kr, nb = nx * nr, RANK // nr, BATCH // nr
    half = hid // ng

    def piece(n):
        return n, RANK // part + 1, RANK // 2

    left, gram, base, bufh = call(
        functools.partial(left_kernel, sizes),
        "hhhhh",
        [((rows, RANK), bf16, "v"), ((RANK + 8, RANK // 2), f32, "v"), ((2, nb, half), f32, "v"), ((rows, hid), bf16, "v")],
        [
            vmem(rows, hid), vmem(rows, hid, dtype=bf16), vmem(kr, hid), vmem(*weights.shape), vmem(*tokens.shape, dtype=bf16),
            pltpu.SemaphoreType.DMA((5,)), vmem(nr, kr, hid, dtype=bf16),
            vmem(nx, rows // nx, RANK), vmem(nx, rows // nx, RANK, dtype=bf16), vmem(nx - 1, rows // nx, RANK, dtype=bf16),
            vmem(nz, rows // nc, RANK), vmem(nz, rows // nc, RANK, dtype=bf16), vmem(nz, rows // nc, RANK, dtype=bf16),
            vmem(nx, nz, rows // nc, RANK, dtype=bf16),
            vmem(*piece(part)), vmem(*piece(part - 1)), vmem(*piece(part)),
            vmem(nr, 2, nb, half), vmem(nr - 1, 2, nb, half),
            pairs(nr - 1), pairs(nx - 1), pairs(nz), pairs(nz), pairs(nx - 1), pairs(part - 1), pairs(part - 1),
            pairs(nr - 1),
        ],
        (mom, grad, fq, weights, tokens), 0, limit=52.3,
    )
    square = ((RANK, RANK), f32, "v")
    start = call(
        start_kernel, "v", [square, square, ((8, RANK), f32, "v"), ((8, 128), f32, "v")],
        [vmem(RANK, RANK), vmem(RANK, 2 * RANK)], (gram,),
    )
    mom_new, lh, oth, rh, rho, norms, share, tl = call(
        functools.partial(right_kernel, sizes),
        "v" * 7 + "hh",
        [
            ((rows, hid), f32, "v"), ((rows, RANK), bf16, "v"), ((rows, RANK), bf16, "v"), ((RANK, hid), bf16, "v"), ((nr, kr, half), bf16, "v"),
            ((nr, ng, 1, 128), f32, "v"), ((kr, hid), f32, "v"), ((2, nb, RANK), bf16, "v"),
        ],
        [
            vmem(rows, hid), vmem(rows, hid, dtype=bf16), pltpu.SemaphoreType.DMA((2,)),
            vmem(nx, nz, rows // nc, RANK, dtype=bf16), vmem(nx, nz, rows // nc, RANK, dtype=bf16), vmem(nr, kr, hid), vmem(nr, kr, hid, dtype=bf16),
            vmem(nr - 1, kr, hid, dtype=bf16), vmem(nr, nb, RANK), vmem(nr, nb, RANK, dtype=bf16),
            vmem(nr - 1, nb, RANK, dtype=bf16), vmem(nb, RANK, dtype=bf16), vmem(nb, RANK, dtype=bf16),
            vmem(nr, kr, hid, dtype=bf16), vmem(kr, half, dtype=bf16), vmem(nr, kr, half, dtype=bf16),
            vmem(1, 128), vmem(ng, nz, 1, 128), vmem(nx, ng, 1, 128), vmem(nr, ng, 1, 128),
            pairs(1), pairs(nr - 1), pairs(nr - 1), pairs(nz), pairs(nx - 1), pairs(nr - 1), pairs(1), pairs(nr - 1),
            pairs(ng * nz - 1), pairs(nx - 1), pairs(nr - 1), pairs(1),
        ],
        (bufh, left, *start, tokens, mom, grad), 1,
    )
    mom_new, new, fac, hidden = call(
        last_kernel, "v" * 10,
        [((rows, hid), f32, "h"), (weights.shape, f32, "h"), ((kr, hid), f32, "v"), ((nb, half), bf16, "v")],
        [vmem(*weights.shape), pltpu.SemaphoreType.DMA((2 * CHUNKS + 1,))],
        (mom_new, weights, base, lh, oth, rh, rho, norms, share, tl),
    )
    return mom_new[None], fac.T[None], new, hidden


def solution(mesh):
    sizes = tuple(mesh.shape[a] for a in ("row", "col", "grp"))
    in_specs = (
        P("grp", "row", "col"),
        P("grp", "row", "col"),
        P("grp", "col", "row"),
        P(None, "row", ("col", "grp")),
        P(None, "row"),
    )
    out_specs = (
        P("grp", "row", "col"),
        P("grp", "col", "row"),
        P(None, "row", ("col", "grp")),
        P("row", ("col", "grp")),
    )
    return jax.shard_map(
        functools.partial(local, sizes), mesh=mesh, in_specs=in_specs, out_specs=out_specs, check_vma=False
    )
```

```python
import functools
import math

import jax
import jax.numpy as jnp
from jax import lax
from jax.experimental import pallas as pl
from jax.experimental.pallas import tpu as pltpu
from jax.sharding import PartitionSpec as P

D = 4096
HID = 16384
RANK = 256
BATCH = 256
FEEDBACK = 0.05
EPSILON = 1e-06
STEP = 0.4 * math.sqrt(max(D, HID))
CHUNKS = 4
NEAR = 0.16
NX = 4

f32, bf16 = jnp.float32, jnp.bfloat16
HI = lax.Precision.HIGHEST
MESH = pl.DeviceIdType.MESH
NN = (((1,), (0,)), ((), ()))
NT = (((1,), (1,)), ((), ()))
TN = (((0,), (0,)), ((), ()))


def mm(a, b, dims=NN, precision=None):
    return lax.dot_general(a, b, dims, precision=precision, preferred_element_type=f32)


def around(i, n):
    return [i if d == 0 else i + d - jnp.where(i + d >= n, n, 0) for d in range(n)]


def far_first(offsets, *rings):
    def way(offset):
        return sum(min(d, n - d) for d, n in zip(offset, rings))

    return sorted((offset for offset in offsets if any(offset)), key=lambda offset: -way(offset))


class Place:
    def __init__(self, sizes):
        self.nr, self.nc, self.ng = sizes
        self.nx, self.nz, self.ny = NX, self.nc // NX, self.nr // 2
        self.r, self.c, self.g = (lax.axis_index(a) for a in ("row", "col", "grp"))
        self.x, self.z = lax.rem(self.c, self.nx), lax.div(self.c, self.nx)
        self.core = lax.rem(self.r, 2)
        self.xs = around(self.x, self.nx)
        ys = around(lax.div(self.r, 2), self.ny)
        self.rs = {(dy, dc): 2 * ys[dy] + (1 - self.core if dc else self.core) for dy in range(self.ny) for dc in range(2)}
        self.row = far_first(self.rs, self.ny)
        self.line = [(d,) for d in range(1, self.nx)]
        self.line = [d for (d,) in far_first(self.line, self.nx)]
        self.plane = far_first([(dx, *d) for dx in range(self.nx) for d in self.rs], self.nx, self.ny)
        last = self.nz - 1
        self.stack = [
            jnp.where(
                self.z <= last // 2,
                last - k - jnp.where(last - k <= self.z, 1, 0),
                k + jnp.where(k >= self.z, 1, 0),
            )
            for k in range(last)
        ]
        around_both = around(self.g * self.nz + self.z, self.ng * self.nz)
        self.ring = [around_both[d] for (d,) in far_first([(d,) for d in range(len(around_both))], len(around_both))]

    def at(self, row=(0, 0), dx=0, z=None, g=None):
        z = self.z if z is None else z
        return (self.rs[row], z * self.nx + self.xs[dx], self.g if g is None else g)

    def up(self, k):
        g = jnp.where(self.ring[k] >= self.nz, 1, 0)
        return self.at(z=self.ring[k] - g * self.nz, g=g)


def greet(partners):
    barrier = pltpu.get_barrier_semaphore()
    for device in partners:
        pl.semaphore_signal(barrier, inc=1, device_id=device, device_id_type=MESH)
    return lambda: pl.semaphore_wait(barrier, len(partners))


def remote(src, dst, sent, received, device):
    return pltpu.make_async_remote_copy(
        src_ref=src, dst_ref=dst, send_sem=sent, recv_sem=received, device_id=device, device_id_type=MESH
    )


def send(src, dst, sems, k, device):
    copy = remote(src, dst, sems.at[0, k], sems.at[1, k], device)
    copy.start()
    return copy


def send_line(pick, slot, sems, at):
    waits = []
    for k, other in enumerate(at.stack):
        device = at.at(z=other)
        remote(pick(other), slot(at.z), sems.at[0, k], sems.at[1, at.z], device).start()
        waits.append(remote(pick(other), slot(other), sems.at[0, k], sems.at[1, other], device))
    return waits


def arrived(copies):
    for copy in copies:
        copy.wait_recv()


def left_kernel(sizes, mom_h, grad_h, fq_h, w_h, tok_h, left_o, gram_o, base_o, bufh,
                mom, grad, fq, w, tok, s_in, qbuf, part, partb, rx, sx, sxb, rz, l512, gp, rg, gf, pre, rpre,
                s_q, s_x, s_z, s_az, s_ax, s_g, s_ag, s_p):
    at = Place(sizes)
    nr, nx, nz = at.nr, at.nx, at.nz
    ready = greet([at.at(z=other) for other in at.stack] + [at.at(row=d[1:], dx=d[0]) for d in at.plane])
    r, x, z = at.r, at.x, at.z
    loads = [
        pltpu.make_async_copy(a, b, s_in.at[k])
        for k, (a, b) in enumerate(((fq_h, fq), (mom_h, mom), (grad_h, grad), (tok_h, tok), (w_h, w)))
    ]
    for load in loads:
        load.start()
    loads[0].wait()
    qbuf[r] = fq[...].astype(bf16)
    ready()
    got_q = [send(qbuf.at[r], qbuf.at[r], s_q, k, at.at(row=d)) for k, d in enumerate(at.row)]
    loads[1].wait()
    loads[2].wait()
    bufh[...] = (mom[...] + grad[...].astype(f32)).astype(bf16)
    arrived(got_q)
    part[...] = mm(bufh[...], qbuf[...].reshape(RANK, -1), NT).reshape(part.shape)
    partb[...] = part[...].astype(bf16)
    got_x = [send(partb.at[at.xs[d]], rx.at[k], s_x, k, at.at(dx=d)) for k, d in enumerate(at.line)]
    loads[3].wait()
    loads[4].wait()
    for p in range(2):
        high = w[p].astype(bf16)
        low = (w[p] - high.astype(f32)).astype(bf16)
        pre[:, p] = (mm(tok[...], high) + mm(tok[...], low)).reshape(pre[:, p].shape)
    arrived(got_x)
    sx[...] = (part[x] + jnp.sum(rx[...].astype(f32), axis=0)).reshape(sx.shape)
    sxb[...] = sx[...].astype(bf16)
    rz[z] = jnp.zeros(rz.shape[1:], bf16)
    got_z = send_line(lambda other: sxb.at[other], lambda place: rz.at[place], s_z, at)
    got_p = [send(pre.at[at.rs[d]], rpre.at[k], s_p, k, at.at(row=d)) for k, d in enumerate(at.row)]
    arrived(got_z)
    l512[x, z] = (sx[z] + jnp.sum(rz[...].astype(f32), axis=0)).astype(bf16)
    got_az = send_line(lambda other: l512.at[x, z], lambda place: l512.at[x, place], s_az, at)
    arrived(got_az)
    rows = l512[x].reshape(-1, RANK)
    gram = mm(rows, rows, TN)
    h = RANK // 2
    i, j = (lax.broadcasted_iota(jnp.int32, (h, h), d) for d in (0, 1))
    packed = jnp.where(i >= j, gram[:h, :h], gram[h:, h:])
    gp[: gp.shape[0] // 2, :-1] = packed.reshape(gp.shape[0] // 2, -1, h)
    gp[gp.shape[0] // 2 :, :-1] = gram[h:, :h].reshape(gp.shape[0] // 2, -1, h)
    gp[:, -1:] = jnp.broadcast_to(
        jnp.sum(jnp.where(i == j, gram[h:, h:], 0.0), axis=0, keepdims=True), (gp.shape[0], 1, h)
    )
    got_g = []
    for k, (dx, *d) in enumerate(at.plane):
        m = at.xs[dx] * nr + at.rs[*d]
        got_g.append(send(gp.at[m], rg.at[k], s_g, k, at.at(row=(*d,), dx=dx)))
    got_ax = [send(l512.at[x], l512.at[x], s_ax, k, at.at(dx=d)) for k, d in enumerate(at.line)]
    arrived(got_g)
    m = x * nr + r
    gf[m] = gp[m] + jnp.sum(rg[...], axis=0)
    got_ag = [send(gf.at[m], gf.at[m], s_ag, k, at.at(row=d[1:], dx=d[0])) for k, d in enumerate(at.plane)]
    arrived(got_p)
    base_o[...] = pre[r] + jnp.sum(rpre[...], axis=0)
    arrived(got_ax)
    left_o[...] = l512[...].reshape(left_o.shape)
    arrived(got_ag)
    gram_o[:RANK] = gf[:, :-1].reshape(RANK, -1)
    gram_o[RANK:] = jnp.broadcast_to(gf[0, -1:], (8, gf.shape[2]))
    for copies in (got_q, got_x, got_p, got_z, got_az, got_g, got_ax, got_ag):
        for copy in copies:
            copy.wait_send()


def tri_half(e):
    i, j = (lax.broadcasted_iota(jnp.int32, e.shape, d) for d in (0, 1))
    return jnp.where(i > j, e, jnp.where(i == j, 0.5 * e, 0.0))


def residual(w, a, precision=None):
    i, j = (lax.broadcasted_iota(jnp.int32, a.shape, d) for d in (0, 1))
    return mm(mm(w, a, NN, precision), w, NT, precision) - jnp.where(i == j, 1.0, 0.0)


def start_kernel(packed, a_o, w_o, across_o, near_o, gram, s):
    n, h = RANK, RANK // 2
    i, j = (lax.broadcasted_iota(jnp.int32, (h, h), d) for d in (0, 1))
    both, turned = packed[:h], packed[:h].T
    gram[:h, :h] = jnp.where(i >= j, both, turned)
    gram[h:, h:] = jnp.where(i > j, turned, jnp.where(i == j, packed[n : n + 1], both))
    gram[h:, :h] = packed[h:n]
    gram[:h, h:] = packed[h:n].T
    i, j = (lax.broadcasted_iota(jnp.int32, (n, n), d) for d in (0, 1))
    eye = jnp.where(i == j, 1.0, 0.0)
    diagonal = jnp.where(i == j, gram[...], 0.0)
    down = lax.rsqrt(jnp.sum(diagonal, axis=1, keepdims=True))
    across = lax.rsqrt(jnp.sum(diagonal, axis=0, keepdims=True))
    a = gram[...] * down * across
    a_o[...] = a
    across_o[...] = jnp.broadcast_to(across, across_o.shape)
    w = eye - tri_half(jnp.where(i == j, 0.0, a))
    w = w - mm(tri_half(residual(w, a)), w)
    w_o[...] = w
    e = residual(w, a)
    far = jnp.sum(e * e)
    near_o[...] = jnp.ones(near_o.shape, f32)

    @pl.when(~(far < NEAR))
    def _():
        s[:, :n] = gram[...]
        s[:, n:] = eye
        row = lax.broadcasted_iota(jnp.int32, (n, 1), 0)

        def eliminate(k, _):
            line = s[pl.ds(k, 1), :]
            column = jnp.sum(jnp.where(j == k, s[:, :n], 0.0), axis=1, keepdims=True)
            pivot = jnp.sum(jnp.where(row == k, column, 0.0), axis=0, keepdims=True)
            s[...] = s[...] - jnp.where(row > k, column / pivot, 0.0) * line
            return 0

        lax.fori_loop(0, n, eliminate, 0)
        pivots = jnp.sum(jnp.where(i == j, s[:, :n], 0.0), axis=1, keepdims=True)
        w_o[...] = s[:, n:] / jnp.sqrt(pivots)
        across_o[...] = jnp.ones(across_o.shape, f32)
        near_o[...] = jnp.zeros(near_o.shape, f32)


def right_kernel(sizes, bufh, left, a, w, across, near, tok, mom_h, grad_h, mom_o, lh_o, oth_o, rh_o, rho_o, nb_o, share_o, tl_o,
                 mom, grad, s_in, lh, oth, rt, rtb, rrt, tl, tlb, rtl, tls, tlo, rh, sho, rho, sq, sqz, sqx,
                 s_l, s_rt, s_tl, s_lz, s_lx, s_rh, s_sh, s_ro, s_sq, s_nb, s_to):
    at = Place(sizes)
    nr, nx, nz, ng = at.nr, at.nx, at.nz, at.ng
    r, c, g, x, z = at.r, at.c, at.g, at.x, at.z
    upwards = range(len(at.ring))
    ready = greet(
        [at.up(k) for k in upwards] + [at.at(row=d[1:], dx=d[0]) for d in at.plane]
    )
    o = 1 - g
    kr = RANK // nr
    half = sho.shape[1]

    loads = [pltpu.make_async_copy(mom_h, mom, s_in.at[0]), pltpu.make_async_copy(grad_h, grad, s_in.at[1])]
    for load in loads:
        load.start()
    inverse = w[...]
    for _ in range(3):
        error = jnp.where(near[:1, :1] > 0, tri_half(residual(inverse, a[...], HI)), 0.0)
        inverse = inverse - mm(error, inverse, NN, HI)
    inverse = inverse * across[:1]
    high = inverse.astype(bf16)
    low = (inverse - high.astype(f32)).astype(bf16)
    left_h = (mm(left[...], high, NT) + mm(left[...], low, NT)).astype(bf16)
    lh[...] = left_h.reshape(lh.shape)
    ready()
    got_l = [send(lh.at[x, z], oth.at[x, z], s_l, 0, at.at(g=o))]
    rt[...] = mm(left_h, bufh[...], TN).reshape(rt.shape)
    rtb[...] = rt[...].astype(bf16)
    got_rt = [send(rtb.at[at.rs[d]], rrt.at[k], s_rt, k, at.at(row=d)) for k, d in enumerate(at.row)]
    tl[...] = mm(tok[...], left_h).reshape(tl.shape)
    tlb[...] = tl[...].astype(bf16)
    got_tl = [send(tlb.at[at.rs[d]], rtl.at[k], s_tl, k, at.at(row=d)) for k, d in enumerate(at.row)]
    arrived(got_rt)
    share = rt[r] + jnp.sum(rrt[...].astype(f32), axis=0)
    share_o[...] = share
    rh[r] = share.astype(bf16)
    sho[...] = share_o[:, pl.ds(pl.multiple_of(o * half, half), half)].astype(bf16)
    got_sh = [send(sho, rho.at[r], s_sh, 0, at.at(g=o))]
    eye = lax.broadcasted_iota(jnp.int32, (kr, 128), 0) == lax.broadcasted_iota(jnp.int32, (kr, 128), 1)
    squares = jnp.sum(share * share, axis=1, keepdims=True)
    line = jnp.sum(jnp.where(eye, squares, 0.0), axis=0, keepdims=True)
    sqz[g, z] = line
    sq[...] = line
    got_sq = [send(sq, sqz.at[g, z], s_sq, k, at.up(k)) for k in upwards]
    arrived(got_l)
    got_lz = send_line(lambda other: oth.at[x, z], lambda place: oth.at[x, place], s_lz, at)
    got_rh = [send(rh.at[r], rh.at[r], s_rh, k, at.at(row=d)) for k, d in enumerate(at.row)]
    arrived(got_tl)
    tls[...] = (tl[r] + jnp.sum(rtl[...].astype(f32), axis=0)).astype(bf16)
    got_to = [send(tls, tlo, s_to, 0, at.at(g=o))]
    arrived(got_sh)
    got_ro = [send(rho.at[r], rho.at[r], s_ro, k, at.at(row=d)) for k, d in enumerate(at.row)]
    arrived(got_lz)
    got_lx = [send(oth.at[x], oth.at[x], s_lx, k, at.at(dx=d)) for k, d in enumerate(at.line)]
    arrived(got_sq)
    sqx[x, r] = jnp.sum(sqz[...], axis=1)
    got_nb = [send(sqx.at[x, r], sqx.at[x, r], s_nb, k, at.at(row=d[1:], dx=d[0])) for k, d in enumerate(at.plane)]
    lh_o[...] = lh[...].reshape(lh_o.shape)
    for load in loads:
        load.wait()
    arrived(got_rh)
    mom_o[...] = mom[...] + grad[...].astype(f32) - FEEDBACK * mm(left_h, rh[...].reshape(RANK, -1))
    rh_o[...] = rh[...].reshape(rh_o.shape)
    arrived(got_lx)
    oth_o[...] = oth[...].reshape(oth_o.shape)
    arrived(got_nb)
    nb_o[...] = jnp.sum(sqx[...], axis=0)
    arrived(got_ro)
    rho_o[...] = rho[...]
    arrived(got_to)
    tl_o[0] = tls[...]
    tl_o[1] = tlo[...]
    for copies in (got_l, got_rt, got_tl, got_lz, got_sh, got_sq, got_rh, got_lx, got_nb, got_ro, got_to):
        for copy in copies:
            copy.wait_send()


def last_kernel(mom, w, base, lh, oth, rh, rho, nb, share, tl, mom_h, new_h, fac_o, hid_o, new_v, sems):
    r, g = lax.axis_index("row"), lax.axis_index("grp")
    o = 1 - g
    nr, kr, half = rho.shape
    rows = lh.shape[0]
    chunk = rows // CHUNKS
    copies = []

    def out(src, dst):
        copies.append(pltpu.make_async_copy(src, dst, sems.at[len(copies)]))
        copies[-1].start()

    out(mom, mom_h)
    eye = lax.broadcasted_iota(jnp.int32, (kr, 128), 0) == lax.broadcasted_iota(jnp.int32, (kr, 128), 1)

    def columns(norms):
        norms = jnp.broadcast_to(jnp.sqrt(norms + EPSILON), (norms.shape[0], kr, 128))
        return jnp.sum(jnp.where(eye[None], norms, 0.0), axis=2, keepdims=True)

    own = rh[:, pl.ds(pl.multiple_of(g * half, half), half)].astype(f32).reshape(rho.shape)
    own_q = (own / columns(nb[:, g])).astype(bf16).reshape(RANK, half)
    other_q = (rho[...].astype(f32) / columns(nb[:, o])).astype(bf16).reshape(RANK, half)
    for p, q, factor in ((g, own_q, lh), (o, other_q, oth)):
        for k in range(CHUNKS):
            at = pl.ds(k * chunk, chunk)
            new_v[p, at] = w[p, at] - STEP * mm(factor[at], q)
            out(new_v.at[p, at], new_h.at[p, at])
    fac_o[...] = share[...] / columns(nb[r, g][None])[0]
    own_pre = base[g] - STEP * mm(tl[0], own_q)
    other_pre = base[o] - STEP * mm(tl[1], other_q)
    gate = jnp.where(g == 0, own_pre, other_pre)
    up = jnp.where(g == 0, other_pre, own_pre)
    hid_o[...] = (gate / (1.0 + jnp.exp(-gate)) * up).astype(bf16)
    for copy in copies:
        copy.wait()


def vmem(*shape, dtype=f32):
    return pltpu.VMEM(shape, dtype)


def pairs(n):
    return pltpu.SemaphoreType.DMA((2, n))


def call(kernel, ins, outs, scratch, args, collective_id=None, limit=24):
    where = {"v": pltpu.VMEM, "h": pltpu.HBM}
    params = {} if collective_id is None else dict(collective_id=collective_id, has_side_effects=True)
    return pl.pallas_call(
        kernel,
        out_shape=[jax.ShapeDtypeStruct(s, t) for s, t, _ in outs],
        in_specs=[pl.BlockSpec(memory_space=where[k]) for k in ins],
        out_specs=[pl.BlockSpec(memory_space=where[k]) for _, _, k in outs],
        scratch_shapes=scratch,
        compiler_params=pltpu.CompilerParams(vmem_limit_bytes=int(limit * 2**20), **params),
    )(*args)


def local(sizes, momentum, gradient, factor_q, weights, tokens):
    nr, nc, ng = sizes
    nx, nz = NX, nc // NX
    mom, grad, fq = momentum[0], gradient[0], factor_q[0].T
    rows, hid = mom.shape
    part, kr, nb = nx * nr, RANK // nr, BATCH // nr
    half = hid // ng

    def piece(n):
        return n, RANK // part + 1, RANK // 2

    left, gram, base, bufh = call(
        functools.partial(left_kernel, sizes),
        "hhhhh",
        [((rows, RANK), bf16, "v"), ((RANK + 8, RANK // 2), f32, "v"), ((2, nb, half), f32, "v"), ((rows, hid), bf16, "v")],
        [
            vmem(rows, hid), vmem(rows, hid, dtype=bf16), vmem(kr, hid), vmem(*weights.shape), vmem(*tokens.shape, dtype=bf16),
            pltpu.SemaphoreType.DMA((5,)), vmem(nr, kr, hid, dtype=bf16),
            vmem(nx, rows // nx, RANK), vmem(nx, rows // nx, RANK, dtype=bf16), vmem(nx - 1, rows // nx, RANK, dtype=bf16),
            vmem(nz, rows // nc, RANK), vmem(nz, rows // nc, RANK, dtype=bf16), vmem(nz, rows // nc, RANK, dtype=bf16),
            vmem(nx, nz, rows // nc, RANK, dtype=bf16),
            vmem(*piece(part)), vmem(*piece(part - 1)), vmem(*piece(part)),
            vmem(nr, 2, nb, half), vmem(nr - 1, 2, nb, half),
            pairs(nr - 1), pairs(nx - 1), pairs(nz), pairs(nz), pairs(nx - 1), pairs(part - 1), pairs(part - 1),
            pairs(nr - 1),
        ],
        [pltpu.with_memory_space_constraint(a, pltpu.HBM) for a in (mom, grad, fq, weights, tokens)], 0,
    )
    square = ((RANK, RANK), f32, "v")
    start = call(
        start_kernel, "v", [square, square, ((8, RANK), f32, "v"), ((8, 128), f32, "v")],
        [vmem(RANK, RANK), vmem(RANK, 2 * RANK)], (gram,),
    )
    mom_new, lh, oth, rh, rho, norms, share, tl = call(
        functools.partial(right_kernel, sizes),
        "v" * 7 + "hh",
        [
            ((rows, hid), f32, "v"), ((rows, RANK), bf16, "v"), ((rows, RANK), bf16, "v"), ((RANK, hid), bf16, "v"), ((nr, kr, half), bf16, "v"),
            ((nr, ng, 1, 128), f32, "v"), ((kr, hid), f32, "v"), ((2, nb, RANK), bf16, "v"),
        ],
        [
            vmem(rows, hid), vmem(rows, hid, dtype=bf16), pltpu.SemaphoreType.DMA((2,)),
            vmem(nx, nz, rows // nc, RANK, dtype=bf16), vmem(nx, nz, rows // nc, RANK, dtype=bf16), vmem(nr, kr, hid), vmem(nr, kr, hid, dtype=bf16),
            vmem(nr - 1, kr, hid, dtype=bf16), vmem(nr, nb, RANK), vmem(nr, nb, RANK, dtype=bf16),
            vmem(nr - 1, nb, RANK, dtype=bf16), vmem(nb, RANK, dtype=bf16), vmem(nb, RANK, dtype=bf16),
            vmem(nr, kr, hid, dtype=bf16), vmem(kr, half, dtype=bf16), vmem(nr, kr, half, dtype=bf16),
            vmem(1, 128), vmem(ng, nz, 1, 128), vmem(nx, nr, ng, 1, 128),
            pairs(1), pairs(nr - 1), pairs(nr - 1), pairs(nz), pairs(nx - 1), pairs(nr - 1), pairs(1), pairs(nr - 1),
            pairs(ng * nz - 1), pairs(part - 1), pairs(1),
        ],
        (bufh, left, *start, tokens, mom, grad), 1,
    )
    mom_new, new, fac, hidden = call(
        last_kernel, "v" * 10,
        [((rows, hid), f32, "h"), (weights.shape, f32, "h"), ((kr, hid), f32, "v"), ((nb, half), bf16, "v")],
        [vmem(*weights.shape), pltpu.SemaphoreType.DMA((2 * CHUNKS + 1,))],
        (mom_new, weights, base, lh, oth, rh, rho, norms, share, tl),
    )
    return mom_new[None], fac.T[None], new, hidden


def solution(mesh):
    sizes = tuple(mesh.shape[a] for a in ("row", "col", "grp"))
    in_specs = (
        P("grp", "row", "col"),
        P("grp", "row", "col"),
        P("grp", "col", "row"),
        P(None, "row", ("col", "grp")),
        P(None, "row"),
    )
    out_specs = (
        P("grp", "row", "col"),
        P("grp", "col", "row"),
        P(None, "row", ("col", "grp")),
        P("row", ("col", "grp")),
    )
    return jax.shard_map(
        functools.partial(local, sizes), mesh=mesh, in_specs=in_specs, out_specs=out_specs, check_vma=False
    )
```

```python
import functools
import math

import jax
import jax.numpy as jnp
from jax import lax
from jax.experimental import pallas as pl
from jax.experimental.pallas import tpu as pltpu
from jax.sharding import PartitionSpec as P

D = 4096
HID = 16384
RANK = 256
BATCH = 256
FEEDBACK = 0.05
EPSILON = 1e-06
STEP = 0.4 * math.sqrt(max(D, HID))
CHUNKS = 4
NEAR = 0.1
NX = 4

f32, bf16 = jnp.float32, jnp.bfloat16
HI = lax.Precision.HIGHEST
MESH = pl.DeviceIdType.MESH
NN = (((1,), (0,)), ((), ()))
NT = (((1,), (1,)), ((), ()))
TN = (((0,), (0,)), ((), ()))


def mm(a, b, dims=NN, precision=None):
    return lax.dot_general(a, b, dims, precision=precision, preferred_element_type=f32)


def around(i, n):
    return [i if d == 0 else i + d - jnp.where(i + d >= n, n, 0) for d in range(n)]


def far_first(offsets, *rings):
    def way(offset):
        return sum(min(d, n - d) for d, n in zip(offset, rings))

    return sorted((offset for offset in offsets if any(offset)), key=lambda offset: -way(offset))


class Place:
    def __init__(self, sizes):
        self.nr, self.nc, self.ng = sizes
        self.nx, self.nz, self.ny = NX, self.nc // NX, self.nr // 2
        self.r, self.c, self.g = (lax.axis_index(a) for a in ("row", "col", "grp"))
        self.x, self.z = lax.rem(self.c, self.nx), lax.div(self.c, self.nx)
        self.core = lax.rem(self.r, 2)
        self.xs = around(self.x, self.nx)
        ys = around(lax.div(self.r, 2), self.ny)
        self.rs = {(dy, dc): 2 * ys[dy] + (1 - self.core if dc else self.core) for dy in range(self.ny) for dc in range(2)}
        self.row = far_first(self.rs, self.ny)
        self.line = [(d,) for d in range(1, self.nx)]
        self.line = [d for (d,) in far_first(self.line, self.nx)]
        self.plane = far_first([(dx, *d) for dx in range(self.nx) for d in self.rs], self.nx, self.ny)
        last = self.nz - 1
        self.stack = [
            jnp.where(
                self.z <= last // 2,
                last - k - jnp.where(last - k <= self.z, 1, 0),
                k + jnp.where(k >= self.z, 1, 0),
            )
            for k in range(last)
        ]
        around_both = around(self.g * self.nz + self.z, self.ng * self.nz)
        self.ring = [around_both[d] for (d,) in far_first([(d,) for d in range(len(around_both))], len(around_both))]

    def at(self, row=(0, 0), dx=0, z=None, g=None):
        z = self.z if z is None else z
        return (self.rs[row], z * self.nx + self.xs[dx], self.g if g is None else g)

    def up(self, k):
        g = jnp.where(self.ring[k] >= self.nz, 1, 0)
        return self.at(z=self.ring[k] - g * self.nz, g=g)


def greet(partners):
    barrier = pltpu.get_barrier_semaphore()
    for device in partners:
        pl.semaphore_signal(barrier, inc=1, device_id=device, device_id_type=MESH)
    return lambda: pl.semaphore_wait(barrier, len(partners))


def remote(src, dst, sent, received, device):
    return pltpu.make_async_remote_copy(
        src_ref=src, dst_ref=dst, send_sem=sent, recv_sem=received, device_id=device, device_id_type=MESH
    )


def send(src, dst, sems, k, device):
    copy = remote(src, dst, sems.at[0, k], sems.at[1, k], device)
    copy.start()
    return copy


def send_line(pick, slot, sems, at):
    waits = []
    for k, other in enumerate(at.stack):
        device = at.at(z=other)
        remote(pick(other), slot(at.z), sems.at[0, k], sems.at[1, at.z], device).start()
        waits.append(remote(pick(other), slot(other), sems.at[0, k], sems.at[1, other], device))
    return waits


def arrived(copies):
    for copy in copies:
        copy.wait_recv()


def left_kernel(sizes, mom_h, grad_h, fq_h, w_h, tok_h, left_o, gram_o, base_o, bufh,
                mom, grad, fq, w, tok, s_in, qbuf, part, partb, rx, sx, sxb, rz, l512, gp, rg, gf, pre, rpre,
                s_q, s_x, s_z, s_az, s_ax, s_g, s_ag, s_p):
    at = Place(sizes)
    nr, nx, nz = at.nr, at.nx, at.nz
    ready = greet([at.at(z=other) for other in at.stack] + [at.at(row=d[1:], dx=d[0]) for d in at.plane])
    r, x, z = at.r, at.x, at.z
    loads = [
        pltpu.make_async_copy(a, b, s_in.at[k])
        for k, (a, b) in enumerate(((fq_h, fq), (mom_h, mom), (grad_h, grad), (tok_h, tok), (w_h, w)))
    ]
    for load in loads:
        load.start()
    loads[0].wait()
    qbuf[r] = fq[...].astype(bf16)
    ready()
    got_q = [send(qbuf.at[r], qbuf.at[r], s_q, k, at.at(row=d)) for k, d in enumerate(at.row)]
    loads[1].wait()
    loads[2].wait()
    bufh[...] = (mom[...] + grad[...].astype(f32)).astype(bf16)
    arrived(got_q)
    part[...] = mm(bufh[...], qbuf[...].reshape(RANK, -1), NT).reshape(part.shape)
    partb[...] = part[...].astype(bf16)
    got_x = [send(partb.at[at.xs[d]], rx.at[k], s_x, k, at.at(dx=d)) for k, d in enumerate(at.line)]
    loads[3].wait()
    loads[4].wait()
    for p in range(2):
        high = w[p].astype(bf16)
        low = (w[p] - high.astype(f32)).astype(bf16)
        pre[:, p] = (mm(tok[...], high) + mm(tok[...], low)).reshape(pre[:, p].shape)
    arrived(got_x)
    sx[...] = (part[x] + jnp.sum(rx[...].astype(f32), axis=0)).reshape(sx.shape)
    sxb[...] = sx[...].astype(bf16)
    rz[z] = jnp.zeros(rz.shape[1:], bf16)
    got_z = send_line(lambda other: sxb.at[other], lambda place: rz.at[place], s_z, at)
    got_p = [send(pre.at[at.rs[d]], rpre.at[k], s_p, k, at.at(row=d)) for k, d in enumerate(at.row)]
    arrived(got_z)
    l512[x, z] = (sx[z] + jnp.sum(rz[...].astype(f32), axis=0)).astype(bf16)
    got_az = send_line(lambda other: l512.at[x, z], lambda place: l512.at[x, place], s_az, at)
    arrived(got_az)
    rows = l512[x].reshape(-1, RANK)
    gram = mm(rows, rows, TN)
    h = RANK // 2
    i, j = (lax.broadcasted_iota(jnp.int32, (h, h), d) for d in (0, 1))
    packed = jnp.where(i >= j, gram[:h, :h], gram[h:, h:])
    gp[: gp.shape[0] // 2, :-1] = packed.reshape(gp.shape[0] // 2, -1, h)
    gp[gp.shape[0] // 2 :, :-1] = gram[h:, :h].reshape(gp.shape[0] // 2, -1, h)
    gp[:, -1:] = jnp.broadcast_to(
        jnp.sum(jnp.where(i == j, gram[h:, h:], 0.0), axis=0, keepdims=True), (gp.shape[0], 1, h)
    )
    got_g = []
    for k, (dx, *d) in enumerate(at.plane):
        m = at.xs[dx] * nr + at.rs[*d]
        got_g.append(send(gp.at[m], rg.at[k], s_g, k, at.at(row=(*d,), dx=dx)))
    got_ax = [send(l512.at[x], l512.at[x], s_ax, k, at.at(dx=d)) for k, d in enumerate(at.line)]
    arrived(got_g)
    m = x * nr + r
    gf[m] = gp[m] + jnp.sum(rg[...], axis=0)
    got_ag = [send(gf.at[m], gf.at[m], s_ag, k, at.at(row=d[1:], dx=d[0])) for k, d in enumerate(at.plane)]
    arrived(got_p)
    base_o[...] = pre[r] + jnp.sum(rpre[...], axis=0)
    arrived(got_ax)
    left_o[...] = l512[...].reshape(left_o.shape)
    arrived(got_ag)
    gram_o[:RANK] = gf[:, :-1].reshape(RANK, -1)
    gram_o[RANK:] = jnp.broadcast_to(gf[0, -1:], (8, gf.shape[2]))
    for copies in (got_q, got_x, got_p, got_z, got_az, got_g, got_ax, got_ag):
        for copy in copies:
            copy.wait_send()


def tri_half(e):
    i, j = (lax.broadcasted_iota(jnp.int32, e.shape, d) for d in (0, 1))
    return jnp.where(i > j, e, jnp.where(i == j, 0.5 * e, 0.0))


def residual(w, a, precision=None):
    i, j = (lax.broadcasted_iota(jnp.int32, a.shape, d) for d in (0, 1))
    return mm(mm(w, a, NN, precision), w, NT, precision) - jnp.where(i == j, 1.0, 0.0)


def start_kernel(packed, a_o, w_o, across_o, near_o, gram, s):
    n, h = RANK, RANK // 2
    i, j = (lax.broadcasted_iota(jnp.int32, (h, h), d) for d in (0, 1))
    both, turned = packed[:h], packed[:h].T
    gram[:h, :h] = jnp.where(i >= j, both, turned)
    gram[h:, h:] = jnp.where(i > j, turned, jnp.where(i == j, packed[n : n + 1], both))
    gram[h:, :h] = packed[h:n]
    gram[:h, h:] = packed[h:n].T
    i, j = (lax.broadcasted_iota(jnp.int32, (n, n), d) for d in (0, 1))
    eye = jnp.where(i == j, 1.0, 0.0)
    diagonal = jnp.where(i == j, gram[...], 0.0)
    down = lax.rsqrt(jnp.sum(diagonal, axis=1, keepdims=True))
    across = lax.rsqrt(jnp.sum(diagonal, axis=0, keepdims=True))
    a = gram[...] * down * across
    a_o[...] = a
    across_o[...] = jnp.broadcast_to(across, across_o.shape)
    w = eye - tri_half(jnp.where(i == j, 0.0, a))
    w = w - mm(tri_half(residual(w, a)), w)
    e = residual(w, a)
    w_o[...] = w - mm(tri_half(e), w)
    far = jnp.sum(e * e)
    near_o[...] = jnp.ones(near_o.shape, f32)

    @pl.when(~(far < NEAR))
    def _():
        s[:, :n] = gram[...]
        s[:, n:] = eye
        row = lax.broadcasted_iota(jnp.int32, (n, 1), 0)

        def eliminate(k, _):
            line = s[pl.ds(k, 1), :]
            column = jnp.sum(jnp.where(j == k, s[:, :n], 0.0), axis=1, keepdims=True)
            pivot = jnp.sum(jnp.where(row == k, column, 0.0), axis=0, keepdims=True)
            s[...] = s[...] - jnp.where(row > k, column / pivot, 0.0) * line
            return 0

        lax.fori_loop(0, n, eliminate, 0)
        pivots = jnp.sum(jnp.where(i == j, s[:, :n], 0.0), axis=1, keepdims=True)
        w_o[...] = s[:, n:] / jnp.sqrt(pivots)
        across_o[...] = jnp.ones(across_o.shape, f32)
        near_o[...] = jnp.zeros(near_o.shape, f32)


def right_kernel(sizes, bufh, left, a, w, across, near, tok, mom_h, grad_h, mom_o, lh_o, oth_o, rh_o, rho_o, nb_o, share_o, tl_o,
                 mom, grad, s_in, lh, oth, rt, rtb, rrt, tl, tlb, rtl, tls, tlo, rh, sho, rho, sq, sqz, sqx, nb,
                 s_l, s_rt, s_tl, s_lz, s_lx, s_rh, s_sh, s_ro, s_sq, s_sx, s_nb, s_to):
    at = Place(sizes)
    nr, nx, nz, ng = at.nr, at.nx, at.nz, at.ng
    r, c, g, x, z = at.r, at.c, at.g, at.x, at.z
    upwards = range(len(at.ring))
    ready = greet(
        [at.up(k) for k in upwards] + [at.at(row=d) for d in at.row] + [at.at(dx=d) for d in at.line]
    )
    o = 1 - g
    kr = RANK // nr
    half = sho.shape[1]

    loads = [pltpu.make_async_copy(mom_h, mom, s_in.at[0]), pltpu.make_async_copy(grad_h, grad, s_in.at[1])]
    for load in loads:
        load.start()
    inverse = w[...]
    for _ in range(2):
        error = jnp.where(near[:1, :1] > 0, tri_half(residual(inverse, a[...], HI)), 0.0)
        inverse = inverse - mm(error, inverse)
    inverse = inverse * across[:1]
    high = inverse.astype(bf16)
    low = (inverse - high.astype(f32)).astype(bf16)
    left_h = (mm(left[...], high, NT) + mm(left[...], low, NT)).astype(bf16)
    lh[...] = left_h.reshape(lh.shape)
    ready()
    got_l = [send(lh.at[x, z], oth.at[x, z], s_l, 0, at.at(g=o))]
    rt[...] = mm(left_h, bufh[...], TN).reshape(rt.shape)
    rtb[...] = rt[...].astype(bf16)
    got_rt = [send(rtb.at[at.rs[d]], rrt.at[k], s_rt, k, at.at(row=d)) for k, d in enumerate(at.row)]
    tl[...] = mm(tok[...], left_h).reshape(tl.shape)
    tlb[...] = tl[...].astype(bf16)
    got_tl = [send(tlb.at[at.rs[d]], rtl.at[k], s_tl, k, at.at(row=d)) for k, d in enumerate(at.row)]
    arrived(got_rt)
    share = rt[r] + jnp.sum(rrt[...].astype(f32), axis=0)
    share_o[...] = share
    rh[r] = share.astype(bf16)
    sho[...] = share_o[:, pl.ds(pl.multiple_of(o * half, half), half)].astype(bf16)
    got_sh = [send(sho, rho.at[r], s_sh, 0, at.at(g=o))]
    eye = lax.broadcasted_iota(jnp.int32, (kr, 128), 0) == lax.broadcasted_iota(jnp.int32, (kr, 128), 1)
    squares = jnp.sum(share * share, axis=1, keepdims=True)
    line = jnp.sum(jnp.where(eye, squares, 0.0), axis=0, keepdims=True)
    sqz[g, z] = line
    sq[...] = line
    got_sq = [send(sq, sqz.at[g, z], s_sq, k, at.up(k)) for k in upwards]
    arrived(got_l)
    got_lz = send_line(lambda other: oth.at[x, z], lambda place: oth.at[x, place], s_lz, at)
    got_rh = [send(rh.at[r], rh.at[r], s_rh, k, at.at(row=d)) for k, d in enumerate(at.row)]
    arrived(got_tl)
    tls[...] = (tl[r] + jnp.sum(rtl[...].astype(f32), axis=0)).astype(bf16)
    got_to = [send(tls, tlo, s_to, 0, at.at(g=o))]
    arrived(got_sh)
    got_ro = [send(rho.at[r], rho.at[r], s_ro, k, at.at(row=d)) for k, d in enumerate(at.row)]
    arrived(got_sq)
    sqx[x] = jnp.sum(sqz[...], axis=1)
    got_sx = [send(sqx.at[x], sqx.at[x], s_sx, k, at.at(dx=d)) for k, d in enumerate(at.line)]
    arrived(got_lz)
    got_lx = [send(oth.at[x], oth.at[x], s_lx, k, at.at(dx=d)) for k, d in enumerate(at.line)]
    arrived(got_sx)
    nb[r] = jnp.sum(sqx[...], axis=0)
    got_nb = [send(nb.at[r], nb.at[r], s_nb, k, at.at(row=d)) for k, d in enumerate(at.row)]
    lh_o[...] = lh[...].reshape(lh_o.shape)
    for load in loads:
        load.wait()
    arrived(got_rh)
    mom_o[...] = mom[...] + grad[...].astype(f32) - FEEDBACK * mm(left_h, rh[...].reshape(RANK, -1))
    rh_o[...] = rh[...].reshape(rh_o.shape)
    arrived(got_lx)
    oth_o[...] = oth[...].reshape(oth_o.shape)
    arrived(got_nb)
    nb_o[...] = nb[...]
    arrived(got_ro)
    rho_o[...] = rho[...]
    arrived(got_to)
    tl_o[0] = tls[...]
    tl_o[1] = tlo[...]
    for copies in (got_l, got_rt, got_tl, got_lz, got_sh, got_sq, got_sx, got_rh, got_lx, got_nb, got_ro, got_to):
        for copy in copies:
            copy.wait_send()


def last_kernel(mom, w, base, lh, oth, rh, rho, nb, share, tl, mom_h, new_h, fac_o, hid_o, new_v, sems):
    r, g = lax.axis_index("row"), lax.axis_index("grp")
    o = 1 - g
    nr, kr, half = rho.shape
    rows = lh.shape[0]
    chunk = rows // CHUNKS
    copies = []

    def out(src, dst):
        copies.append(pltpu.make_async_copy(src, dst, sems.at[len(copies)]))
        copies[-1].start()

    out(mom, mom_h)
    eye = lax.broadcasted_iota(jnp.int32, (kr, 128), 0) == lax.broadcasted_iota(jnp.int32, (kr, 128), 1)

    def columns(norms):
        norms = jnp.broadcast_to(jnp.sqrt(norms + EPSILON), (norms.shape[0], kr, 128))
        return jnp.sum(jnp.where(eye[None], norms, 0.0), axis=2, keepdims=True)

    own = rh[:, pl.ds(pl.multiple_of(g * half, half), half)].astype(f32).reshape(rho.shape)
    own_q = (own / columns(nb[:, g])).astype(bf16).reshape(RANK, half)
    other_q = (rho[...].astype(f32) / columns(nb[:, o])).astype(bf16).reshape(RANK, half)
    for p, q, factor in ((g, own_q, lh), (o, other_q, oth)):
        for k in range(CHUNKS):
            at = pl.ds(k * chunk, chunk)
            new_v[p, at] = w[p, at] - STEP * mm(factor[at], q)
            out(new_v.at[p, at], new_h.at[p, at])
    fac_o[...] = share[...] / columns(nb[r, g][None])[0]
    own_pre = base[g] - STEP * mm(tl[0], own_q)
    other_pre = base[o] - STEP * mm(tl[1], other_q)
    gate = jnp.where(g == 0, own_pre, other_pre)
    up = jnp.where(g == 0, other_pre, own_pre)
    hid_o[...] = (gate / (1.0 + jnp.exp(-gate)) * up).astype(bf16)
    for copy in copies:
        copy.wait()


def vmem(*shape, dtype=f32):
    return pltpu.VMEM(shape, dtype)


def pairs(n):
    return pltpu.SemaphoreType.DMA((2, n))


def call(kernel, ins, outs, scratch, args, collective_id=None, limit=24):
    where = {"v": pltpu.VMEM, "h": pltpu.HBM}
    params = {} if collective_id is None else dict(collective_id=collective_id, has_side_effects=True)
    return pl.pallas_call(
        kernel,
        out_shape=[jax.ShapeDtypeStruct(s, t) for s, t, _ in outs],
        in_specs=[pl.BlockSpec(memory_space=where[k]) for k in ins],
        out_specs=[pl.BlockSpec(memory_space=where[k]) for _, _, k in outs],
        scratch_shapes=scratch,
        compiler_params=pltpu.CompilerParams(vmem_limit_bytes=int(limit * 2**20), **params),
    )(*args)


def local(sizes, momentum, gradient, factor_q, weights, tokens):
    nr, nc, ng = sizes
    nx, nz = NX, nc // NX
    mom, grad, fq = momentum[0], gradient[0], factor_q[0].T
    rows, hid = mom.shape
    part, kr, nb = nx * nr, RANK // nr, BATCH // nr
    half = hid // ng

    def piece(n):
        return n, RANK // part + 1, RANK // 2

    left, gram, base, bufh = call(
        functools.partial(left_kernel, sizes),
        "hhhhh",
        [((rows, RANK), bf16, "v"), ((RANK + 8, RANK // 2), f32, "v"), ((2, nb, half), f32, "v"), ((rows, hid), bf16, "v")],
        [
            vmem(rows, hid), vmem(rows, hid, dtype=bf16), vmem(kr, hid), vmem(*weights.shape), vmem(*tokens.shape, dtype=bf16),
            pltpu.SemaphoreType.DMA((5,)), vmem(nr, kr, hid, dtype=bf16),
            vmem(nx, rows // nx, RANK), vmem(nx, rows // nx, RANK, dtype=bf16), vmem(nx - 1, rows // nx, RANK, dtype=bf16),
            vmem(nz, rows // nc, RANK), vmem(nz, rows // nc, RANK, dtype=bf16), vmem(nz, rows // nc, RANK, dtype=bf16),
            vmem(nx, nz, rows // nc, RANK, dtype=bf16),
            vmem(*piece(part)), vmem(*piece(part - 1)), vmem(*piece(part)),
            vmem(nr, 2, nb, half), vmem(nr - 1, 2, nb, half),
            pairs(nr - 1), pairs(nx - 1), pairs(nz), pairs(nz), pairs(nx - 1), pairs(part - 1), pairs(part - 1),
            pairs(nr - 1),
        ],
        [pltpu.with_memory_space_constraint(a, pltpu.HBM) for a in (mom, grad, fq, weights, tokens)], 0,
    )
    square = ((RANK, RANK), f32, "v")
    start = call(
        start_kernel, "v", [square, square, ((8, RANK), f32, "v"), ((8, 128), f32, "v")],
        [vmem(RANK, RANK), vmem(RANK, 2 * RANK)], (gram,),
    )
    mom_new, lh, oth, rh, rho, norms, share, tl = call(
        functools.partial(right_kernel, sizes),
        "v" * 7 + "hh",
        [
            ((rows, hid), f32, "v"), ((rows, RANK), bf16, "v"), ((rows, RANK), bf16, "v"), ((RANK, hid), bf16, "v"), ((nr, kr, half), bf16, "v"),
            ((nr, ng, 1, 128), f32, "v"), ((kr, hid), f32, "v"), ((2, nb, RANK), bf16, "v"),
        ],
        [
            vmem(rows, hid), vmem(rows, hid, dtype=bf16), pltpu.SemaphoreType.DMA((2,)),
            vmem(nx, nz, rows // nc, RANK, dtype=bf16), vmem(nx, nz, rows // nc, RANK, dtype=bf16), vmem(nr, kr, hid), vmem(nr, kr, hid, dtype=bf16),
            vmem(nr - 1, kr, hid, dtype=bf16), vmem(nr, nb, RANK), vmem(nr, nb, RANK, dtype=bf16),
            vmem(nr - 1, nb, RANK, dtype=bf16), vmem(nb, RANK, dtype=bf16), vmem(nb, RANK, dtype=bf16),
            vmem(nr, kr, hid, dtype=bf16), vmem(kr, half, dtype=bf16), vmem(nr, kr, half, dtype=bf16),
            vmem(1, 128), vmem(ng, nz, 1, 128), vmem(nx, ng, 1, 128), vmem(nr, ng, 1, 128),
            pairs(1), pairs(nr - 1), pairs(nr - 1), pairs(nz), pairs(nx - 1), pairs(nr - 1), pairs(1), pairs(nr - 1),
            pairs(ng * nz - 1), pairs(nx - 1), pairs(nr - 1), pairs(1),
        ],
        (bufh, left, *start, tokens, mom, grad), 1,
    )
    mom_new, new, fac, hidden = call(
        last_kernel, "v" * 10,
        [((rows, hid), f32, "h"), (weights.shape, f32, "h"), ((kr, hid), f32, "v"), ((nb, half), bf16, "v")],
        [vmem(*weights.shape), pltpu.SemaphoreType.DMA((2 * CHUNKS + 1,))],
        (mom_new, weights, base, lh, oth, rh, rho, norms, share, tl),
    )
    return mom_new[None], fac.T[None], new, hidden


def solution(mesh):
    sizes = tuple(mesh.shape[a] for a in ("row", "col", "grp"))
    in_specs = (
        P("grp", "row", "col"),
        P("grp", "row", "col"),
        P("grp", "col", "row"),
        P(None, "row", ("col", "grp")),
        P(None, "row"),
    )
    out_specs = (
        P("grp", "row", "col"),
        P("grp", "col", "row"),
        P(None, "row", ("col", "grp")),
        P("row", ("col", "grp")),
    )
    return jax.shard_map(
        functools.partial(local, sizes), mesh=mesh, in_specs=in_specs, out_specs=out_specs, check_vma=False
    )
```

```python
import functools
import math

import jax
import jax.numpy as jnp
from jax import lax
from jax.experimental import pallas as pl
from jax.experimental.pallas import tpu as pltpu
from jax.sharding import PartitionSpec as P

D = 4096
HID = 16384
RANK = 256
BATCH = 256
FEEDBACK = 0.05
EPSILON = 1e-06
STEP = 0.4 * math.sqrt(max(D, HID))
CHUNKS = 4
NEAR = 0.1
NX = 4

f32, bf16 = jnp.float32, jnp.bfloat16
HI = lax.Precision.HIGHEST
MESH = pl.DeviceIdType.MESH
NN = (((1,), (0,)), ((), ()))
NT = (((1,), (1,)), ((), ()))
TN = (((0,), (0,)), ((), ()))


def mm(a, b, dims=NN, precision=None):
    return lax.dot_general(a, b, dims, precision=precision, preferred_element_type=f32)


def around(i, n):
    return [i if d == 0 else i + d - jnp.where(i + d >= n, n, 0) for d in range(n)]


def far_first(offsets, *rings):
    def way(offset):
        return sum(min(d, n - d) for d, n in zip(offset, rings))

    return sorted((offset for offset in offsets if any(offset)), key=lambda offset: -way(offset))


class Place:
    def __init__(self, sizes):
        self.nr, self.nc, self.ng = sizes
        self.nx, self.nz, self.ny = NX, self.nc // NX, self.nr // 2
        self.r, self.c, self.g = (lax.axis_index(a) for a in ("row", "col", "grp"))
        self.x, self.z = lax.rem(self.c, self.nx), lax.div(self.c, self.nx)
        self.core = lax.rem(self.r, 2)
        self.xs = around(self.x, self.nx)
        ys = around(lax.div(self.r, 2), self.ny)
        self.rs = {(dy, dc): 2 * ys[dy] + (1 - self.core if dc else self.core) for dy in range(self.ny) for dc in range(2)}
        self.row = far_first(self.rs, self.ny)
        self.line = [(d,) for d in range(1, self.nx)]
        self.line = [d for (d,) in far_first(self.line, self.nx)]
        self.plane = far_first([(dx, *d) for dx in range(self.nx) for d in self.rs], self.nx, self.ny)
        last = self.nz - 1
        self.stack = [
            jnp.where(
                self.z <= last // 2,
                last - k - jnp.where(last - k <= self.z, 1, 0),
                k + jnp.where(k >= self.z, 1, 0),
            )
            for k in range(last)
        ]
        around_both = around(self.g * self.nz + self.z, self.ng * self.nz)
        self.ring = [around_both[d] for (d,) in far_first([(d,) for d in range(len(around_both))], len(around_both))]

    def at(self, row=(0, 0), dx=0, z=None, g=None):
        z = self.z if z is None else z
        return (self.rs[row], z * self.nx + self.xs[dx], self.g if g is None else g)

    def up(self, k):
        g = jnp.where(self.ring[k] >= self.nz, 1, 0)
        return self.at(z=self.ring[k] - g * self.nz, g=g)


def greet(partners):
    barrier = pltpu.get_barrier_semaphore()
    for device in partners:
        pl.semaphore_signal(barrier, inc=1, device_id=device, device_id_type=MESH)
    return lambda: pl.semaphore_wait(barrier, len(partners))


def remote(src, dst, sent, received, device):
    return pltpu.make_async_remote_copy(
        src_ref=src, dst_ref=dst, send_sem=sent, recv_sem=received, device_id=device, device_id_type=MESH
    )


def send(src, dst, sems, k, device):
    copy = remote(src, dst, sems.at[0, k], sems.at[1, k], device)
    copy.start()
    return copy


def send_line(pick, slot, sems, at):
    waits = []
    for k, other in enumerate(at.stack):
        device = at.at(z=other)
        remote(pick(other), slot(at.z), sems.at[0, k], sems.at[1, at.z], device).start()
        waits.append(remote(pick(other), slot(other), sems.at[0, k], sems.at[1, other], device))
    return waits


def arrived(copies):
    for copy in copies:
        copy.wait_recv()


def left_kernel(sizes, mom_h, grad_h, fq_h, w_h, tok_h, left_o, gram_o, base_o, bufh,
                mom, grad, fq, w, tok, s_in, qbuf, part, partb, rx, sx, sxb, rz, l512, gp, rg, gf, pre, rpre,
                s_q, s_x, s_z, s_az, s_ax, s_g, s_ag, s_p):
    at = Place(sizes)
    nr, nx, nz = at.nr, at.nx, at.nz
    ready = greet([at.at(z=other) for other in at.stack] + [at.at(row=d[1:], dx=d[0]) for d in at.plane])
    r, x, z = at.r, at.x, at.z
    loads = [
        pltpu.make_async_copy(a, b, s_in.at[k])
        for k, (a, b) in enumerate(((fq_h, fq), (mom_h, mom), (grad_h, grad), (tok_h, tok), (w_h, w)))
    ]
    for load in loads:
        load.start()
    loads[0].wait()
    qbuf[r] = fq[...].astype(bf16)
    ready()
    got_q = [send(qbuf.at[r], qbuf.at[r], s_q, k, at.at(row=d)) for k, d in enumerate(at.row)]
    loads[1].wait()
    loads[2].wait()
    bufh[...] = (mom[...] + grad[...].astype(f32)).astype(bf16)
    arrived(got_q)
    part[...] = mm(bufh[...], qbuf[...].reshape(RANK, -1), NT).reshape(part.shape)
    partb[...] = part[...].astype(bf16)
    got_x = [send(partb.at[at.xs[d]], rx.at[k], s_x, k, at.at(dx=d)) for k, d in enumerate(at.line)]
    loads[3].wait()
    loads[4].wait()
    for p in range(2):
        high = w[p].astype(bf16)
        low = (w[p] - high.astype(f32)).astype(bf16)
        pre[:, p] = (mm(tok[...], high) + mm(tok[...], low)).reshape(pre[:, p].shape)
    arrived(got_x)
    sx[...] = (part[x] + jnp.sum(rx[...].astype(f32), axis=0)).reshape(sx.shape)
    sxb[...] = sx[...].astype(bf16)
    rz[z] = jnp.zeros(rz.shape[1:], bf16)
    got_z = send_line(lambda other: sxb.at[other], lambda place: rz.at[place], s_z, at)
    got_p = [send(pre.at[at.rs[d]], rpre.at[k], s_p, k, at.at(row=d)) for k, d in enumerate(at.row)]
    arrived(got_z)
    l512[x, z] = (sx[z] + jnp.sum(rz[...].astype(f32), axis=0)).astype(bf16)
    got_az = send_line(lambda other: l512.at[x, z], lambda place: l512.at[x, place], s_az, at)
    arrived(got_az)
    rows = l512[x].reshape(-1, RANK)
    gram = mm(rows, rows, TN)
    h = RANK // 2
    i, j = (lax.broadcasted_iota(jnp.int32, (h, h), d) for d in (0, 1))
    packed = jnp.where(i >= j, gram[:h, :h], gram[h:, h:])
    gp[: gp.shape[0] // 2, :-1] = packed.reshape(gp.shape[0] // 2, -1, h)
    gp[gp.shape[0] // 2 :, :-1] = gram[h:, :h].reshape(gp.shape[0] // 2, -1, h)
    gp[:, -1:] = jnp.broadcast_to(
        jnp.sum(jnp.where(i == j, gram[h:, h:], 0.0), axis=0, keepdims=True), (gp.shape[0], 1, h)
    )
    got_g = []
    for k, (dx, *d) in enumerate(at.plane):
        m = at.xs[dx] * nr + at.rs[*d]
        got_g.append(send(gp.at[m], rg.at[k], s_g, k, at.at(row=(*d,), dx=dx)))
    got_ax = [send(l512.at[x], l512.at[x], s_ax, k, at.at(dx=d)) for k, d in enumerate(at.line)]
    arrived(got_g)
    m = x * nr + r
    gf[m] = gp[m] + jnp.sum(rg[...], axis=0)
    got_ag = [send(gf.at[m], gf.at[m], s_ag, k, at.at(row=d[1:], dx=d[0])) for k, d in enumerate(at.plane)]
    arrived(got_p)
    base_o[...] = pre[r] + jnp.sum(rpre[...], axis=0)
    arrived(got_ax)
    left_o[...] = l512[...].reshape(left_o.shape)
    arrived(got_ag)
    gram_o[:RANK] = gf[:, :-1].reshape(RANK, -1)
    gram_o[RANK:] = jnp.broadcast_to(gf[0, -1:], (8, gf.shape[2]))
    for copies in (got_q, got_x, got_p, got_z, got_az, got_g, got_ax, got_ag):
        for copy in copies:
            copy.wait_send()


def tri_half(e):
    i, j = (lax.broadcasted_iota(jnp.int32, e.shape, d) for d in (0, 1))
    return jnp.where(i > j, e, jnp.where(i == j, 0.5 * e, 0.0))


def residual(w, a, precision=None):
    i, j = (lax.broadcasted_iota(jnp.int32, a.shape, d) for d in (0, 1))
    return mm(mm(w, a, NN, precision), w, NT, precision) - jnp.where(i == j, 1.0, 0.0)


def start_kernel(packed, a_o, w_o, across_o, near_o, gram, s):
    n, h = RANK, RANK // 2
    i, j = (lax.broadcasted_iota(jnp.int32, (h, h), d) for d in (0, 1))
    both, turned = packed[:h], packed[:h].T
    gram[:h, :h] = jnp.where(i >= j, both, turned)
    gram[h:, h:] = jnp.where(i > j, turned, jnp.where(i == j, packed[n : n + 1], both))
    gram[h:, :h] = packed[h:n]
    gram[:h, h:] = packed[h:n].T
    i, j = (lax.broadcasted_iota(jnp.int32, (n, n), d) for d in (0, 1))
    eye = jnp.where(i == j, 1.0, 0.0)
    diagonal = jnp.where(i == j, gram[...], 0.0)
    down = lax.rsqrt(jnp.sum(diagonal, axis=1, keepdims=True))
    across = lax.rsqrt(jnp.sum(diagonal, axis=0, keepdims=True))
    a = gram[...] * down * across
    a_o[...] = a
    across_o[...] = jnp.broadcast_to(across, across_o.shape)
    w = eye - tri_half(jnp.where(i == j, 0.0, a))
    w = w - mm(tri_half(residual(w, a)), w)
    e = residual(w, a)
    w_o[...] = w - mm(tri_half(e), w)
    far = jnp.sum(e * e)
    near_o[...] = jnp.ones(near_o.shape, f32)

    @pl.when(~(far < NEAR))
    def _():
        s[:, :n] = gram[...]
        s[:, n:] = eye
        row = lax.broadcasted_iota(jnp.int32, (n, 1), 0)

        def eliminate(k, _):
            line = s[pl.ds(k, 1), :]
            column = jnp.sum(jnp.where(j == k, s[:, :n], 0.0), axis=1, keepdims=True)
            pivot = jnp.sum(jnp.where(row == k, column, 0.0), axis=0, keepdims=True)
            s[...] = s[...] - jnp.where(row > k, column / pivot, 0.0) * line
            return 0

        lax.fori_loop(0, n, eliminate, 0)
        pivots = jnp.sum(jnp.where(i == j, s[:, :n], 0.0), axis=1, keepdims=True)
        w_o[...] = s[:, n:] / jnp.sqrt(pivots)
        across_o[...] = jnp.ones(across_o.shape, f32)
        near_o[...] = jnp.zeros(near_o.shape, f32)


def right_kernel(sizes, bufh, left, a, w, across, near, tok, mom_h, grad_h, mom_o, lh_o, oth_o, rh_o, rho_o, nb_o, share_o, tl_o,
                 mom, grad, s_in, lh, oth, rt, rtb, rrt, tl, tlb, rtl, tls, tlo, rh, sho, rho, sq, sqz, sqx,
                 s_l, s_rt, s_tl, s_lz, s_lx, s_rh, s_sh, s_ro, s_sq, s_nb, s_to):
    at = Place(sizes)
    nr, nx, nz, ng = at.nr, at.nx, at.nz, at.ng
    r, c, g, x, z = at.r, at.c, at.g, at.x, at.z
    upwards = range(len(at.ring))
    ready = greet(
        [at.up(k) for k in upwards] + [at.at(row=d[1:], dx=d[0]) for d in at.plane]
    )
    o = 1 - g
    kr = RANK // nr
    half = sho.shape[1]

    loads = [pltpu.make_async_copy(mom_h, mom, s_in.at[0]), pltpu.make_async_copy(grad_h, grad, s_in.at[1])]
    for load in loads:
        load.start()
    inverse = w[...]
    for _ in range(2):
        error = jnp.where(near[:1, :1] > 0, tri_half(residual(inverse, a[...], HI)), 0.0)
        inverse = inverse - mm(error, inverse)
    inverse = inverse * across[:1]
    high = inverse.astype(bf16)
    low = (inverse - high.astype(f32)).astype(bf16)
    left_h = (mm(left[...], high, NT) + mm(left[...], low, NT)).astype(bf16)
    lh[...] = left_h.reshape(lh.shape)
    ready()
    got_l = [send(lh.at[x, z], oth.at[x, z], s_l, 0, at.at(g=o))]
    rt[...] = mm(left_h, bufh[...], TN).reshape(rt.shape)
    rtb[...] = rt[...].astype(bf16)
    got_rt = [send(rtb.at[at.rs[d]], rrt.at[k], s_rt, k, at.at(row=d)) for k, d in enumerate(at.row)]
    tl[...] = mm(tok[...], left_h).reshape(tl.shape)
    tlb[...] = tl[...].astype(bf16)
    got_tl = [send(tlb.at[at.rs[d]], rtl.at[k], s_tl, k, at.at(row=d)) for k, d in enumerate(at.row)]
    arrived(got_rt)
    share = rt[r] + jnp.sum(rrt[...].astype(f32), axis=0)
    share_o[...] = share
    rh[r] = share.astype(bf16)
    sho[...] = share_o[:, pl.ds(pl.multiple_of(o * half, half), half)].astype(bf16)
    got_sh = [send(sho, rho.at[r], s_sh, 0, at.at(g=o))]
    eye = lax.broadcasted_iota(jnp.int32, (kr, 128), 0) == lax.broadcasted_iota(jnp.int32, (kr, 128), 1)
    squares = jnp.sum(share * share, axis=1, keepdims=True)
    line = jnp.sum(jnp.where(eye, squares, 0.0), axis=0, keepdims=True)
    sqz[g, z] = line
    sq[...] = line
    got_sq = [send(sq, sqz.at[g, z], s_sq, k, at.up(k)) for k in upwards]
    arrived(got_l)
    got_lz = send_line(lambda other: oth.at[x, z], lambda place: oth.at[x, place], s_lz, at)
    got_rh = [send(rh.at[r], rh.at[r], s_rh, k, at.at(row=d)) for k, d in enumerate(at.row)]
    arrived(got_tl)
    tls[...] = (tl[r] + jnp.sum(rtl[...].astype(f32), axis=0)).astype(bf16)
    got_to = [send(tls, tlo, s_to, 0, at.at(g=o))]
    arrived(got_sh)
    got_ro = [send(rho.at[r], rho.at[r], s_ro, k, at.at(row=d)) for k, d in enumerate(at.row)]
    arrived(got_lz)
    got_lx = [send(oth.at[x], oth.at[x], s_lx, k, at.at(dx=d)) for k, d in enumerate(at.line)]
    arrived(got_sq)
    sqx[x, r] = jnp.sum(sqz[...], axis=1)
    got_nb = [send(sqx.at[x, r], sqx.at[x, r], s_nb, k, at.at(row=d[1:], dx=d[0])) for k, d in enumerate(at.plane)]
    lh_o[...] = lh[...].reshape(lh_o.shape)
    for load in loads:
        load.wait()
    arrived(got_rh)
    mom_o[...] = mom[...] + grad[...].astype(f32) - FEEDBACK * mm(left_h, rh[...].reshape(RANK, -1))
    rh_o[...] = rh[...].reshape(rh_o.shape)
    arrived(got_lx)
    oth_o[...] = oth[...].reshape(oth_o.shape)
    arrived(got_nb)
    nb_o[...] = jnp.sum(sqx[...], axis=0)
    arrived(got_ro)
    rho_o[...] = rho[...]
    arrived(got_to)
    tl_o[0] = tls[...]
    tl_o[1] = tlo[...]
    for copies in (got_l, got_rt, got_tl, got_lz, got_sh, got_sq, got_rh, got_lx, got_nb, got_ro, got_to):
        for copy in copies:
            copy.wait_send()


def last_kernel(mom, w, base, lh, oth, rh, rho, nb, share, tl, mom_h, new_h, fac_o, hid_o, new_v, sems):
    r, g = lax.axis_index("row"), lax.axis_index("grp")
    o = 1 - g
    nr, kr, half = rho.shape
    rows = lh.shape[0]
    chunk = rows // CHUNKS
    copies = []

    def out(src, dst):
        copies.append(pltpu.make_async_copy(src, dst, sems.at[len(copies)]))
        copies[-1].start()

    out(mom, mom_h)
    eye = lax.broadcasted_iota(jnp.int32, (kr, 128), 0) == lax.broadcasted_iota(jnp.int32, (kr, 128), 1)

    def columns(norms):
        norms = jnp.broadcast_to(jnp.sqrt(norms + EPSILON), (norms.shape[0], kr, 128))
        return jnp.sum(jnp.where(eye[None], norms, 0.0), axis=2, keepdims=True)

    own = rh[:, pl.ds(pl.multiple_of(g * half, half), half)].astype(f32).reshape(rho.shape)
    own_q = (own / columns(nb[:, g])).astype(bf16).reshape(RANK, half)
    other_q = (rho[...].astype(f32) / columns(nb[:, o])).astype(bf16).reshape(RANK, half)
    for p, q, factor in ((g, own_q, lh), (o, other_q, oth)):
        for k in range(CHUNKS):
            at = pl.ds(k * chunk, chunk)
            new_v[p, at] = w[p, at] - STEP * mm(factor[at], q)
            out(new_v.at[p, at], new_h.at[p, at])
    fac_o[...] = share[...] / columns(nb[r, g][None])[0]
    own_pre = base[g] - STEP * mm(tl[0], own_q)
    other_pre = base[o] - STEP * mm(tl[1], other_q)
    gate = jnp.where(g == 0, own_pre, other_pre)
    up = jnp.where(g == 0, other_pre, own_pre)
    hid_o[...] = (gate / (1.0 + jnp.exp(-gate)) * up).astype(bf16)
    for copy in copies:
        copy.wait()


def vmem(*shape, dtype=f32):
    return pltpu.VMEM(shape, dtype)


def pairs(n):
    return pltpu.SemaphoreType.DMA((2, n))


def call(kernel, ins, outs, scratch, args, collective_id=None, limit=24):
    where = {"v": pltpu.VMEM, "h": pltpu.HBM}
    params = {} if collective_id is None else dict(collective_id=collective_id, has_side_effects=True)
    return pl.pallas_call(
        kernel,
        out_shape=[jax.ShapeDtypeStruct(s, t) for s, t, _ in outs],
        in_specs=[pl.BlockSpec(memory_space=where[k]) for k in ins],
        out_specs=[pl.BlockSpec(memory_space=where[k]) for _, _, k in outs],
        scratch_shapes=scratch,
        compiler_params=pltpu.CompilerParams(vmem_limit_bytes=int(limit * 2**20), **params),
    )(*args)


def local(sizes, momentum, gradient, factor_q, weights, tokens):
    nr, nc, ng = sizes
    nx, nz = NX, nc // NX
    mom, grad, fq = momentum[0], gradient[0], factor_q[0].T
    rows, hid = mom.shape
    part, kr, nb = nx * nr, RANK // nr, BATCH // nr
    half = hid // ng

    def piece(n):
        return n, RANK // part + 1, RANK // 2

    left, gram, base, bufh = call(
        functools.partial(left_kernel, sizes),
        "hhhhh",
        [((rows, RANK), bf16, "v"), ((RANK + 8, RANK // 2), f32, "v"), ((2, nb, half), f32, "v"), ((rows, hid), bf16, "v")],
        [
            vmem(rows, hid), vmem(rows, hid, dtype=bf16), vmem(kr, hid), vmem(*weights.shape), vmem(*tokens.shape, dtype=bf16),
            pltpu.SemaphoreType.DMA((5,)), vmem(nr, kr, hid, dtype=bf16),
            vmem(nx, rows // nx, RANK), vmem(nx, rows // nx, RANK, dtype=bf16), vmem(nx - 1, rows // nx, RANK, dtype=bf16),
            vmem(nz, rows // nc, RANK), vmem(nz, rows // nc, RANK, dtype=bf16), vmem(nz, rows // nc, RANK, dtype=bf16),
            vmem(nx, nz, rows // nc, RANK, dtype=bf16),
            vmem(*piece(part)), vmem(*piece(part - 1)), vmem(*piece(part)),
            vmem(nr, 2, nb, half), vmem(nr - 1, 2, nb, half),
            pairs(nr - 1), pairs(nx - 1), pairs(nz), pairs(nz), pairs(nx - 1), pairs(part - 1), pairs(part - 1),
            pairs(nr - 1),
        ],
        [pltpu.with_memory_space_constraint(a, pltpu.HBM) for a in (mom, grad, fq, weights, tokens)], 0,
    )
    square = ((RANK, RANK), f32, "v")
    start = call(
        start_kernel, "v", [square, square, ((8, RANK), f32, "v"), ((8, 128), f32, "v")],
        [vmem(RANK, RANK), vmem(RANK, 2 * RANK)], (gram,),
    )
    mom_new, lh, oth, rh, rho, norms, share, tl = call(
        functools.partial(right_kernel, sizes),
        "v" * 7 + "hh",
        [
            ((rows, hid), f32, "v"), ((rows, RANK), bf16, "v"), ((rows, RANK), bf16, "v"), ((RANK, hid), bf16, "v"), ((nr, kr, half), bf16, "v"),
            ((nr, ng, 1, 128), f32, "v"), ((kr, hid), f32, "v"), ((2, nb, RANK), bf16, "v"),
        ],
        [
            vmem(rows, hid), vmem(rows, hid, dtype=bf16), pltpu.SemaphoreType.DMA((2,)),
            vmem(nx, nz, rows // nc, RANK, dtype=bf16), vmem(nx, nz, rows // nc, RANK, dtype=bf16), vmem(nr, kr, hid), vmem(nr, kr, hid, dtype=bf16),
            vmem(nr - 1, kr, hid, dtype=bf16), vmem(nr, nb, RANK), vmem(nr, nb, RANK, dtype=bf16),
            vmem(nr - 1, nb, RANK, dtype=bf16), vmem(nb, RANK, dtype=bf16), vmem(nb, RANK, dtype=bf16),
            vmem(nr, kr, hid, dtype=bf16), vmem(kr, half, dtype=bf16), vmem(nr, kr, half, dtype=bf16),
            vmem(1, 128), vmem(ng, nz, 1, 128), vmem(nx, nr, ng, 1, 128),
            pairs(1), pairs(nr - 1), pairs(nr - 1), pairs(nz), pairs(nx - 1), pairs(nr - 1), pairs(1), pairs(nr - 1),
            pairs(ng * nz - 1), pairs(part - 1), pairs(1),
        ],
        (bufh, left, *start, tokens, mom, grad), 1,
    )
    mom_new, new, fac, hidden = call(
        last_kernel, "v" * 10,
        [((rows, hid), f32, "h"), (weights.shape, f32, "h"), ((kr, hid), f32, "v"), ((nb, half), bf16, "v")],
        [vmem(*weights.shape), pltpu.SemaphoreType.DMA((2 * CHUNKS + 1,))],
        (mom_new, weights, base, lh, oth, rh, rho, norms, share, tl),
    )
    return mom_new[None], fac.T[None], new, hidden


def solution(mesh):
    sizes = tuple(mesh.shape[a] for a in ("row", "col", "grp"))
    in_specs = (
        P("grp", "row", "col"),
        P("grp", "row", "col"),
        P("grp", "col", "row"),
        P(None, "row", ("col", "grp")),
        P(None, "row"),
    )
    out_specs = (
        P("grp", "row", "col"),
        P("grp", "col", "row"),
        P(None, "row", ("col", "grp")),
        P("row", ("col", "grp")),
    )
    return jax.shard_map(
        functools.partial(local, sizes), mesh=mesh, in_specs=in_specs, out_specs=out_specs, check_vma=False
    )
```

```python
import functools
import math

import jax
import jax.numpy as jnp
from jax import lax
from jax.experimental import pallas as pl
from jax.experimental.pallas import tpu as pltpu
from jax.sharding import PartitionSpec as P

D = 4096
HID = 16384
RANK = 256
BATCH = 256
FEEDBACK = 0.05
EPSILON = 1e-06
STEP = 0.4 * math.sqrt(max(D, HID))
CHUNKS = 4
NEAR = 0.1
NX = 4

f32, bf16 = jnp.float32, jnp.bfloat16
HI = lax.Precision.HIGHEST
MESH = pl.DeviceIdType.MESH
NN = (((1,), (0,)), ((), ()))
NT = (((1,), (1,)), ((), ()))
TN = (((0,), (0,)), ((), ()))


def mm(a, b, dims=NN, precision=None):
    return lax.dot_general(a, b, dims, precision=precision, preferred_element_type=f32)


def around(i, n):
    return [i if d == 0 else i + d - jnp.where(i + d >= n, n, 0) for d in range(n)]


def far_first(offsets, *rings):
    def way(offset):
        return sum(min(d, n - d) for d, n in zip(offset, rings))

    return sorted((offset for offset in offsets if any(offset)), key=lambda offset: -way(offset))


class Place:
    def __init__(self, sizes):
        self.nr, self.nc, self.ng = sizes
        self.nx, self.nz, self.ny = NX, self.nc // NX, self.nr // 2
        self.r, self.c, self.g = (lax.axis_index(a) for a in ("row", "col", "grp"))
        self.x, self.z = lax.rem(self.c, self.nx), lax.div(self.c, self.nx)
        self.core = lax.rem(self.r, 2)
        self.xs = around(self.x, self.nx)
        ys = around(lax.div(self.r, 2), self.ny)
        self.rs = {(dy, dc): 2 * ys[dy] + (1 - self.core if dc else self.core) for dy in range(self.ny) for dc in range(2)}
        self.row = far_first(self.rs, self.ny)
        self.line = [(d,) for d in range(1, self.nx)]
        self.line = [d for (d,) in far_first(self.line, self.nx)]
        self.plane = far_first([(dx, *d) for dx in range(self.nx) for d in self.rs], self.nx, self.ny)
        last = self.nz - 1
        self.stack = [
            jnp.where(
                self.z <= last // 2,
                last - k - jnp.where(last - k <= self.z, 1, 0),
                k + jnp.where(k >= self.z, 1, 0),
            )
            for k in range(last)
        ]
        around_both = around(self.g * self.nz + self.z, self.ng * self.nz)
        self.ring = [around_both[d] for (d,) in far_first([(d,) for d in range(len(around_both))], len(around_both))]

    def at(self, row=(0, 0), dx=0, z=None, g=None):
        z = self.z if z is None else z
        return (self.rs[row], z * self.nx + self.xs[dx], self.g if g is None else g)

    def up(self, k):
        g = jnp.where(self.ring[k] >= self.nz, 1, 0)
        return self.at(z=self.ring[k] - g * self.nz, g=g)


def greet(partners):
    barrier = pltpu.get_barrier_semaphore()
    for device in partners:
        pl.semaphore_signal(barrier, inc=1, device_id=device, device_id_type=MESH)
    return lambda: pl.semaphore_wait(barrier, len(partners))


def remote(src, dst, sent, received, device):
    return pltpu.make_async_remote_copy(
        src_ref=src, dst_ref=dst, send_sem=sent, recv_sem=received, device_id=device, device_id_type=MESH
    )


def send(src, dst, sems, k, device):
    copy = remote(src, dst, sems.at[0, k], sems.at[1, k], device)
    copy.start()
    return copy


def send_line(pick, slot, sems, at):
    waits = []
    for k, other in enumerate(at.stack):
        device = at.at(z=other)
        remote(pick(other), slot(at.z), sems.at[0, k], sems.at[1, at.z], device).start()
        waits.append(remote(pick(other), slot(other), sems.at[0, k], sems.at[1, other], device))
    return waits


def arrived(copies):
    for copy in copies:
        copy.wait_recv()


def left_kernel(sizes, mom_h, grad_h, fq_h, w_h, tok_h, left_o, gram_o, base_o, bufh,
                mom, grad, fq, w, tok, s_in, qbuf, part, partb, rx, sx, sxb, rz, l512, gp, rg, gf, pre, rpre,
                s_q, s_x, s_z, s_az, s_ax, s_g, s_ag, s_p):
    at = Place(sizes)
    nr, nx, nz = at.nr, at.nx, at.nz
    ready = greet([at.at(z=other) for other in at.stack] + [at.at(row=d[1:], dx=d[0]) for d in at.plane])
    r, x, z = at.r, at.x, at.z
    loads = [
        pltpu.make_async_copy(a, b, s_in.at[k])
        for k, (a, b) in enumerate(((fq_h, fq), (mom_h, mom), (grad_h, grad), (tok_h, tok), (w_h, w)))
    ]
    for load in loads:
        load.start()
    loads[0].wait()
    qbuf[r] = fq[...].astype(bf16)
    ready()
    got_q = [send(qbuf.at[r], qbuf.at[r], s_q, k, at.at(row=d)) for k, d in enumerate(at.row)]
    loads[1].wait()
    loads[2].wait()
    bufh[...] = (mom[...] + grad[...].astype(f32)).astype(bf16)
    arrived(got_q)
    part[...] = mm(bufh[...], qbuf[...].reshape(RANK, -1), NT).reshape(part.shape)
    partb[...] = part[...].astype(bf16)
    got_x = [send(partb.at[at.xs[d]], rx.at[k], s_x, k, at.at(dx=d)) for k, d in enumerate(at.line)]
    loads[3].wait()
    loads[4].wait()
    for p in range(2):
        high = w[p].astype(bf16)
        low = (w[p] - high.astype(f32)).astype(bf16)
        pre[:, p] = (mm(tok[...], high) + mm(tok[...], low)).reshape(pre[:, p].shape)
    arrived(got_x)
    sx[...] = (part[x] + jnp.sum(rx[...].astype(f32), axis=0)).reshape(sx.shape)
    sxb[...] = sx[...].astype(bf16)
    rz[z] = jnp.zeros(rz.shape[1:], bf16)
    got_z = send_line(lambda other: sxb.at[other], lambda place: rz.at[place], s_z, at)
    got_p = [send(pre.at[at.rs[d]], rpre.at[k], s_p, k, at.at(row=d)) for k, d in enumerate(at.row)]
    arrived(got_z)
    l512[x, z] = (sx[z] + jnp.sum(rz[...].astype(f32), axis=0)).astype(bf16)
    got_az = send_line(lambda other: l512.at[x, z], lambda place: l512.at[x, place], s_az, at)
    arrived(got_az)
    rows = l512[x].reshape(-1, RANK)
    gram = mm(rows, rows, TN)
    h = RANK // 2
    i, j = (lax.broadcasted_iota(jnp.int32, (h, h), d) for d in (0, 1))
    packed = jnp.where(i >= j, gram[:h, :h], gram[h:, h:])
    gp[: gp.shape[0] // 2, :-1] = packed.reshape(gp.shape[0] // 2, -1, h)
    gp[gp.shape[0] // 2 :, :-1] = gram[h:, :h].reshape(gp.shape[0] // 2, -1, h)
    gp[:, -1:] = jnp.broadcast_to(
        jnp.sum(jnp.where(i == j, gram[h:, h:], 0.0), axis=0, keepdims=True), (gp.shape[0], 1, h)
    )
    got_g = []
    for k, (dx, *d) in enumerate(at.plane):
        m = at.xs[dx] * nr + at.rs[*d]
        got_g.append(send(gp.at[m], rg.at[k], s_g, k, at.at(row=(*d,), dx=dx)))
    got_ax = [send(l512.at[x], l512.at[x], s_ax, k, at.at(dx=d)) for k, d in enumerate(at.line)]
    arrived(got_g)
    m = x * nr + r
    gf[m] = gp[m] + jnp.sum(rg[...], axis=0)
    got_ag = [send(gf.at[m], gf.at[m], s_ag, k, at.at(row=d[1:], dx=d[0])) for k, d in enumerate(at.plane)]
    arrived(got_p)
    base_o[...] = pre[r] + jnp.sum(rpre[...], axis=0)
    arrived(got_ax)
    left_o[...] = l512[...].reshape(left_o.shape)
    arrived(got_ag)
    gram_o[:RANK] = gf[:, :-1].reshape(RANK, -1)
    gram_o[RANK:] = jnp.broadcast_to(gf[0, -1:], (8, gf.shape[2]))
    for copies in (got_q, got_x, got_p, got_z, got_az, got_g, got_ax, got_ag):
        for copy in copies:
            copy.wait_send()


def tri_half(e):
    i, j = (lax.broadcasted_iota(jnp.int32, e.shape, d) for d in (0, 1))
    return jnp.where(i > j, e, jnp.where(i == j, 0.5 * e, 0.0))


def residual(w, a, precision=None):
    i, j = (lax.broadcasted_iota(jnp.int32, a.shape, d) for d in (0, 1))
    return mm(mm(w, a, NN, precision), w, NT, precision) - jnp.where(i == j, 1.0, 0.0)


def start_kernel(packed, a_o, w_o, across_o, near_o, gram, s):
    n, h = RANK, RANK // 2
    i, j = (lax.broadcasted_iota(jnp.int32, (h, h), d) for d in (0, 1))
    both, turned = packed[:h], packed[:h].T
    gram[:h, :h] = jnp.where(i >= j, both, turned)
    gram[h:, h:] = jnp.where(i > j, turned, jnp.where(i == j, packed[n : n + 1], both))
    gram[h:, :h] = packed[h:n]
    gram[:h, h:] = packed[h:n].T
    i, j = (lax.broadcasted_iota(jnp.int32, (n, n), d) for d in (0, 1))
    eye = jnp.where(i == j, 1.0, 0.0)
    diagonal = jnp.where(i == j, gram[...], 0.0)
    down = lax.rsqrt(jnp.sum(diagonal, axis=1, keepdims=True))
    across = lax.rsqrt(jnp.sum(diagonal, axis=0, keepdims=True))
    a = gram[...] * down * across
    a_o[...] = a
    across_o[...] = jnp.broadcast_to(across, across_o.shape)
    w = eye - tri_half(jnp.where(i == j, 0.0, a))
    w = w - mm(tri_half(residual(w, a)), w)
    e = residual(w, a)
    w_o[...] = w - mm(tri_half(e), w)
    far = jnp.sum(e * e)
    near_o[...] = jnp.ones(near_o.shape, f32)

    @pl.when(~(far < NEAR))
    def _():
        s[:, :n] = gram[...]
        s[:, n:] = eye
        row = lax.broadcasted_iota(jnp.int32, (n, 1), 0)

        def eliminate(k, _):
            line = s[pl.ds(k, 1), :]
            column = jnp.sum(jnp.where(j == k, s[:, :n], 0.0), axis=1, keepdims=True)
            pivot = jnp.sum(jnp.where(row == k, column, 0.0), axis=0, keepdims=True)
            s[...] = s[...] - jnp.where(row > k, column / pivot, 0.0) * line
            return 0

        lax.fori_loop(0, n, eliminate, 0)
        pivots = jnp.sum(jnp.where(i == j, s[:, :n], 0.0), axis=1, keepdims=True)
        w_o[...] = s[:, n:] / jnp.sqrt(pivots)
        across_o[...] = jnp.ones(across_o.shape, f32)
        near_o[...] = jnp.zeros(near_o.shape, f32)


def right_kernel(sizes, bufh, left, a, w, across, near, tok, mom_h, grad_h, mom_o, lh_o, oth_o, rh_o, rho_o, nb_o, share_o, tl_o,
                 mom, grad, s_in, lh, oth, rt, rtb, rrt, tl, tlb, rtl, tls, tlo, rh, sho, rho, sq, sqz, sqx, nb,
                 s_l, s_rt, s_tl, s_lz, s_lx, s_rh, s_sh, s_ro, s_sq, s_sx, s_nb, s_to):
    at = Place(sizes)
    nr, nx, nz, ng = at.nr, at.nx, at.nz, at.ng
    r, c, g, x, z = at.r, at.c, at.g, at.x, at.z
    upwards = range(len(at.ring))
    ready = greet(
        [at.up(k) for k in upwards] + [at.at(row=d) for d in at.row] + [at.at(dx=d) for d in at.line]
    )
    o = 1 - g
    kr = RANK // nr
    half = sho.shape[1]

    loads = [pltpu.make_async_copy(mom_h, mom, s_in.at[0]), pltpu.make_async_copy(grad_h, grad, s_in.at[1])]
    for load in loads:
        load.start()
    inverse = w[...]
    for _ in range(2):
        error = jnp.where(near[:1, :1] > 0, tri_half(residual(inverse, a[...], HI)), 0.0)
        inverse = inverse - mm(error, inverse)
    inverse = inverse * across[:1]
    high = inverse.astype(bf16)
    low = (inverse - high.astype(f32)).astype(bf16)
    left_h = (mm(left[...], high, NT) + mm(left[...], low, NT)).astype(bf16)
    lh[...] = left_h.reshape(lh.shape)
    ready()
    got_l = [send(lh.at[x, z], oth.at[x, z], s_l, 0, at.at(g=o))]
    rt[...] = mm(left_h, bufh[...], TN).reshape(rt.shape)
    rtb[...] = rt[...].astype(bf16)
    got_rt = [send(rtb.at[at.rs[d]], rrt.at[k], s_rt, k, at.at(row=d)) for k, d in enumerate(at.row)]
    tl[...] = mm(tok[...], left_h).reshape(tl.shape)
    tlb[...] = tl[...].astype(bf16)
    got_tl = [send(tlb.at[at.rs[d]], rtl.at[k], s_tl, k, at.at(row=d)) for k, d in enumerate(at.row)]
    arrived(got_rt)
    share = rt[r] + jnp.sum(rrt[...].astype(f32), axis=0)
    share_o[...] = share
    rh[r] = share.astype(bf16)
    sho[...] = share_o[:, pl.ds(pl.multiple_of(o * half, half), half)].astype(bf16)
    got_sh = [send(sho, rho.at[r], s_sh, 0, at.at(g=o))]
    eye = lax.broadcasted_iota(jnp.int32, (kr, 128), 0) == lax.broadcasted_iota(jnp.int32, (kr, 128), 1)
    squares = jnp.sum(share * share, axis=1, keepdims=True)
    line = jnp.sum(jnp.where(eye, squares, 0.0), axis=0, keepdims=True)
    sqz[g, z] = line
    sq[...] = line
    got_sq = [send(sq, sqz.at[g, z], s_sq, k, at.up(k)) for k in upwards]
    got_rh = [send(rh.at[r], rh.at[r], s_rh, k, at.at(row=d)) for k, d in enumerate(at.row)]
    arrived(got_tl)
    tls[...] = (tl[r] + jnp.sum(rtl[...].astype(f32), axis=0)).astype(bf16)
    got_to = [send(tls, tlo, s_to, 0, at.at(g=o))]
    arrived(got_l)
    got_lz = send_line(lambda other: oth.at[x, z], lambda place: oth.at[x, place], s_lz, at)
    arrived(got_sh)
    got_ro = [send(rho.at[r], rho.at[r], s_ro, k, at.at(row=d)) for k, d in enumerate(at.row)]
    arrived(got_sq)
    sqx[x] = jnp.sum(sqz[...], axis=1)
    got_sx = [send(sqx.at[x], sqx.at[x], s_sx, k, at.at(dx=d)) for k, d in enumerate(at.line)]
    arrived(got_lz)
    got_lx = [send(oth.at[x], oth.at[x], s_lx, k, at.at(dx=d)) for k, d in enumerate(at.line)]
    arrived(got_sx)
    nb[r] = jnp.sum(sqx[...], axis=0)
    got_nb = [send(nb.at[r], nb.at[r], s_nb, k, at.at(row=d)) for k, d in enumerate(at.row)]
    lh_o[...] = lh[...].reshape(lh_o.shape)
    for load in loads:
        load.wait()
    arrived(got_rh)
    mom_o[...] = mom[...] + grad[...].astype(f32) - FEEDBACK * mm(left_h, rh[...].reshape(RANK, -1))
    rh_o[...] = rh[...].reshape(rh_o.shape)
    arrived(got_lx)
    oth_o[...] = oth[...].reshape(oth_o.shape)
    arrived(got_nb)
    nb_o[...] = nb[...]
    arrived(got_ro)
    rho_o[...] = rho[...]
    arrived(got_to)
    tl_o[0] = tls[...]
    tl_o[1] = tlo[...]
    for copies in (got_l, got_rt, got_tl, got_lz, got_sh, got_sq, got_sx, got_rh, got_lx, got_nb, got_ro, got_to):
        for copy in copies:
            copy.wait_send()


def last_kernel(mom, w, base, lh, oth, rh, rho, nb, share, tl, mom_h, new_h, fac_o, hid_o, new_v, sems):
    r, g = lax.axis_index("row"), lax.axis_index("grp")
    o = 1 - g
    nr, kr, half = rho.shape
    rows = lh.shape[0]
    chunk = rows // CHUNKS
    copies = []

    def out(src, dst):
        copies.append(pltpu.make_async_copy(src, dst, sems.at[len(copies)]))
        copies[-1].start()

    out(mom, mom_h)
    eye = lax.broadcasted_iota(jnp.int32, (kr, 128), 0) == lax.broadcasted_iota(jnp.int32, (kr, 128), 1)

    def columns(norms):
        norms = jnp.broadcast_to(jnp.sqrt(norms + EPSILON), (norms.shape[0], kr, 128))
        return jnp.sum(jnp.where(eye[None], norms, 0.0), axis=2, keepdims=True)

    own = rh[:, pl.ds(pl.multiple_of(g * half, half), half)].astype(f32).reshape(rho.shape)
    own_q = (own / columns(nb[:, g])).astype(bf16).reshape(RANK, half)
    other_q = (rho[...].astype(f32) / columns(nb[:, o])).astype(bf16).reshape(RANK, half)
    for p, q, factor in ((g, own_q, lh), (o, other_q, oth)):
        for k in range(CHUNKS):
            at = pl.ds(k * chunk, chunk)
            new_v[p, at] = w[p, at] - STEP * mm(factor[at], q)
            out(new_v.at[p, at], new_h.at[p, at])
    fac_o[...] = share[...] / columns(nb[r, g][None])[0]
    own_pre = base[g] - STEP * mm(tl[0], own_q)
    other_pre = base[o] - STEP * mm(tl[1], other_q)
    gate = jnp.where(g == 0, own_pre, other_pre)
    up = jnp.where(g == 0, other_pre, own_pre)
    hid_o[...] = (gate / (1.0 + jnp.exp(-gate)) * up).astype(bf16)
    for copy in copies:
        copy.wait()


def vmem(*shape, dtype=f32):
    return pltpu.VMEM(shape, dtype)


def pairs(n):
    return pltpu.SemaphoreType.DMA((2, n))


def call(kernel, ins, outs, scratch, args, collective_id=None, limit=24):
    where = {"v": pltpu.VMEM, "h": pltpu.HBM}
    params = {} if collective_id is None else dict(collective_id=collective_id, has_side_effects=True)
    return pl.pallas_call(
        kernel,
        out_shape=[jax.ShapeDtypeStruct(s, t) for s, t, _ in outs],
        in_specs=[pl.BlockSpec(memory_space=where[k]) for k in ins],
        out_specs=[pl.BlockSpec(memory_space=where[k]) for _, _, k in outs],
        scratch_shapes=scratch,
        compiler_params=pltpu.CompilerParams(vmem_limit_bytes=int(limit * 2**20), **params),
    )(*args)


def local(sizes, momentum, gradient, factor_q, weights, tokens):
    nr, nc, ng = sizes
    nx, nz = NX, nc // NX
    mom, grad, fq = momentum[0], gradient[0], factor_q[0].T
    rows, hid = mom.shape
    part, kr, nb = nx * nr, RANK // nr, BATCH // nr
    half = hid // ng

    def piece(n):
        return n, RANK // part + 1, RANK // 2

    left, gram, base, bufh = call(
        functools.partial(left_kernel, sizes),
        "hhhhh",
        [((rows, RANK), bf16, "v"), ((RANK + 8, RANK // 2), f32, "v"), ((2, nb, half), f32, "v"), ((rows, hid), bf16, "v")],
        [
            vmem(rows, hid), vmem(rows, hid, dtype=bf16), vmem(kr, hid), vmem(*weights.shape), vmem(*tokens.shape, dtype=bf16),
            pltpu.SemaphoreType.DMA((5,)), vmem(nr, kr, hid, dtype=bf16),
            vmem(nx, rows // nx, RANK), vmem(nx, rows // nx, RANK, dtype=bf16), vmem(nx - 1, rows // nx, RANK, dtype=bf16),
            vmem(nz, rows // nc, RANK), vmem(nz, rows // nc, RANK, dtype=bf16), vmem(nz, rows // nc, RANK, dtype=bf16),
            vmem(nx, nz, rows // nc, RANK, dtype=bf16),
            vmem(*piece(part)), vmem(*piece(part - 1)), vmem(*piece(part)),
            vmem(nr, 2, nb, half), vmem(nr - 1, 2, nb, half),
            pairs(nr - 1), pairs(nx - 1), pairs(nz), pairs(nz), pairs(nx - 1), pairs(part - 1), pairs(part - 1),
            pairs(nr - 1),
        ],
        [pltpu.with_memory_space_constraint(a, pltpu.HBM) for a in (mom, grad, fq, weights, tokens)], 0,
    )
    square = ((RANK, RANK), f32, "v")
    start = call(
        start_kernel, "v", [square, square, ((8, RANK), f32, "v"), ((8, 128), f32, "v")],
        [vmem(RANK, RANK), vmem(RANK, 2 * RANK)], (gram,),
    )
    mom_new, lh, oth, rh, rho, norms, share, tl = call(
        functools.partial(right_kernel, sizes),
        "v" * 7 + "hh",
        [
            ((rows, hid), f32, "v"), ((rows, RANK), bf16, "v"), ((rows, RANK), bf16, "v"), ((RANK, hid), bf16, "v"), ((nr, kr, half), bf16, "v"),
            ((nr, ng, 1, 128), f32, "v"), ((kr, hid), f32, "v"), ((2, nb, RANK), bf16, "v"),
        ],
        [
            vmem(rows, hid), vmem(rows, hid, dtype=bf16), pltpu.SemaphoreType.DMA((2,)),
            vmem(nx, nz, rows // nc, RANK, dtype=bf16), vmem(nx, nz, rows // nc, RANK, dtype=bf16), vmem(nr, kr, hid), vmem(nr, kr, hid, dtype=bf16),
            vmem(nr - 1, kr, hid, dtype=bf16), vmem(nr, nb, RANK), vmem(nr, nb, RANK, dtype=bf16),
            vmem(nr - 1, nb, RANK, dtype=bf16), vmem(nb, RANK, dtype=bf16), vmem(nb, RANK, dtype=bf16),
            vmem(nr, kr, hid, dtype=bf16), vmem(kr, half, dtype=bf16), vmem(nr, kr, half, dtype=bf16),
            vmem(1, 128), vmem(ng, nz, 1, 128), vmem(nx, ng, 1, 128), vmem(nr, ng, 1, 128),
            pairs(1), pairs(nr - 1), pairs(nr - 1), pairs(nz), pairs(nx - 1), pairs(nr - 1), pairs(1), pairs(nr - 1),
            pairs(ng * nz - 1), pairs(nx - 1), pairs(nr - 1), pairs(1),
        ],
        (bufh, left, *start, tokens, mom, grad), 1,
    )
    mom_new, new, fac, hidden = call(
        last_kernel, "v" * 10,
        [((rows, hid), f32, "h"), (weights.shape, f32, "h"), ((kr, hid), f32, "v"), ((nb, half), bf16, "v")],
        [vmem(*weights.shape), pltpu.SemaphoreType.DMA((2 * CHUNKS + 1,))],
        (mom_new, weights, base, lh, oth, rh, rho, norms, share, tl),
    )
    return mom_new[None], fac.T[None], new, hidden


def solution(mesh):
    sizes = tuple(mesh.shape[a] for a in ("row", "col", "grp"))
    in_specs = (
        P("grp", "row", "col"),
        P("grp", "row", "col"),
        P("grp", "col", "row"),
        P(None, "row", ("col", "grp")),
        P(None, "row"),
    )
    out_specs = (
        P("grp", "row", "col"),
        P("grp", "col", "row"),
        P(None, "row", ("col", "grp")),
        P("row", ("col", "grp")),
    )
    return jax.shard_map(
        functools.partial(local, sizes), mesh=mesh, in_specs=in_specs, out_specs=out_specs, check_vma=False
    )
```

```python
import functools
import math

import jax
import jax.numpy as jnp
from jax import lax
from jax.experimental import pallas as pl
from jax.experimental.pallas import tpu as pltpu
from jax.sharding import PartitionSpec as P

D = 4096
HID = 16384
RANK = 256
BATCH = 256
FEEDBACK = 0.05
EPSILON = 1e-06
STEP = 0.4 * math.sqrt(max(D, HID))
CHUNKS = 4
NEAR = 0.1
NX = 4

f32, bf16 = jnp.float32, jnp.bfloat16
HI = lax.Precision.HIGHEST
MESH = pl.DeviceIdType.MESH
NN = (((1,), (0,)), ((), ()))
NT = (((1,), (1,)), ((), ()))
TN = (((0,), (0,)), ((), ()))


def mm(a, b, dims=NN, precision=None):
    return lax.dot_general(a, b, dims, precision=precision, preferred_element_type=f32)


def around(i, n):
    return [i if d == 0 else i + d - jnp.where(i + d >= n, n, 0) for d in range(n)]


def far_first(offsets, *rings):
    def way(offset):
        return sum(min(d, n - d) for d, n in zip(offset, rings))

    return sorted((offset for offset in offsets if any(offset)), key=lambda offset: -way(offset))


class Place:
    def __init__(self, sizes):
        self.nr, self.nc, self.ng = sizes
        self.nx, self.nz, self.ny = NX, self.nc // NX, self.nr // 2
        self.r, self.c, self.g = (lax.axis_index(a) for a in ("row", "col", "grp"))
        self.x, self.z = lax.rem(self.c, self.nx), lax.div(self.c, self.nx)
        self.core = lax.rem(self.r, 2)
        self.xs = around(self.x, self.nx)
        ys = around(lax.div(self.r, 2), self.ny)
        self.rs = {(dy, dc): 2 * ys[dy] + (1 - self.core if dc else self.core) for dy in range(self.ny) for dc in range(2)}
        self.row = far_first(self.rs, self.ny)
        self.line = [(d,) for d in range(1, self.nx)]
        self.line = [d for (d,) in far_first(self.line, self.nx)]
        self.plane = far_first([(dx, *d) for dx in range(self.nx) for d in self.rs], self.nx, self.ny)
        last = self.nz - 1
        self.stack = [
            jnp.where(
                self.z <= last // 2,
                last - k - jnp.where(last - k <= self.z, 1, 0),
                k + jnp.where(k >= self.z, 1, 0),
            )
            for k in range(last)
        ]
        around_both = around(self.g * self.nz + self.z, self.ng * self.nz)
        self.ring = [around_both[d] for (d,) in far_first([(d,) for d in range(len(around_both))], len(around_both))]

    def at(self, row=(0, 0), dx=0, z=None, g=None):
        z = self.z if z is None else z
        return (self.rs[row], z * self.nx + self.xs[dx], self.g if g is None else g)

    def up(self, k):
        g = jnp.where(self.ring[k] >= self.nz, 1, 0)
        return self.at(z=self.ring[k] - g * self.nz, g=g)


def greet(partners):
    barrier = pltpu.get_barrier_semaphore()
    for device in partners:
        pl.semaphore_signal(barrier, inc=1, device_id=device, device_id_type=MESH)
    return lambda: pl.semaphore_wait(barrier, len(partners))


def remote(src, dst, sent, received, device):
    return pltpu.make_async_remote_copy(
        src_ref=src, dst_ref=dst, send_sem=sent, recv_sem=received, device_id=device, device_id_type=MESH
    )


def send(src, dst, sems, k, device):
    copy = remote(src, dst, sems.at[0, k], sems.at[1, k], device)
    copy.start()
    return copy


def send_line(pick, slot, sems, at):
    waits = []
    for k, other in enumerate(at.stack):
        device = at.at(z=other)
        remote(pick(other), slot(at.z), sems.at[0, k], sems.at[1, at.z], device).start()
        waits.append(remote(pick(other), slot(other), sems.at[0, k], sems.at[1, other], device))
    return waits


def arrived(copies):
    for copy in copies:
        copy.wait_recv()


def left_kernel(sizes, mom_h, grad_h, fq_h, w_h, tok_h, left_o, gram_o, base_o, bufh,
                mom, grad, fq, w, tok, s_in, qbuf, part, partb, rx, sx, sxb, rz, l512, gp, rg, gf, pre, rpre,
                s_q, s_x, s_z, s_az, s_ax, s_g, s_ag, s_p):
    at = Place(sizes)
    nr, nx, nz = at.nr, at.nx, at.nz
    ready = greet([at.at(z=other) for other in at.stack] + [at.at(row=d[1:], dx=d[0]) for d in at.plane])
    r, x, z = at.r, at.x, at.z
    loads = [
        pltpu.make_async_copy(a, b, s_in.at[k])
        for k, (a, b) in enumerate(((fq_h, fq), (mom_h, mom), (grad_h, grad), (tok_h, tok), (w_h, w)))
    ]
    for load in loads:
        load.start()
    loads[0].wait()
    qbuf[r] = fq[...].astype(bf16)
    ready()
    got_q = [send(qbuf.at[r], qbuf.at[r], s_q, k, at.at(row=d)) for k, d in enumerate(at.row)]
    loads[1].wait()
    loads[2].wait()
    bufh[...] = (mom[...] + grad[...].astype(f32)).astype(bf16)
    arrived(got_q)
    part[...] = mm(bufh[...], qbuf[...].reshape(RANK, -1), NT).reshape(part.shape)
    partb[...] = part[...].astype(bf16)
    got_x = [send(partb.at[at.xs[d]], rx.at[k], s_x, k, at.at(dx=d)) for k, d in enumerate(at.line)]
    loads[3].wait()
    loads[4].wait()
    for p in range(2):
        high = w[p].astype(bf16)
        low = (w[p] - high.astype(f32)).astype(bf16)
        pre[:, p] = (mm(tok[...], high) + mm(tok[...], low)).reshape(pre[:, p].shape)
    arrived(got_x)
    sx[...] = (part[x] + jnp.sum(rx[...].astype(f32), axis=0)).reshape(sx.shape)
    sxb[...] = sx[...].astype(bf16)
    rz[z] = jnp.zeros(rz.shape[1:], bf16)
    got_z = send_line(lambda other: sxb.at[other], lambda place: rz.at[place], s_z, at)
    got_p = [send(pre.at[at.rs[d]], rpre.at[k], s_p, k, at.at(row=d)) for k, d in enumerate(at.row)]
    arrived(got_z)
    l512[x, z] = (sx[z] + jnp.sum(rz[...].astype(f32), axis=0)).astype(bf16)
    got_az = send_line(lambda other: l512.at[x, z], lambda place: l512.at[x, place], s_az, at)
    arrived(got_az)
    rows = l512[x].reshape(-1, RANK)
    gram = mm(rows, rows, TN)
    h = RANK // 2
    i, j = (lax.broadcasted_iota(jnp.int32, (h, h), d) for d in (0, 1))
    packed = jnp.where(i >= j, gram[:h, :h], gram[h:, h:])
    gp[: gp.shape[0] // 2, :-1] = packed.reshape(gp.shape[0] // 2, -1, h)
    gp[gp.shape[0] // 2 :, :-1] = gram[h:, :h].reshape(gp.shape[0] // 2, -1, h)
    gp[:, -1:] = jnp.broadcast_to(
        jnp.sum(jnp.where(i == j, gram[h:, h:], 0.0), axis=0, keepdims=True), (gp.shape[0], 1, h)
    )
    got_g = []
    for k, (dx, *d) in enumerate(at.plane):
        m = at.xs[dx] * nr + at.rs[*d]
        got_g.append(send(gp.at[m], rg.at[k], s_g, k, at.at(row=(*d,), dx=dx)))
    got_ax = [send(l512.at[x], l512.at[x], s_ax, k, at.at(dx=d)) for k, d in enumerate(at.line)]
    arrived(got_g)
    m = x * nr + r
    gf[m] = gp[m] + jnp.sum(rg[...], axis=0)
    got_ag = [send(gf.at[m], gf.at[m], s_ag, k, at.at(row=d[1:], dx=d[0])) for k, d in enumerate(at.plane)]
    arrived(got_p)
    base_o[...] = pre[r] + jnp.sum(rpre[...], axis=0)
    arrived(got_ax)
    left_o[...] = l512[...].reshape(left_o.shape)
    arrived(got_ag)
    gram_o[:RANK] = gf[:, :-1].reshape(RANK, -1)
    gram_o[RANK:] = jnp.broadcast_to(gf[0, -1:], (8, gf.shape[2]))
    for copies in (got_q, got_x, got_p, got_z, got_az, got_g, got_ax, got_ag):
        for copy in copies:
            copy.wait_send()


def tri_half(e):
    i, j = (lax.broadcasted_iota(jnp.int32, e.shape, d) for d in (0, 1))
    return jnp.where(i > j, e, jnp.where(i == j, 0.5 * e, 0.0))


def residual(w, a, precision=None):
    i, j = (lax.broadcasted_iota(jnp.int32, a.shape, d) for d in (0, 1))
    return mm(mm(w, a, NN, precision), w, NT, precision) - jnp.where(i == j, 1.0, 0.0)


def start_kernel(packed, a_o, w_o, across_o, near_o, gram, s):
    n, h = RANK, RANK // 2
    i, j = (lax.broadcasted_iota(jnp.int32, (h, h), d) for d in (0, 1))
    both, turned = packed[:h], packed[:h].T
    gram[:h, :h] = jnp.where(i >= j, both, turned)
    gram[h:, h:] = jnp.where(i > j, turned, jnp.where(i == j, packed[n : n + 1], both))
    gram[h:, :h] = packed[h:n]
    gram[:h, h:] = packed[h:n].T
    i, j = (lax.broadcasted_iota(jnp.int32, (n, n), d) for d in (0, 1))
    eye = jnp.where(i == j, 1.0, 0.0)
    diagonal = jnp.where(i == j, gram[...], 0.0)
    down = lax.rsqrt(jnp.sum(diagonal, axis=1, keepdims=True))
    across = lax.rsqrt(jnp.sum(diagonal, axis=0, keepdims=True))
    a = gram[...] * down * across
    a_o[...] = a
    across_o[...] = jnp.broadcast_to(across, across_o.shape)
    w = eye - tri_half(jnp.where(i == j, 0.0, a))
    w = w - mm(tri_half(residual(w, a)), w)
    e = residual(w, a)
    w_o[...] = w - mm(tri_half(e), w)
    far = jnp.sum(e * e)
    near_o[...] = jnp.ones(near_o.shape, f32)

    @pl.when(~(far < NEAR))
    def _():
        s[:, :n] = gram[...]
        s[:, n:] = eye
        row = lax.broadcasted_iota(jnp.int32, (n, 1), 0)

        def eliminate(k, _):
            line = s[pl.ds(k, 1), :]
            column = jnp.sum(jnp.where(j == k, s[:, :n], 0.0), axis=1, keepdims=True)
            pivot = jnp.sum(jnp.where(row == k, column, 0.0), axis=0, keepdims=True)
            s[...] = s[...] - jnp.where(row > k, column / pivot, 0.0) * line
            return 0

        lax.fori_loop(0, n, eliminate, 0)
        pivots = jnp.sum(jnp.where(i == j, s[:, :n], 0.0), axis=1, keepdims=True)
        w_o[...] = s[:, n:] / jnp.sqrt(pivots)
        across_o[...] = jnp.ones(across_o.shape, f32)
        near_o[...] = jnp.zeros(near_o.shape, f32)


def right_kernel(sizes, bufh, left, a, w, across, near, tok, mom_h, grad_h, mom_o, lh_o, oth_o, rh_o, rho_o, nb_o, share_o, tl_o,
                 mom, grad, s_in, lh, oth, rt, rtb, rrt, tl, tlb, rtl, tls, tlo, rh, sho, rho, sq, sqz, sqx, nb,
                 s_l, s_rt, s_tl, s_lz, s_lx, s_rh, s_sh, s_ro, s_sq, s_sx, s_nb, s_to):
    at = Place(sizes)
    nr, nx, nz, ng = at.nr, at.nx, at.nz, at.ng
    r, c, g, x, z = at.r, at.c, at.g, at.x, at.z
    upwards = range(len(at.ring))
    ready = greet(
        [at.up(k) for k in upwards] + [at.at(row=d) for d in at.row] + [at.at(dx=d) for d in at.line]
    )
    o = 1 - g
    kr = RANK // nr
    half = sho.shape[1]

    loads = [pltpu.make_async_copy(mom_h, mom, s_in.at[0]), pltpu.make_async_copy(grad_h, grad, s_in.at[1])]
    for load in loads:
        load.start()
    inverse = w[...]
    for _ in range(2):
        error = jnp.where(near[:1, :1] > 0, tri_half(residual(inverse, a[...], HI)), 0.0)
        inverse = inverse - mm(error, inverse)
    inverse = inverse * across[:1]
    high = inverse.astype(bf16)
    low = (inverse - high.astype(f32)).astype(bf16)
    left_h = (mm(left[...], high, NT) + mm(left[...], low, NT)).astype(bf16)
    lh[...] = left_h.reshape(lh.shape)
    ready()
    got_l = [send(lh.at[x, z], oth.at[x, z], s_l, 0, at.at(g=o))]
    rt[...] = mm(left_h, bufh[...], TN).reshape(rt.shape)
    rtb[...] = rt[...].astype(bf16)
    got_rt = [send(rtb.at[at.rs[d]], rrt.at[k], s_rt, k, at.at(row=d)) for k, d in enumerate(at.row)]
    tl[...] = mm(tok[...], left_h).reshape(tl.shape)
    tlb[...] = tl[...].astype(bf16)
    got_tl = [send(tlb.at[at.rs[d]], rtl.at[k], s_tl, k, at.at(row=d)) for k, d in enumerate(at.row)]
    arrived(got_rt)
    share = rt[r] + jnp.sum(rrt[...].astype(f32), axis=0)
    eye = lax.broadcasted_iota(jnp.int32, (kr, 128), 0) == lax.broadcasted_iota(jnp.int32, (kr, 128), 1)
    squares = jnp.sum(share * share, axis=1, keepdims=True)
    line = jnp.sum(jnp.where(eye, squares, 0.0), axis=0, keepdims=True)
    sqz[g, z] = line
    sq[...] = line
    got_sq = [send(sq, sqz.at[g, z], s_sq, k, at.up(k)) for k in upwards]
    share_o[...] = share
    rh[r] = share.astype(bf16)
    sho[...] = share_o[:, pl.ds(pl.multiple_of(o * half, half), half)].astype(bf16)
    got_sh = [send(sho, rho.at[r], s_sh, 0, at.at(g=o))]
    arrived(got_l)
    got_lz = send_line(lambda other: oth.at[x, z], lambda place: oth.at[x, place], s_lz, at)
    got_rh = [send(rh.at[r], rh.at[r], s_rh, k, at.at(row=d)) for k, d in enumerate(at.row)]
    arrived(got_tl)
    tls[...] = (tl[r] + jnp.sum(rtl[...].astype(f32), axis=0)).astype(bf16)
    got_to = [send(tls, tlo, s_to, 0, at.at(g=o))]
    arrived(got_sh)
    got_ro = [send(rho.at[r], rho.at[r], s_ro, k, at.at(row=d)) for k, d in enumerate(at.row)]
    arrived(got_sq)
    sqx[x] = jnp.sum(sqz[...], axis=1)
    got_sx = [send(sqx.at[x], sqx.at[x], s_sx, k, at.at(dx=d)) for k, d in enumerate(at.line)]
    arrived(got_lz)
    got_lx = [send(oth.at[x], oth.at[x], s_lx, k, at.at(dx=d)) for k, d in enumerate(at.line)]
    arrived(got_sx)
    nb[r] = jnp.sum(sqx[...], axis=0)
    got_nb = [send(nb.at[r], nb.at[r], s_nb, k, at.at(row=d)) for k, d in enumerate(at.row)]
    lh_o[...] = lh[...].reshape(lh_o.shape)
    for load in loads:
        load.wait()
    arrived(got_rh)
    mom_o[...] = mom[...] + grad[...].astype(f32) - FEEDBACK * mm(left_h, rh[...].reshape(RANK, -1))
    rh_o[...] = rh[...].reshape(rh_o.shape)
    arrived(got_lx)
    oth_o[...] = oth[...].reshape(oth_o.shape)
    arrived(got_nb)
    nb_o[...] = nb[...]
    arrived(got_ro)
    rho_o[...] = rho[...]
    arrived(got_to)
    tl_o[0] = tls[...]
    tl_o[1] = tlo[...]
    for copies in (got_l, got_rt, got_tl, got_lz, got_sh, got_sq, got_sx, got_rh, got_lx, got_nb, got_ro, got_to):
        for copy in copies:
            copy.wait_send()


def last_kernel(mom, w, base, lh, oth, rh, rho, nb, share, tl, mom_h, new_h, fac_o, hid_o, new_v, sems):
    r, g = lax.axis_index("row"), lax.axis_index("grp")
    o = 1 - g
    nr, kr, half = rho.shape
    rows = lh.shape[0]
    chunk = rows // CHUNKS
    copies = []

    def out(src, dst):
        copies.append(pltpu.make_async_copy(src, dst, sems.at[len(copies)]))
        copies[-1].start()

    out(mom, mom_h)
    eye = lax.broadcasted_iota(jnp.int32, (kr, 128), 0) == lax.broadcasted_iota(jnp.int32, (kr, 128), 1)

    def columns(norms):
        norms = jnp.broadcast_to(jnp.sqrt(norms + EPSILON), (norms.shape[0], kr, 128))
        return jnp.sum(jnp.where(eye[None], norms, 0.0), axis=2, keepdims=True)

    own = rh[:, pl.ds(pl.multiple_of(g * half, half), half)].astype(f32).reshape(rho.shape)
    own_q = (own / columns(nb[:, g])).astype(bf16).reshape(RANK, half)
    other_q = (rho[...].astype(f32) / columns(nb[:, o])).astype(bf16).reshape(RANK, half)
    for p, q, factor in ((g, own_q, lh), (o, other_q, oth)):
        for k in range(CHUNKS):
            at = pl.ds(k * chunk, chunk)
            new_v[p, at] = w[p, at] - STEP * mm(factor[at], q)
            out(new_v.at[p, at], new_h.at[p, at])
    fac_o[...] = share[...] / columns(nb[r, g][None])[0]
    own_pre = base[g] - STEP * mm(tl[0], own_q)
    other_pre = base[o] - STEP * mm(tl[1], other_q)
    gate = jnp.where(g == 0, own_pre, other_pre)
    up = jnp.where(g == 0, other_pre, own_pre)
    hid_o[...] = (gate / (1.0 + jnp.exp(-gate)) * up).astype(bf16)
    for copy in copies:
        copy.wait()


def vmem(*shape, dtype=f32):
    return pltpu.VMEM(shape, dtype)


def pairs(n):
    return pltpu.SemaphoreType.DMA((2, n))


def call(kernel, ins, outs, scratch, args, collective_id=None, limit=24):
    where = {"v": pltpu.VMEM, "h": pltpu.HBM}
    params = {} if collective_id is None else dict(collective_id=collective_id, has_side_effects=True)
    return pl.pallas_call(
        kernel,
        out_shape=[jax.ShapeDtypeStruct(s, t) for s, t, _ in outs],
        in_specs=[pl.BlockSpec(memory_space=where[k]) for k in ins],
        out_specs=[pl.BlockSpec(memory_space=where[k]) for _, _, k in outs],
        scratch_shapes=scratch,
        compiler_params=pltpu.CompilerParams(vmem_limit_bytes=int(limit * 2**20), **params),
    )(*args)


def local(sizes, momentum, gradient, factor_q, weights, tokens):
    nr, nc, ng = sizes
    nx, nz = NX, nc // NX
    mom, grad, fq = momentum[0], gradient[0], factor_q[0].T
    rows, hid = mom.shape
    part, kr, nb = nx * nr, RANK // nr, BATCH // nr
    half = hid // ng

    def piece(n):
        return n, RANK // part + 1, RANK // 2

    left, gram, base, bufh = call(
        functools.partial(left_kernel, sizes),
        "hhhhh",
        [((rows, RANK), bf16, "v"), ((RANK + 8, RANK // 2), f32, "v"), ((2, nb, half), f32, "v"), ((rows, hid), bf16, "v")],
        [
            vmem(rows, hid), vmem(rows, hid, dtype=bf16), vmem(kr, hid), vmem(*weights.shape), vmem(*tokens.shape, dtype=bf16),
            pltpu.SemaphoreType.DMA((5,)), vmem(nr, kr, hid, dtype=bf16),
            vmem(nx, rows // nx, RANK), vmem(nx, rows // nx, RANK, dtype=bf16), vmem(nx - 1, rows // nx, RANK, dtype=bf16),
            vmem(nz, rows // nc, RANK), vmem(nz, rows // nc, RANK, dtype=bf16), vmem(nz, rows // nc, RANK, dtype=bf16),
            vmem(nx, nz, rows // nc, RANK, dtype=bf16),
            vmem(*piece(part)), vmem(*piece(part - 1)), vmem(*piece(part)),
            vmem(nr, 2, nb, half), vmem(nr - 1, 2, nb, half),
            pairs(nr - 1), pairs(nx - 1), pairs(nz), pairs(nz), pairs(nx - 1), pairs(part - 1), pairs(part - 1),
            pairs(nr - 1),
        ],
        [pltpu.with_memory_space_constraint(a, pltpu.HBM) for a in (mom, grad, fq, weights, tokens)], 0,
    )
    square = ((RANK, RANK), f32, "v")
    start = call(
        start_kernel, "v", [square, square, ((8, RANK), f32, "v"), ((8, 128), f32, "v")],
        [vmem(RANK, RANK), vmem(RANK, 2 * RANK)], (gram,),
    )
    mom_new, lh, oth, rh, rho, norms, share, tl = call(
        functools.partial(right_kernel, sizes),
        "v" * 7 + "hh",
        [
            ((rows, hid), f32, "v"), ((rows, RANK), bf16, "v"), ((rows, RANK), bf16, "v"), ((RANK, hid), bf16, "v"), ((nr, kr, half), bf16, "v"),
            ((nr, ng, 1, 128), f32, "v"), ((kr, hid), f32, "v"), ((2, nb, RANK), bf16, "v"),
        ],
        [
            vmem(rows, hid), vmem(rows, hid, dtype=bf16), pltpu.SemaphoreType.DMA((2,)),
            vmem(nx, nz, rows // nc, RANK, dtype=bf16), vmem(nx, nz, rows // nc, RANK, dtype=bf16), vmem(nr, kr, hid), vmem(nr, kr, hid, dtype=bf16),
            vmem(nr - 1, kr, hid, dtype=bf16), vmem(nr, nb, RANK), vmem(nr, nb, RANK, dtype=bf16),
            vmem(nr - 1, nb, RANK, dtype=bf16), vmem(nb, RANK, dtype=bf16), vmem(nb, RANK, dtype=bf16),
            vmem(nr, kr, hid, dtype=bf16), vmem(kr, half, dtype=bf16), vmem(nr, kr, half, dtype=bf16),
            vmem(1, 128), vmem(ng, nz, 1, 128), vmem(nx, ng, 1, 128), vmem(nr, ng, 1, 128),
            pairs(1), pairs(nr - 1), pairs(nr - 1), pairs(nz), pairs(nx - 1), pairs(nr - 1), pairs(1), pairs(nr - 1),
            pairs(ng * nz - 1), pairs(nx - 1), pairs(nr - 1), pairs(1),
        ],
        (bufh, left, *start, tokens, mom, grad), 1,
    )
    mom_new, new, fac, hidden = call(
        last_kernel, "v" * 10,
        [((rows, hid), f32, "h"), (weights.shape, f32, "h"), ((kr, hid), f32, "v"), ((nb, half), bf16, "v")],
        [vmem(*weights.shape), pltpu.SemaphoreType.DMA((2 * CHUNKS + 1,))],
        (mom_new, weights, base, lh, oth, rh, rho, norms, share, tl),
    )
    return mom_new[None], fac.T[None], new, hidden


def solution(mesh):
    sizes = tuple(mesh.shape[a] for a in ("row", "col", "grp"))
    in_specs = (
        P("grp", "row", "col"),
        P("grp", "row", "col"),
        P("grp", "col", "row"),
        P(None, "row", ("col", "grp")),
        P(None, "row"),
    )
    out_specs = (
        P("grp", "row", "col"),
        P("grp", "col", "row"),
        P(None, "row", ("col", "grp")),
        P("row", ("col", "grp")),
    )
    return jax.shard_map(
        functools.partial(local, sizes), mesh=mesh, in_specs=in_specs, out_specs=out_specs, check_vma=False
    )
```
